32 devices in a mesh: groups: 1, expert: 32 (over z, y, x, core).
Axes of the slice: x: 2, y: 2, z: 4, core: 2. Of those that a mesh axis runs over, the one named last changes fastest.
Arguments:
- tokens: bfloat16 [256, 3584], P(('groups', 'expert')), may hold values from -6 to 6
- cotangent: bfloat16 [256, 3584], P(('groups', 'expert')), may hold values from -4 to 4
- route_probs: float32 [256, 8], P(('groups', 'expert')), may hold values from 0.02 to 0.5
- expert_ids: int32 [256, 8], P(('groups', 'expert')), may hold values from 0 to 15, all different within a row; in each aligned block of 8 rows (0 to 7, 8 to 15, ...) at most 6 rows name the same one
- gate_weight: bfloat16 [3584, 16384], P(None, 'expert'), as said below
- up_weight: bfloat16 [3584, 16384], P(None, 'expert'), as said below
- down_weight: bfloat16 [16384, 3584], P('expert'), as said below
- narrow_factors: bfloat16 [3, 16, 16384], P(None, None, 'expert'), may hold values from -1.5 to 1.5
- wide_factors: bfloat16 [3, 16, 57344], P(None, None, 'expert'), may hold values from -1.5 to 1.5
Outputs:
- grad_tokens: bfloat16 [256, 3584], P(('groups', 'expert'))
- grad_probs: float32 [256, 8], P(('groups', 'expert'))
- grad_narrow: float32 [3, 16, 16384], P('groups', None, 'expert')
- grad_wide: float32 [3, 16, 57344], P('groups', None, 'expert')
The draws below stay inside these ranges and needn't reach their ends.
Inputs may be any that keep to these rules, and one draw needn't show every extreme that they name: `expert_ids`: in each aligned block of 8 rows no expert is named more than 6 times, a bound that some block reaches. `gate_weight`: of every four consecutive rows of a column, two entries are zero. `up_weight`: of every four consecutive rows of a column, two entries are zero. `down_weight`: of every four consecutive rows of a column, two entries are zero.
All inputs are finite; a program needn't handle non-finite values.
Results may differ from the reference program's by a relative error of at most 0.0088.
Values may be sent and summed in bfloat16 or wider, within the bound.
No kernel may reach another device: no remote copies, remote signals or barrier semaphores. Data moves between devices by JAX's collectives and lax.ppermute only.
A program may use at most 128 MiB of HBM per device.

```python
import math
import jax
import jax.numpy as jnp
import numpy as np
from jax import lax

D = 3584
FF = 1024
RANK = 16
TOP = 8
TOK_DEV = 8
EXPERTS = 16
TOKENS = 256
CAP = 6
N_EXPERT = 32


pair_patterns = [[1, 1, 0, 0], [1, 0, 1, 0], [1, 0, 0, 1], [0, 1, 1, 0], [0, 1, 0, 1], [0, 0, 1, 1]]


def keep_pattern(key, group_count, column_count):
    pattern = jax.random.randint(key, (group_count, column_count), 0, 6)
    pair_rows = jnp.array(pair_patterns, jnp.float32)
    chosen = jnp.take(pair_rows, pattern, axis=0)
    return jnp.transpose(chosen, (0, 2, 1)).reshape(group_count * 4, column_count)


def pruned_values(key, row_count, column_count, spread_factor):
    values = jnp.clip(jax.random.normal(jax.random.fold_in(key, 1), (row_count, column_count), jnp.float32), -4.0, 4.0)
    kept = keep_pattern(jax.random.fold_in(key, 2), row_count // 4, column_count)
    return (values * spread_factor * kept).astype(jnp.bfloat16)


def draw_gate_weight(key, part):
    key = jax.random.fold_in(key, 11)
    return pruned_values(key, D, EXPERTS * FF, (2.0 / D) ** 0.5)


def draw_up_weight(key, part):
    key = jax.random.fold_in(key, 23)
    return pruned_values(key, D, EXPERTS * FF, (2.0 / D) ** 0.5)


def draw_down_weight(key, part):
    key = jax.random.fold_in(key, 37)
    return pruned_values(key, EXPERTS * FF, D, (2.0 / FF) ** 0.5)


def steps_of(own_key, dims, cuts, least, high):
    gain = 1.0
    for dim, shards_of in cuts:
        steps = jax.random.uniform(jax.random.fold_in(jax.random.fold_in(own_key, 6), dim), (shards_of,), jnp.float32, least / len(cuts), high / len(cuts))
        gain = gain * jnp.repeat(jnp.exp(steps), dims[dim] // shards_of).reshape((-1,) + (1,) * (len(dims) - 1 - dim))
    return gain


def routed_block(key, own, number, rows, number_of, top, limit, lean):
    order = jax.random.permutation(key, number_of)
    heavy_load, usual = shares(number_of, rows * top, limit, lean, True), shares(number_of, rows * top, limit, lean, False)
    places = jnp.arange(number_of)

    def named(tallies, turn):
        used = int((tallies > 0).sum())
        fixed = max(1, used // 4)
        passed = fixed + (places - fixed + turn * (used - fixed)) % max(1, number_of - fixed)
        return jnp.zeros((number_of,), jnp.int32).at[order[jnp.where(places < fixed, places, passed)]].set(jnp.asarray(tallies, jnp.int32))

    tallies = jnp.where(number % 4 == 0, named(heavy_load, number // 4), named(usual, number - number // 4 - 1))
    mixed = jax.random.permutation(jax.random.fold_in(own, 3), number_of)
    giver, taker = mixed[0:number_of // 2 * 2:2], mixed[1:number_of // 2 * 2:2]
    slack = jnp.minimum(tallies[giver] - 1, limit - tallies[taker]) // 2
    slack = jnp.where((giver == order[0]) | (taker == order[0]) | (tallies[taker] == 0), 0, jnp.maximum(slack, 0))
    passed = jax.random.randint(jax.random.fold_in(own, 4), (number_of // 2,), 0, 1 << 20) % (slack + 1)
    tallies = tallies.at[giver].add(-passed).at[taker].add(passed)
    items = jnp.searchsorted(jnp.cumsum(tallies), jnp.arange(rows * top), side="right").astype(jnp.int32)
    listing = items.reshape(top, rows).T
    listing = listing[jax.random.permutation(jax.random.fold_in(own, 1), rows)]
    turn = jax.random.randint(jax.random.fold_in(own, 2), (rows, 1), 0, top)
    return jnp.take_along_axis(listing, (jnp.arange(top)[None, :] + turn) % top, axis=1)


def shares(amount, total, bound, slope, full):
    loads = [(1 << 20) // math.isqrt(standing ** slope) + 1 for standing in range(1, amount + 1)]
    largest = bound if full else min(bound, max(-(-total // amount), total * loads[0] // sum(loads)))
    least = 1 if total - largest >= amount - 1 else 0
    holding, surplus = [largest] + [least] * (amount - 1), total - largest - least * (amount - 1)
    while surplus > 0:
        movable = [i for i in range(1, amount) if holding[i] < largest] or [i for i in range(1, amount) if holding[i] < bound]
        mass, budget = sum([loads[i] for i in movable]), surplus
        for i in movable:
            extra = min(bound - holding[i], max(1, budget * loads[i] // mass), surplus)
            holding[i] = holding[i] + extra
            surplus = surplus - extra
    return np.array(holding)


def centred(own_key, shape, scale, limit, shards=(), kind=jnp.bfloat16):
    entries = scale * jax.random.normal(own_key, shape, jnp.float32)
    if shards:
        entries = entries * steps_of(own_key, shape, shards, -0.22, 0.18)
    return jnp.clip(entries, -limit, limit).astype(kind)


def setup_inputs(seed: int = 0, part: int = 0) -> dict:
    splits = jax.random.split(jax.random.key(seed), 10)
    part_splits = jax.random.split(jax.random.fold_in(splits[9], part), 10)
    tokens = centred(part_splits[0], (TOKENS, D), 1.0, 6.0, ((0, 32),))
    cotangent = centred(part_splits[1], (TOKENS, D), 0.5, 4.0, ((0, 32),))
    route_probs = jnp.clip(jnp.exp(math.log(0.5) - 3.218876 * jax.random.uniform(part_splits[2], (TOKENS, TOP), jnp.float32) ** steps_of(part_splits[2], (TOKENS, TOP), ((0, 32),), -0.2, 0.2)), 0.02, 0.5)
    expert_ids_keys = jax.random.split(jax.random.fold_in(part_splits[3], 1), TOKENS // TOK_DEV)
    expert_ids_turns = jax.random.permutation(jax.random.fold_in(part_splits[3], 3), TOKENS // TOK_DEV)
    expert_ids = jax.vmap(lambda own, number: routed_block(jax.random.fold_in(part_splits[3], 2), own, number, TOK_DEV, EXPERTS, TOP, CAP, 2))(expert_ids_keys, expert_ids_turns).reshape((TOKENS, TOP))
    gate_weight = draw_gate_weight(jax.random.fold_in(splits[9], 71), part)
    up_weight = draw_up_weight(jax.random.fold_in(splits[9], 71), part)
    down_weight = draw_down_weight(jax.random.fold_in(splits[9], 71), part)
    narrow_factors = centred(splits[7], (3, RANK, EXPERTS * FF), 0.3, 1.5, ((2, 32),))
    wide_factors = centred(splits[8], (3, RANK, EXPERTS * D), 0.3, 1.5, ((2, 32),))
    return {"tokens": tokens, "cotangent": cotangent, "route_probs": route_probs, "expert_ids": expert_ids, "gate_weight": gate_weight, "up_weight": up_weight, "down_weight": down_weight, "narrow_factors": narrow_factors, "wide_factors": wide_factors}


def block_slots(route_ids, experts):
    chosen = (route_ids[:, :, None] == jnp.arange(experts, dtype=jnp.int32)[None, None, :]).astype(jnp.int32)
    before = jnp.cumsum(chosen, axis=1) - chosen
    return jnp.sum(before * chosen, axis=2).astype(jnp.int32)


def expert_half(slot_inputs, slot_grads, gate_half, up_half, down_half, narrow_rows, wide_rows):
    highest = lax.Precision.HIGHEST
    gate_eff = (gate_half.astype(jnp.float32) * (1.0 + jnp.einsum('rd,rf->df', wide_rows[0], narrow_rows[0], precision=highest))).astype(jnp.bfloat16)
    up_eff = (up_half.astype(jnp.float32) * (1.0 + jnp.einsum('rd,rf->df', wide_rows[1], narrow_rows[1], precision=highest))).astype(jnp.bfloat16)
    down_eff = (down_half.astype(jnp.float32) * (1.0 + jnp.einsum('rf,rd->fd', narrow_rows[2], wide_rows[2], precision=highest))).astype(jnp.bfloat16)
    pre_gate = jnp.dot(slot_inputs, gate_eff, preferred_element_type=jnp.float32)
    pre_up = jnp.dot(slot_inputs, up_eff, preferred_element_type=jnp.float32)
    sigmoid_gate = jax.nn.sigmoid(pre_gate)
    activated = pre_gate * sigmoid_gate
    hidden = (activated * pre_up).astype(jnp.bfloat16)
    part_out = jnp.dot(hidden, down_eff, preferred_element_type=jnp.float32).astype(jnp.bfloat16)
    grad_hidden = jnp.dot(slot_grads, down_eff.T, preferred_element_type=jnp.float32)
    grad_gate = (grad_hidden * pre_up * sigmoid_gate * (1.0 + pre_gate * (1.0 - sigmoid_gate))).astype(jnp.bfloat16)
    grad_up = (grad_hidden * activated).astype(jnp.bfloat16)
    part_in = (jnp.dot(grad_gate, gate_eff.T, preferred_element_type=jnp.float32) + jnp.dot(grad_up, up_eff.T, preferred_element_type=jnp.float32)).astype(jnp.bfloat16)
    masked_gate = jnp.dot(slot_inputs.T, grad_gate, preferred_element_type=jnp.float32) * gate_half.astype(jnp.float32)
    masked_up = jnp.dot(slot_inputs.T, grad_up, preferred_element_type=jnp.float32) * up_half.astype(jnp.float32)
    masked_down = jnp.dot(hidden.T, slot_grads, preferred_element_type=jnp.float32) * down_half.astype(jnp.float32)
    narrow_grad = jnp.stack([
        jnp.einsum('rd,df->rf', wide_rows[0], masked_gate, precision=highest),
        jnp.einsum('rd,df->rf', wide_rows[1], masked_up, precision=highest),
        jnp.einsum('rd,fd->rf', wide_rows[2], masked_down, precision=highest)])
    wide_grad = jnp.stack([
        jnp.einsum('rf,df->rd', narrow_rows[0], masked_gate, precision=highest),
        jnp.einsum('rf,df->rd', narrow_rows[1], masked_up, precision=highest),
        jnp.einsum('rf,fd->rd', narrow_rows[2], masked_down, precision=highest)])
    return part_out, part_in, narrow_grad, wide_grad


def reference(tokens, cotangent, route_probs, expert_ids, gate_weight, up_weight, down_weight, narrow_factors, wide_factors):
    half_ff = FF // 2
    blocks = N_EXPERT
    route_ids = expert_ids.reshape(blocks, TOK_DEV * TOP).astype(jnp.int32)
    slot_index = block_slots(route_ids, EXPERTS)
    block_of = jnp.arange(blocks, dtype=jnp.int32)[:, None]
    position = ((route_ids * blocks + block_of) * CAP + slot_index).reshape(-1).astype(jnp.int32)
    token_row = jnp.repeat(jnp.arange(TOKENS, dtype=jnp.int32), TOP)
    scaled = (route_probs[:, :, None].astype(jnp.float32) * cotangent[:, None, :].astype(jnp.float32)).astype(jnp.bfloat16)
    scaled = scaled.reshape(TOKENS * TOP, D)
    slot_inputs = jnp.zeros((EXPERTS * blocks * CAP, D), jnp.bfloat16).at[position].set(tokens[token_row])
    slot_grads = jnp.zeros((EXPERTS * blocks * CAP, D), jnp.bfloat16).at[position].set(scaled)
    slot_inputs = slot_inputs.reshape(EXPERTS, blocks * CAP, D)
    slot_grads = slot_grads.reshape(EXPERTS, blocks * CAP, D)

    def one_expert(expert_index):
        inputs_here = slot_inputs[expert_index]
        grads_here = slot_grads[expert_index]
        wide_rows = lax.dynamic_slice_in_dim(wide_factors, (expert_index * D).astype(jnp.int32), D, 2).astype(jnp.float32)
        out_parts = []
        in_parts = []
        narrow_parts = []
        wide_total = jnp.zeros((3, RANK, D), jnp.float32)
        for half_index in range(2):
            column = ((2 * expert_index + half_index) * half_ff).astype(jnp.int32)
            gate_half = lax.dynamic_slice_in_dim(gate_weight, column, half_ff, 1)
            up_half = lax.dynamic_slice_in_dim(up_weight, column, half_ff, 1)
            down_half = lax.dynamic_slice_in_dim(down_weight, column, half_ff, 0)
            narrow_rows = lax.dynamic_slice_in_dim(narrow_factors, column, half_ff, 2).astype(jnp.float32)
            part_out, part_in, narrow_grad, wide_grad = expert_half(inputs_here, grads_here, gate_half, up_half, down_half, narrow_rows, wide_rows)
            out_parts.append(part_out)
            in_parts.append(part_in)
            narrow_parts.append(narrow_grad)
            wide_total = wide_total + wide_grad
        expert_out = (out_parts[0].astype(jnp.float32) + out_parts[1].astype(jnp.float32)).astype(jnp.bfloat16)
        slot_in = (in_parts[0].astype(jnp.float32) + in_parts[1].astype(jnp.float32)).astype(jnp.bfloat16)
        return expert_out, slot_in, jnp.concatenate(narrow_parts, axis=2), wide_total

    expert_out, slot_in, narrow_all, wide_all = lax.map(one_expert, jnp.arange(EXPERTS, dtype=jnp.int32))
    grad_narrow = jnp.transpose(narrow_all, (1, 2, 0, 3)).reshape(3, RANK, EXPERTS * FF)
    grad_wide = jnp.transpose(wide_all, (1, 2, 0, 3)).reshape(3, RANK, EXPERTS * D)
    picked_out = expert_out.reshape(-1, D)[position].reshape(TOKENS, TOP, D)
    picked_in = slot_in.reshape(-1, D)[position].reshape(TOKENS, TOP, D)
    grad_probs = jnp.einsum('td,tkd->tk', cotangent.astype(jnp.float32), picked_out.astype(jnp.float32))
    grad_tokens = jnp.sum(picked_in.astype(jnp.float32), axis=1).astype(jnp.bfloat16)
    return (grad_tokens, grad_probs, grad_narrow, grad_wide)
```

```python
import jax
import jax.numpy as jnp
from jax import lax
from jax.sharding import PartitionSpec as P

ROWS = (((1,), (1,)), ((), ()))
COLS = (((0,), (0,)), ((), ()))


def send(value, mask):
    pairs = [(source, source ^ mask) for source in range(lax.axis_size("expert"))]
    return lax.ppermute(value, "expert", pairs)


def stages():
    found, bit, top = [], 1, lax.axis_size("expert").bit_length() - 1
    while bit < top:
        if bit + 1 < top:
            found.append((2**bit, 2 ** (bit + 1), 3 * 2**bit))
        else:
            found.append((2**bit,))
        bit += 2
    return found


def gather_rows(block):
    for masks in reversed(stages()):
        block = jnp.concatenate([block] + [send(block, mask) for mask in masks], axis=0)
    return jnp.concatenate([block, send(block, 1)], axis=0)


def scatter_rows(block):
    half = block.shape[0] // 2
    total = block[:half].astype(jnp.float32) + send(block[half:], 1).astype(jnp.float32)
    for masks in stages():
        parts = jnp.split(total.astype(jnp.bfloat16), len(masks) + 1, axis=0)
        total = parts[0].astype(jnp.float32)
        for part, mask in zip(parts[1:], masks):
            total = total + send(part, mask).astype(jnp.float32)
    return total


def two_terms(value):
    high = value.astype(jnp.bfloat16)
    low = (value - high.astype(jnp.float32)).astype(jnp.bfloat16)
    return jnp.concatenate([high, low], axis=-1)


def dot32(left, right, dims=(((1,), (0,)), ((), ()))):
    return lax.dot_general(left, right, dims, preferred_element_type=jnp.float32)


def join_halves(mine, other, is_lower):
    return jnp.where(
        is_lower, jnp.concatenate([mine, other], axis=-1), jnp.concatenate([other, mine], axis=-1)
    )


def scaled_weight(weight, left, right):
    return (weight.astype(jnp.float32) * (1.0 + dot32(left, right, COLS))).astype(jnp.bfloat16)


def body(
    tokens,
    cotangent,
    route_probs,
    expert_ids,
    gate_weight,
    up_weight,
    down_weight,
    narrow_factors,
    wide_factors,
):
    tok_rows, width = tokens.shape
    devices = lax.axis_size("expert")
    experts = devices // 2
    me = lax.axis_index("expert")
    is_lower = me % 2 == 0
    half_width = width // 2
    chosen = expert_ids[:, :, None] == jnp.arange(experts, dtype=jnp.int32)[None, None, :]
    dense_probs = jnp.sum(jnp.where(chosen, route_probs[:, :, None], 0.0), axis=1)
    lanes = -(-2 * experts // 128) * 128
    extra = jnp.pad(two_terms(dense_probs), ((0, 0), (0, lanes - 2 * experts)))
    all_tokens = gather_rows(jnp.concatenate([tokens, extra], axis=1))
    all_cot = gather_rows(cotangent)
    wide = join_halves(wide_factors, send(wide_factors, 1), is_lower)
    narrow = narrow_factors
    gate_eff = scaled_weight(gate_weight, wide[0], narrow[0])
    up_eff = scaled_weight(up_weight, wide[1], narrow[1])
    down_eff = scaled_weight(down_weight, narrow[2], wide[2])
    inputs = all_tokens[:, :width]
    lane = jnp.arange(lanes, dtype=jnp.int32)
    own_lanes = (lane % experts == me // 2) & (lane < 2 * experts)
    probs = jnp.sum(
        jnp.where(own_lanes[None, :], all_tokens[:, width:].astype(jnp.float32), 0.0),
        axis=1,
        keepdims=True,
    )
    routed = probs > 0.0
    pre_gate = dot32(inputs, gate_eff)
    pre_up = dot32(inputs, up_eff)
    sigmoid_gate = jax.nn.sigmoid(pre_gate)
    activated = pre_gate * sigmoid_gate
    hidden = jnp.where(routed, activated * pre_up, 0.0)
    grad_full = dot32(all_cot, down_eff, ROWS)
    grad_hidden = probs * grad_full
    own_probs = jnp.sum(hidden * grad_full, axis=1, keepdims=True)
    hidden_scaled = (hidden * probs).astype(jnp.bfloat16)
    grad_gate = jnp.where(
        routed, grad_hidden * pre_up * sigmoid_gate * (1.0 + pre_gate * (1.0 - sigmoid_gate)), 0.0
    ).astype(jnp.bfloat16)
    grad_up = jnp.where(routed, grad_hidden * activated, 0.0).astype(jnp.bfloat16)
    part_in = (dot32(grad_gate, gate_eff, ROWS) + dot32(grad_up, up_eff, ROWS)).astype(jnp.bfloat16)
    prob_lanes = jnp.where(
        own_lanes[None, :],
        jnp.where(lane[None, :] < experts, own_probs, own_probs - own_probs.astype(jnp.bfloat16).astype(jnp.float32)),
        0.0,
    ).astype(jnp.bfloat16)
    summed = scatter_rows(jnp.concatenate([part_in, prob_lanes], axis=1))
    masked_gate = (dot32(inputs, grad_gate, COLS) * gate_weight.astype(jnp.float32)).astype(jnp.bfloat16)
    masked_up = (dot32(inputs, grad_up, COLS) * up_weight.astype(jnp.float32)).astype(jnp.bfloat16)
    masked_down = (dot32(hidden_scaled, all_cot, COLS) * down_weight.astype(jnp.float32)).astype(jnp.bfloat16)
    grad_narrow = jnp.stack(
        [dot32(wide[0], masked_gate), dot32(wide[1], masked_up), dot32(wide[2], masked_down, ROWS)]
    )
    wide_part = jnp.stack(
        [dot32(narrow[0], masked_gate, ROWS), dot32(narrow[1], masked_up, ROWS), dot32(narrow[2], masked_down)]
    )
    keep_part = jnp.where(is_lower, wide_part[:, :, :half_width], wide_part[:, :, half_width:])
    give_part = jnp.where(is_lower, wide_part[:, :, half_width:], wide_part[:, :, :half_width])
    grad_wide = keep_part + send(give_part.astype(jnp.bfloat16), 1).astype(jnp.float32)
    grad_tokens = summed[:, :width].astype(jnp.bfloat16)
    dense_grads = summed[:, width : width + experts] + summed[:, width + experts : width + 2 * experts]
    grad_probs = jnp.sum(jnp.where(chosen, dense_grads[:, None, :], 0.0), axis=2)
    return (grad_tokens, grad_probs, grad_narrow, grad_wide)


def solution(mesh):
    in_specs = (
        P(("groups", "expert"), None),
        P(("groups", "expert"), None),
        P(("groups", "expert"), None),
        P(("groups", "expert"), None),
        P(None, "expert"),
        P(None, "expert"),
        P("expert", None),
        P(None, None, "expert"),
        P(None, None, "expert"),
    )
    out_specs = (
        P(("groups", "expert"), None),
        P(("groups", "expert"), None),
        P("groups", None, "expert"),
        P("groups", None, "expert"),
    )
    return jax.shard_map(body, mesh=mesh, in_specs=in_specs, out_specs=out_specs, check_vma=False)
```

```python
import functools

import jax
import jax.numpy as jnp
from jax import lax
from jax.experimental import pallas as pl
from jax.experimental.pallas import tpu as pltpu
from jax.sharding import PartitionSpec as P

NN = (((1,), (0,)), ((), ()))
NT = (((1,), (1,)), ((), ()))
TN = (((0,), (0,)), ((), ()))
F32, B16 = jnp.float32, jnp.bfloat16


def send(value, mask):
    pairs = [(source, source ^ mask) for source in range(lax.axis_size("expert"))]
    return lax.ppermute(value, "expert", pairs)


def stages():
    found, bit, top = [], 1, lax.axis_size("expert").bit_length() - 1
    while bit < top:
        if bit + 1 < top:
            found.append((2**bit, 2 ** (bit + 1), 3 * 2**bit))
        else:
            found.append((2**bit,))
        bit += 2
    return found


def dot32(left, right, dims=NN):
    return lax.dot_general(left, right, dims, preferred_element_type=F32)


def in_vmem(kernel, outs, args, flops=0):
    moved = sum(a.size * a.dtype.itemsize for a in args)
    moved += sum(s[0] * s[1] * jnp.dtype(d).itemsize for s, d in outs)
    return pl.pallas_call(
        kernel,
        out_shape=[pltpu.VMEM(shape, dtype) for shape, dtype in outs],
        in_specs=[pl.BlockSpec(memory_space=pltpu.VMEM)] * len(args),
        out_specs=[pl.BlockSpec(memory_space=pltpu.VMEM)] * len(outs),
        compiler_params=pltpu.CompilerParams(vmem_limit_bytes=20 * 2**20),
        cost_estimate=pl.CostEstimate(flops=flops, bytes_accessed=moved, transcendentals=0),
    )(*[pltpu.with_memory_space_constraint(a, pltpu.VMEM) for a in args])


def stacked(refs):
    return jnp.concatenate([ref[...].astype(F32) for ref in refs], axis=0)


def chunks_of(width):
    step = next(s for s in (512, 256, 128) if width % s == 0)
    return [pl.ds(at, step) for at in range(0, width, step)]


def weights_kernel(
    gate_ref, up_ref, down_ref, narrow_ref, wide_ref, gate_out, up_out, down_out
):
    for part in chunks_of(gate_ref.shape[0]):
        for i, (src, dst) in enumerate(((gate_ref, gate_out), (up_ref, up_out))):
            factor = 1.0 + dot32(wide_ref[i, :, part], narrow_ref[i], TN)
            dst[part, :] = (src[part, :].astype(F32) * factor).astype(B16)
        factor = 1.0 + dot32(narrow_ref[2], wide_ref[2, :, part], TN)
        down_out[:, part] = (down_ref[:, part].astype(F32) * factor).astype(B16)


def pack_tokens_kernel(masks, rows, capacity, experts, width, *refs):
    pieces, outs = refs[: -len(masks) - 2], refs[-len(masks) - 2 :]
    block = stacked(pieces)
    held = block.astype(B16)
    outs[0][...] = held
    count = block.shape[0]
    slots = count // rows * capacity
    me = lax.axis_index("expert")
    extra = block[:, width:]
    named = (extra > 0.0).astype(B16)
    lane = lax.broadcasted_iota(jnp.int32, (8, extra.shape[1]), 1)
    line = lax.broadcasted_iota(jnp.int32, (8, extra.shape[1]), 0)
    wanted = jnp.zeros((8, extra.shape[1]), F32)
    for i, mask in enumerate(masks):
        wanted = jnp.where((line == i) & (lane == (me ^ mask) // 2), 1.0, wanted)
    chosen = dot32(wanted.astype(B16), named, NT)
    earlier = lax.broadcasted_iota(jnp.int32, (count, count), 0)
    later = lax.broadcasted_iota(jnp.int32, (count, count), 1)
    before = (earlier // rows == later // rows) & (earlier < later)
    slot = dot32(chosen.astype(B16), before.astype(F32).astype(B16))
    to = lax.broadcasted_iota(jnp.int32, (slots, count), 0)
    of = lax.broadcasted_iota(jnp.int32, (slots, count), 1)
    in_block = to // capacity == of // rows
    place = (to % capacity).astype(F32)
    picks = []
    for i in range(len(masks)):
        pick = in_block & (place == slot[i : i + 1, :]) & (chosen[i : i + 1, :] > 0.5)
        pick = jnp.where(pick, 1.0, 0.0)
        picks.append(pick)
        outs[1 + i][...] = dot32(pick.astype(B16), held).astype(B16)
    outs[-1][...] = jnp.concatenate(picks, axis=0)


def pack_kernel(*refs):
    pick_ref, refs = refs[0], refs[1:]
    ways = pick_ref.shape[0] // refs[-1].shape[0]
    pieces, outs = refs[: -ways - 1], refs[-ways - 1 :]
    held = stacked(pieces).astype(B16)
    outs[0][...] = held
    slots = pick_ref.shape[0] // ways
    for i in range(ways):
        pick = pick_ref[i * slots : (i + 1) * slots, :].astype(B16)
        outs[1 + i][...] = dot32(pick, held).astype(B16)


def pre_kernel(experts, width, gate_ref, up_ref, *refs):
    pieces, (x_ref, prob_ref, pre_gate_ref, pre_up_ref) = refs[:-4], refs[-4:]
    for part in chunks_of(width):
        x_ref[:, part] = jnp.concatenate(
            [piece[:, part].astype(F32) for piece in pieces], axis=0
        ).astype(B16)
    extra = jnp.concatenate([piece[:, width:].astype(F32) for piece in pieces], axis=0)
    lane = lax.broadcasted_iota(jnp.int32, extra.shape, 1)
    own = (lane % experts == lax.axis_index("expert") // 2) & (lane < 2 * experts)
    probs = jnp.sum(jnp.where(own, extra, 0.0), axis=1, keepdims=True)
    prob_ref[...] = jnp.broadcast_to(probs, prob_ref.shape)
    pre_gate_ref[...] = dot32(x_ref[...], gate_ref[...])
    pre_up_ref[...] = dot32(x_ref[...], up_ref[...])


def mid_kernel(
    experts, width, gate_ref, up_ref, down_ref, prob_ref, pre_gate_ref, pre_up_ref, *refs
):
    pieces, outs = refs[:-6], refs[-6:]
    y_ref, hidden_ref, grad_gate_ref, grad_up_ref, mine_ref, give_ref = outs
    for part in chunks_of(width):
        y_ref[:, part] = jnp.concatenate(
            [piece[:, part].astype(F32) for piece in pieces], axis=0
        ).astype(B16)
    grad_full = dot32(y_ref[...], down_ref[...], NT)
    pre_gate, pre_up = pre_gate_ref[...], pre_up_ref[...]
    probs = prob_ref[:, :1]
    routed = probs > 0.0
    sigmoid_gate = jax.nn.sigmoid(pre_gate)
    activated = pre_gate * sigmoid_gate
    hidden = jnp.where(routed, activated * pre_up, 0.0)
    hidden_ref[...] = (hidden * probs).astype(B16)
    own_probs = jnp.sum(hidden * grad_full, axis=1, keepdims=True)
    grad_hidden = grad_full * probs
    grad_gate_ref[...] = jnp.where(
        routed, grad_hidden * pre_up * sigmoid_gate * (1.0 + pre_gate * (1.0 - sigmoid_gate)), 0.0
    ).astype(B16)
    grad_up_ref[...] = jnp.where(routed, grad_hidden * activated, 0.0).astype(B16)
    half = mine_ref.shape[0]
    for part in chunks_of(width):
        product = dot32(grad_gate_ref[...], gate_ref[part, :], NT)
        product = product + dot32(grad_up_ref[...], up_ref[part, :], NT)
        mine_ref[:, part] = product[:half].astype(B16)
        give_ref[:, part] = product[half:].astype(B16)
    lanes = mine_ref.shape[1] - width
    lane = lax.broadcasted_iota(jnp.int32, (2 * half, lanes), 1)
    expert = lax.axis_index("expert") // 2
    high = own_probs.astype(B16).astype(F32)
    extra = jnp.where(lane == expert, high, jnp.where(lane == expert + experts, own_probs - high, 0.0))
    mine_ref[:, width:] = extra[:half].astype(B16)
    give_ref[:, width:] = extra[half:].astype(B16)


def first_sum_kernel(experts, width, mine_ref, other_ref, own_ref, *outs):
    total = mine_ref[...].astype(F32) + other_ref[...].astype(F32)
    count = own_ref.shape[0]
    own_ref[...] = total[:count]
    rest, extra = total[count:, :width], total[count:, width:]
    lane = lax.broadcasted_iota(jnp.int32, extra.shape, 1)
    lost = jnp.where(lane < experts, extra - extra.astype(B16).astype(F32), 0.0)
    extra = extra + pltpu.roll(lost, experts, 1) - lost
    slots = outs[0].shape[0]
    for i, out in enumerate(outs):
        out[:, :width] = rest[i * slots : (i + 1) * slots].astype(B16)
        out[:, width:] = extra[i * slots : (i + 1) * slots].astype(B16)


def second_sum_kernel(pick_ref, own_ref, *refs):
    came, out = refs[:-1], refs[-1]
    out[...] = own_ref[...] + dot32(pick_ref[...].astype(B16), stacked(came).astype(B16), TN)


def grads_kernel(
    x_ref, y_ref, hidden_ref, grad_gate_ref, grad_up_ref, gate_ref, up_ref, down_ref,
    narrow_ref, wide_ref, after_ref, narrow_out, wide_out,
):
    del after_ref
    narrow_out[...] = jnp.zeros_like(narrow_out)
    rank = narrow_ref.shape[1]
    for part in chunks_of(x_ref.shape[1]):
        for i, (grad, weight) in enumerate(((grad_gate_ref, gate_ref), (grad_up_ref, up_ref))):
            masked = dot32(x_ref[:, part], grad[...], TN) * weight[part, :].astype(F32)
            masked = masked.astype(B16)
            lines = pl.ds(i * rank, rank)
            narrow_out[lines, :] += dot32(wide_ref[i, :, part], masked)
            wide_out[lines, part] = dot32(narrow_ref[i], masked, NT)
        masked = dot32(hidden_ref[...], y_ref[:, part], TN) * down_ref[:, part].astype(F32)
        masked = masked.astype(B16)
        lines = pl.ds(2 * rank, rank)
        narrow_out[lines, :] += dot32(wide_ref[2, :, part], masked, NT)
        wide_out[lines, part] = dot32(narrow_ref[2], masked)


def join_halves(mine, other, is_lower):
    return jnp.where(
        is_lower, jnp.concatenate([mine, other], axis=-1), jnp.concatenate([other, mine], axis=-1)
    )


def body(
    tokens,
    cotangent,
    route_probs,
    expert_ids,
    gate_weight,
    up_weight,
    down_weight,
    narrow,
    wide_factors,
):
    rows, width = tokens.shape
    hidden_units = gate_weight.shape[1]
    top_count = expert_ids.shape[1]
    devices = lax.axis_size("expert")
    experts = devices // 2
    capacity = min(rows, max(2, (3 * rows * top_count + 2 * experts - 1) // (2 * experts)))
    is_lower = lax.axis_index("expert") % 2 == 0
    half_width = width // 2
    near, far = stages()[0], stages()[1:]
    count = rows * devices // 2 // (len(near) + 1)
    slots = count // rows * capacity
    half = count + len(near) * slots
    lanes = -(-2 * experts // 128) * 128
    full = width + lanes

    chosen = expert_ids[:, :, None] == jnp.arange(experts, dtype=jnp.int32)[None, None, :]
    dense = jnp.sum(jnp.where(chosen, route_probs[:, :, None], 0.0), axis=1)
    high = dense.astype(B16)
    low = (dense - high.astype(F32)).astype(B16)
    tail = jnp.zeros((rows, lanes - 2 * experts), B16)
    message = jnp.concatenate([tokens, high, low, tail], axis=1)

    def pieces_of(block):
        for masks in reversed(far[1:]):
            block = jnp.concatenate([block] + [send(block, mask) for mask in masks], axis=0)
        if far:
            return [block] + [send(block, mask) for mask in far[0]]
        return [block]

    def all_of(held, packed):
        mine = jnp.concatenate([held] + [send(p, mask) for p, mask in zip(packed, near)], axis=0)
        return [mine, send(mine, 1)]

    token_pieces = pieces_of(message)
    packed_type = [((slots, full), B16)] * len(near)
    held, *packed, pick = in_vmem(
        functools.partial(pack_tokens_kernel, near, rows, capacity, experts, width),
        [((count, full), B16)] + packed_type + [((len(near) * slots, count), F32)],
        token_pieces,
    )
    token_rows = all_of(held, packed)
    cot_pieces = pieces_of(cotangent)
    cot_held, *cot_packed = in_vmem(
        pack_kernel,
        [((count, width), B16)] + [((slots, width), B16)] * len(near),
        [pick] + cot_pieces,
    )
    cot_rows = all_of(cot_held, cot_packed)

    wide = join_halves(wide_factors, send(wide_factors, 1), is_lower)
    matmul = 2 * 2 * half * width * hidden_units
    weight_type = [((width, hidden_units), B16)] * 2 + [((hidden_units, width), B16)]
    weights = (gate_weight, up_weight, down_weight)
    gate_eff, up_eff, down_eff = in_vmem(
        weights_kernel, weight_type, (*weights, narrow, wide), 3 * matmul
    )
    wide_type, unit_type = ((2 * half, width), B16), ((2 * half, hidden_units), B16)
    x, probs, pre_gate, pre_up = in_vmem(
        functools.partial(pre_kernel, experts, width),
        [wide_type, ((2 * half, 128), F32)] + [((2 * half, hidden_units), F32)] * 2,
        (gate_eff, up_eff, *token_rows),
        2 * matmul,
    )
    y, hidden, grad_gate, grad_up, mine, give = in_vmem(
        functools.partial(mid_kernel, experts, width),
        [wide_type] + [unit_type] * 3 + [((half, full), B16)] * 2,
        (gate_eff, up_eff, down_eff, probs, pre_gate, pre_up, *cot_rows),
        3 * matmul,
    )
    own, *parts = in_vmem(
        functools.partial(first_sum_kernel, experts, width),
        [((count, full), F32)] + packed_type,
        (mine, send(give, 1)),
    )
    rank = narrow.shape[1]
    grad_narrow, wide_part = in_vmem(
        grads_kernel,
        [((3 * rank, hidden_units), F32), ((3 * rank, width), F32)],
        (x, y, hidden, grad_gate, grad_up, *weights, narrow, wide, parts[0]),
        9 * matmul,
    )
    (total,) = in_vmem(
        second_sum_kernel,
        [((count, full), F32)],
        (pick, own, *[send(part, mask) for part, mask in zip(parts, near)]),
    )
    for masks in far:
        pieces = jnp.split(total, len(masks) + 1, axis=0)
        total = pieces[0]
        for piece, mask in zip(pieces[1:], masks):
            total = total + send(piece.astype(B16), mask).astype(F32)
    grad_narrow = grad_narrow.reshape(3, rank, hidden_units)
    wide_part = wide_part.reshape(3, rank, width)
    keep_part = jnp.where(is_lower, wide_part[:, :, :half_width], wide_part[:, :, half_width:])
    give_part = jnp.where(is_lower, wide_part[:, :, half_width:], wide_part[:, :, :half_width])
    grad_wide = keep_part + send(give_part.astype(B16), 1).astype(F32)
    grad_tokens = total[:, :width].astype(B16)
    dense_grads = total[:, width : width + experts] + total[:, width + experts : width + 2 * experts]
    grad_probs = jnp.sum(jnp.where(chosen, dense_grads[:, None, :], 0.0), axis=2)
    return (grad_tokens, grad_probs, grad_narrow, grad_wide)


def solution(mesh):
    in_specs = (
        P(("groups", "expert"), None),
        P(("groups", "expert"), None),
        P(("groups", "expert"), None),
        P(("groups", "expert"), None),
        P(None, "expert"),
        P(None, "expert"),
        P("expert", None),
        P(None, None, "expert"),
        P(None, None, "expert"),
    )
    out_specs = (
        P(("groups", "expert"), None),
        P(("groups", "expert"), None),
        P("groups", None, "expert"),
        P("groups", None, "expert"),
    )
    return jax.shard_map(body, mesh=mesh, in_specs=in_specs, out_specs=out_specs, check_vma=False)
```

```python
import functools

import jax
import jax.numpy as jnp
from jax import lax
from jax.experimental import pallas as pl
from jax.experimental.pallas import tpu as pltpu
from jax.sharding import PartitionSpec as P

NN = (((1,), (0,)), ((), ()))
NT = (((1,), (1,)), ((), ()))
TN = (((0,), (0,)), ((), ()))
F32, B16 = jnp.float32, jnp.bfloat16


def send(value, mask):
    pairs = [(source, source ^ mask) for source in range(lax.axis_size("expert"))]
    return lax.ppermute(value, "expert", pairs)


def stages():
    found, bit, top = [], 1, lax.axis_size("expert").bit_length() - 1
    while bit < top:
        if bit + 1 < top:
            found.append((2**bit, 2 ** (bit + 1), 3 * 2**bit))
        else:
            found.append((2**bit,))
        bit += 2
    return found


def dot32(left, right, dims=NN):
    return lax.dot_general(left, right, dims, preferred_element_type=F32)


def in_vmem(kernel, outs, args, flops=0, outside=0, results=(), scratch=()):
    moved = sum(a.size * a.dtype.itemsize for a in args)
    spaces = [pltpu.HBM] * outside + [pltpu.VMEM] * (len(args) - outside)
    return pl.pallas_call(
        kernel,
        out_shape=[
            (jax.ShapeDtypeStruct if i in results else pltpu.VMEM)(shape, dtype)
            for i, (shape, dtype) in enumerate(outs)
        ],
        in_specs=[pl.BlockSpec(memory_space=space) for space in spaces],
        out_specs=[pl.BlockSpec(memory_space=pltpu.VMEM)] * len(outs),
        scratch_shapes=list(scratch),
        compiler_params=pltpu.CompilerParams(vmem_limit_bytes=20 * 2**20),
        cost_estimate=pl.CostEstimate(flops=flops, bytes_accessed=moved, transcendentals=0),
    )(*[pltpu.with_memory_space_constraint(a, space) for a, space in zip(args, spaces)])


def stacked(refs):
    return jnp.concatenate([ref[...].astype(F32) for ref in refs], axis=0)


def chunks_of(width, step=512):
    return [pl.ds(at, step) for at in range(0, width, step)]


def copied(sources, targets, sems):
    copies = [pltpu.make_async_copy(*pair, sems.at[i]) for i, pair in enumerate(zip(sources, targets))]
    for copy in copies:
        copy.start()
    return copies


def message_kernel(experts, width, *refs):
    sources, out_ref, probs_ref, ids_ref, sems = refs[:4], refs[4], refs[5], refs[6], refs[7]
    tail = out_ref.shape[1] - width
    targets = (out_ref.at[:, :width], out_ref.at[:, tail:], probs_ref, ids_ref)
    copies = copied(sources, targets, sems)
    for copy in copies[2:]:
        copy.wait()
    ids, probs = ids_ref[...], probs_ref[...]
    high = probs.astype(B16).astype(F32)
    low = probs - high
    lane = lax.broadcasted_iota(jnp.int32, (ids.shape[0], tail - width), 1)
    extra = jnp.zeros(lane.shape, F32)
    for k in range(ids.shape[1]):
        one = slice(k, k + 1)
        extra = jnp.where(lane == ids[:, one], high[:, one], extra)
        extra = jnp.where(lane == ids[:, one] + experts, low[:, one], extra)
    out_ref[:, width:tail] = extra.astype(B16)
    for copy in copies[:2]:
        copy.wait()


def weights_into(which, sources, raws, outs, narrow_ref, wide_ref, sems):
    pieces = sems.shape[0] // len(sources)
    parts = []
    for i, (source, raw) in enumerate(zip(sources, raws)):
        step = source.shape[0] // pieces
        for j in range(pieces):
            rows = pl.ds(j * step, step)
            sem = sems.at[i * pieces + j]
            parts.append((i, rows, pltpu.make_async_copy(source.at[rows, :], raw.at[rows, :], sem)))
    ahead = 5
    for _, _, copy in parts[:ahead]:
        copy.start()
    for at, (i, rows, copy) in enumerate(parts):
        copy.wait()
        if at + ahead < len(parts):
            parts[at + ahead][2].start()
        raw, out, kind = raws[i], outs[i], which + i
        if kind < 2:
            for line in range(rows.start, rows.start + rows.size, 128):
                lines = pl.ds(line, 128)
                factor = 1.0 + dot32(wide_ref[kind, :, lines], narrow_ref[kind], TN)
                out[lines, :] = (raw[lines, :].astype(F32) * factor).astype(B16)
        else:
            for lanes in chunks_of(raw.shape[1]):
                factor = 1.0 + dot32(narrow_ref[kind, :, rows], wide_ref[kind, :, lanes], TN)
                out[rows, lanes] = (raw[rows, lanes].astype(F32) * factor).astype(B16)


def weights_kernel(gate_ref, up_ref, down_ref, narrow_hbm, mine_hbm, other_ref, *refs):
    raws, outs, (narrow_out, wide_out, mine_ref, small_sems, sems) = refs[:3], refs[3:6], refs[6:]
    for copy in copied((narrow_hbm, mine_hbm), (narrow_out, mine_ref), small_sems):
        copy.wait()
    half = mine_ref.shape[2]
    is_lower = lax.axis_index("expert") % 2 == 0

    @pl.when(is_lower)
    def _():
        wide_out[:, :, :half] = mine_ref[...]
        wide_out[:, :, half:] = other_ref[...]

    @pl.when(jnp.logical_not(is_lower))
    def _():
        wide_out[:, :, :half] = other_ref[...]
        wide_out[:, :, half:] = mine_ref[...]

    weights_into(0, (gate_ref, up_ref, down_ref), raws, outs, narrow_out, wide_out, sems)


def picks_of(extra, wanted_experts, rows, capacity):
    count, lanes = extra.shape
    slots = count // rows * capacity
    named = (extra > 0.0).astype(B16)
    lane = lax.broadcasted_iota(jnp.int32, (8, lanes), 1)
    line = lax.broadcasted_iota(jnp.int32, (8, lanes), 0)
    wanted = jnp.zeros((8, lanes), F32)
    for i, expert in enumerate(wanted_experts):
        wanted = jnp.where((line == i) & (lane == expert), 1.0, wanted)
    chosen = dot32(wanted.astype(B16), named, NT)
    earlier = lax.broadcasted_iota(jnp.int32, (count, count), 0)
    later = lax.broadcasted_iota(jnp.int32, (count, count), 1)
    before = (earlier // rows == later // rows) & (earlier < later)
    slot = dot32(chosen.astype(B16), before.astype(F32).astype(B16))
    to = lax.broadcasted_iota(jnp.int32, (slots, count), 0)
    of = lax.broadcasted_iota(jnp.int32, (slots, count), 1)
    in_block = to // capacity == of // rows
    place = (to % capacity).astype(F32)
    picks = []
    for i in range(len(wanted_experts)):
        pick = in_block & (place == slot[i : i + 1, :]) & (chosen[i : i + 1, :] > 0.5)
        picks.append(jnp.where(pick, 1.0, 0.0))
    return picks


def pack_kernel(masks, rows, capacity, waits, *refs):
    refs, ways = refs[waits:], min(len(masks), 2)
    pieces, (tokens_out, cot_out, pick_out), outs = (
        refs[: -3 - ways], refs[-3 - ways : -ways], refs[-ways:]
    )
    block = stacked(pieces)
    held = block.astype(B16)
    full, width = tokens_out.shape[1], cot_out.shape[1]
    tokens_out[...] = held[:, :full]
    cot_out[...] = held[:, full:]
    me = lax.axis_index("expert")
    wanted = [(me ^ mask) // 2 for mask in masks]
    picks = picks_of(block[:, width:full], wanted, rows, capacity)
    for pick, out in zip(picks, outs):
        out[...] = dot32(pick.astype(B16), held).astype(B16)
    pick_out[...] = jnp.concatenate(picks, axis=0)


def stack_kernel(tokens_ref, cot_ref, *refs):
    pieces, (tokens_out, cot_out) = refs[:-2], refs[-2:]
    full = tokens_out.shape[1]
    for out, first, own in ((tokens_out, 0, tokens_ref), (cot_out, full, cot_ref)):
        parts = [own[...].astype(F32)]
        parts += [piece[:, first : first + out.shape[1]].astype(F32) for piece in pieces]
        out[...] = jnp.concatenate(parts, axis=0).astype(B16)


def pre_kernel(experts, width, rows, capacity, gate_ref, up_ref, *refs):
    pieces, (x_ref, prob_ref, pre_gate_ref, pre_up_ref, pick_ref) = refs[:-5], refs[-5:]
    count = pick_ref.shape[1]
    crossed = pieces[0][:, width:].astype(F32)[-count:]
    (pick_ref[...],) = picks_of(crossed, [lax.axis_index("expert") // 2], rows, capacity)
    for part in chunks_of(width):
        x_ref[:, part] = jnp.concatenate(
            [piece[:, part].astype(F32) for piece in pieces], axis=0
        ).astype(B16)
    extra = jnp.concatenate([piece[:, width:].astype(F32) for piece in pieces], axis=0)
    lane = lax.broadcasted_iota(jnp.int32, extra.shape, 1)
    own = (lane % experts == lax.axis_index("expert") // 2) & (lane < 2 * experts)
    probs = jnp.sum(jnp.where(own, extra, 0.0), axis=1, keepdims=True)
    prob_ref[...] = jnp.broadcast_to(probs, prob_ref.shape)
    pre_gate_ref[...] = dot32(x_ref[...], gate_ref[...])
    pre_up_ref[...] = dot32(x_ref[...], up_ref[...])


def mid_kernel(
    experts, width, gate_ref, up_ref, down_ref, prob_ref, pre_gate_ref, pre_up_ref, *refs
):
    pieces, outs = refs[:-6], refs[-6:]
    y_ref, hidden_ref, grad_gate_ref, grad_up_ref, mine_ref, give_ref = outs
    for part in chunks_of(width):
        y_ref[:, part] = jnp.concatenate(
            [piece[:, part].astype(F32) for piece in pieces], axis=0
        ).astype(B16)
    grad_full = dot32(y_ref[...], down_ref[...], NT)
    pre_gate, pre_up = pre_gate_ref[...], pre_up_ref[...]
    probs = prob_ref[:, :1]
    routed = probs > 0.0
    sigmoid_gate = jax.nn.sigmoid(pre_gate)
    activated = pre_gate * sigmoid_gate
    hidden = jnp.where(routed, activated * pre_up, 0.0)
    hidden_ref[...] = (hidden * probs).astype(B16)
    own_probs = jnp.sum(hidden * grad_full, axis=1, keepdims=True)
    grad_hidden = grad_full * probs
    grad_gate_ref[...] = jnp.where(
        routed, grad_hidden * pre_up * sigmoid_gate * (1.0 + pre_gate * (1.0 - sigmoid_gate)), 0.0
    ).astype(B16)
    grad_up_ref[...] = jnp.where(routed, grad_hidden * activated, 0.0).astype(B16)
    half = mine_ref.shape[0]
    for part in chunks_of(width):
        product = dot32(grad_gate_ref[...], gate_ref[part, :], NT)
        product = product + dot32(grad_up_ref[...], up_ref[part, :], NT)
        mine_ref[:, part] = product[:half].astype(B16)
        give_ref[:, part] = product[half:].astype(B16)
    lanes = mine_ref.shape[1] - width
    lane = lax.broadcasted_iota(jnp.int32, (2 * half, lanes), 1)
    expert = lax.axis_index("expert") // 2
    high = own_probs.astype(B16).astype(F32)
    extra = jnp.where(lane == expert, high, jnp.where(lane == expert + experts, own_probs - high, 0.0))
    mine_ref[:, width:] = extra[:half].astype(B16)
    give_ref[:, width:] = extra[half:].astype(B16)


def first_sum_kernel(experts, width, mine_ref, other_ref, pick_ref, after_ref, own_ref, *outs):
    del after_ref
    total = mine_ref[...].astype(F32) + other_ref[...].astype(F32)
    count = own_ref.shape[0]
    own_ref[...] = total[:count]
    extra = total[count:, width:]
    lane = lax.broadcasted_iota(jnp.int32, extra.shape, 1)
    lost = jnp.where(lane < experts, extra - extra.astype(B16).astype(F32), 0.0)
    extra = extra + pltpu.roll(lost, experts, 1) - lost
    slots = outs[0].shape[0]
    for i, out in enumerate(outs):
        if i < 2:
            part = slice(i * slots, (i + 1) * slots)
            out[:, :width] = total[count:, :width][part].astype(B16)
            out[:, width:] = extra[part].astype(B16)
        else:
            pick = pick_ref[...].astype(B16)
            out[:, :width] = dot32(pick, total[-count:, :width].astype(B16)).astype(B16)
            out[:, width:] = dot32(pick, extra[-count:].astype(B16)).astype(B16)


def second_sum_kernel(ways, pick_ref, own_ref, *refs):
    came, own_out, outs = refs[: -2 - ways], refs[-1 - ways], refs[len(refs) - ways :]
    total = own_ref[...] + dot32(pick_ref[...].astype(B16), stacked(came).astype(B16), TN)
    count = own_out.shape[0]
    own_out[...] = total[:count]
    for i, out in enumerate(outs):
        out[...] = total[(i + 1) * count : (i + 2) * count].astype(B16)


def down_grads_kernel(y_ref, hidden_ref, down_ref, narrow_ref, wide_ref, narrow_out, wide_out):
    width = y_ref.shape[1]
    narrow_out[...] = jnp.zeros_like(narrow_out)
    for part in chunks_of(width, width // 2):
        masked = dot32(hidden_ref[...], y_ref[:, part], TN) * down_ref[:, part].astype(F32)
        masked = masked.astype(B16)
        narrow_out[...] += dot32(wide_ref[2, :, part], masked, NT)
        wide_out[:, part] = dot32(narrow_ref[2], masked)


def feature_grads_kernel(
    x_ref, grad_gate_ref, grad_up_ref, gate_ref, up_ref, narrow_ref, wide_ref, after_ref,
    down_narrow_ref, down_wide_ref, narrow_out, keep_out, give_out, wide_all,
):
    del after_ref
    width, rank = x_ref.shape[1], narrow_ref.shape[1]
    lines = pl.ds(2 * rank, rank)
    narrow_out[lines, :] = down_narrow_ref[...]
    wide_all[lines, :] = down_wide_ref[...]
    for i, (grad, raw) in enumerate(((grad_gate_ref, gate_ref), (grad_up_ref, up_ref))):
        lines = pl.ds(i * rank, rank)
        narrow_out[lines, :] = jnp.zeros((rank, narrow_out.shape[1]), F32)
        for part in chunks_of(width, width // 2):
            masked = dot32(x_ref[:, part], grad[...], TN) * raw[part, :].astype(F32)
            masked = masked.astype(B16)
            narrow_out[lines, :] += dot32(wide_ref[i, :, part], masked)
            wide_all[lines, part] = dot32(narrow_ref[i], masked, NT)
    half = keep_out.shape[1]
    is_lower = lax.axis_index("expert") % 2 == 0

    @pl.when(is_lower)
    def _():
        keep_out[...] = wide_all[:, :half]
        give_out[...] = wide_all[:, half:].astype(B16)

    @pl.when(jnp.logical_not(is_lower))
    def _():
        keep_out[...] = wide_all[:, half:]
        give_out[...] = wide_all[:, :half].astype(B16)


def last_kernel(experts, width, ids_ref, keep_ref, given_ref, own_ref, *refs):
    came, (tokens_out, probs_out, wide_out) = refs[:-3], refs[-3:]
    total = own_ref[...]
    for ref in came:
        total = total + ref[...].astype(F32)
    tokens_out[...] = total[:, :width].astype(B16)
    extra, ids = total[:, width:], ids_ref[...]
    lane = lax.broadcasted_iota(jnp.int32, extra.shape, 1)
    spot = lax.broadcasted_iota(jnp.int32, ids.shape, 1)
    probs = jnp.zeros(ids.shape, F32)
    for k in range(ids.shape[1]):
        wanted = ids[:, k : k + 1]
        found = jnp.where((lane == wanted) | (lane == wanted + experts), extra, 0.0)
        probs = jnp.where(spot == k, jnp.sum(found, axis=1, keepdims=True), probs)
    probs_out[...] = probs
    wide_out[...] = keep_ref[...] + given_ref[...].astype(F32)


def body(
    tokens,
    cotangent,
    route_probs,
    expert_ids,
    gate_weight,
    up_weight,
    down_weight,
    narrow,
    wide_factors,
):
    rows, width = tokens.shape
    hidden_units = gate_weight.shape[1]
    top_count = expert_ids.shape[1]
    rank = narrow.shape[1]
    devices = lax.axis_size("expert")
    experts = devices // 2
    capacity = min(rows, max(2, (3 * rows * top_count + 2 * experts - 1) // (2 * experts)))
    near, far = stages()[0], stages()[1:]
    count = rows * devices // 2 // (len(near) + 1)
    slots = count // rows * capacity
    half = count + len(near[:2]) * slots + len(near[2:]) * count
    lanes = -(-2 * experts // 128) * 128
    full = width + lanes

    def pieces_of(block):
        for masks in reversed(far[1:]):
            block = jnp.concatenate([block] + [send(block, mask) for mask in masks], axis=0)
        if far:
            return [block] + [send(block, mask) for mask in far[0]]
        return [block]

    (message,) = in_vmem(
        functools.partial(message_kernel, experts, width),
        [((rows, full + width), B16)],
        (tokens, cotangent, route_probs, expert_ids),
        outside=4,
        scratch=[
            pltpu.VMEM(route_probs.shape, F32),
            pltpu.VMEM(expert_ids.shape, jnp.int32),
            pltpu.SemaphoreType.DMA((4,)),
        ],
    )
    pieces = pieces_of(message)
    crossed = [send(message, mask) for mask in near[2:]]
    matmul = 2 * 2 * half * width * hidden_units
    weights = (gate_weight, up_weight, down_weight)
    gate_raw, up_raw, down_raw, gate_eff, up_eff, down_eff, narrow, wide = in_vmem(
        weights_kernel,
        [(weight.shape, B16) for weight in weights] * 2
        + [(narrow.shape, B16), ((3, rank, width), B16)],
        (*weights, narrow, wide_factors, send(wide_factors, 1)),
        3 * matmul,
        outside=5,
        scratch=[
            pltpu.VMEM(wide_factors.shape, B16),
            pltpu.SemaphoreType.DMA((2,)),
            pltpu.SemaphoreType.DMA((12,)),
        ],
    )
    held, cot_held, pick, *packed = in_vmem(
        functools.partial(pack_kernel, near, rows, capacity, 1 + len(crossed)),
        [((count, full), B16), ((count, width), B16), ((len(near) * slots, count), F32)]
        + [((slots, full + width), B16)] * len(near[:2]),
        [wide] + crossed + pieces,
    )
    came = [send(block, mask) for block, mask in zip(packed, near)]
    for block in crossed:
        came += pieces_of(block)
    mine_rows, cot_mine = in_vmem(
        stack_kernel, [((half, full), B16), ((half, width), B16)], [held, cot_held, *came]
    )
    token_rows = [mine_rows, send(mine_rows, 1)]
    cot_rows = [cot_mine, send(cot_mine, 1)]
    packed_type = [((slots, full), B16)] * len(near)

    wide_type, unit_type = ((2 * half, width), B16), ((2 * half, hidden_units), B16)
    x, probs, pre_gate, pre_up, cross_pick = in_vmem(
        functools.partial(pre_kernel, experts, width, rows, capacity),
        [wide_type, ((2 * half, 128), F32)]
        + [((2 * half, hidden_units), F32)] * 2
        + [((slots, count), F32)],
        (gate_eff, up_eff, *token_rows),
        2 * matmul,
    )
    y, hidden, grad_gate, grad_up, mine, give = in_vmem(
        functools.partial(mid_kernel, experts, width),
        [wide_type] + [unit_type] * 3 + [((half, full), B16)] * 2,
        (gate_eff, up_eff, down_eff, probs, pre_gate, pre_up, *cot_rows),
        3 * matmul,
    )
    other = send(give, 1)
    down_narrow, down_wide = in_vmem(
        down_grads_kernel,
        [((rank, hidden_units), F32), ((rank, width), F32)],
        (y, hidden, down_raw, narrow, wide),
        2 * matmul,
    )
    own, *parts = in_vmem(
        functools.partial(first_sum_kernel, experts, width),
        [((count, full), F32)] + packed_type,
        (mine, other, cross_pick, down_narrow),
    )
    grad_narrow, keep, give = in_vmem(
        feature_grads_kernel,
        [((3 * rank, hidden_units), F32), ((3 * rank, width // 2), F32), ((3 * rank, width // 2), B16)],
        (x, grad_gate, grad_up, gate_raw, up_raw, narrow, wide, parts[0], down_narrow, down_wide),
        4 * matmul,
        results=(0,),
        scratch=[pltpu.VMEM((3 * rank, width), F32)],
    )
    ways = len(far[0]) if far else 0
    own, *parts = in_vmem(
        functools.partial(second_sum_kernel, ways),
        [((count // (ways + 1), full), F32)] + [((count // (ways + 1), full), B16)] * ways,
        (pick, own, *[send(part, mask) for part, mask in zip(parts, near)], keep),
    )
    came = [send(part, mask) for part, mask in zip(parts, far[0] if far else ())]
    for masks in far[1:]:
        total = own
        for part in came:
            total = total + part.astype(F32)
        own, *parts = jnp.split(total, len(masks) + 1, axis=0)
        came = [send(part.astype(B16), mask) for part, mask in zip(parts, masks)]
    grad_tokens, grad_probs, grad_wide = in_vmem(
        functools.partial(last_kernel, experts, width),
        [((rows, width), B16), (expert_ids.shape, F32), ((3 * rank, width // 2), F32)],
        (expert_ids, keep, send(give, 1), own, *came),
        results=(0, 1, 2),
    )
    return (
        grad_tokens,
        grad_probs,
        grad_narrow.reshape(3, rank, hidden_units),
        grad_wide.reshape(3, rank, width // 2),
    )


def solution(mesh):
    in_specs = (
        P(("groups", "expert"), None),
        P(("groups", "expert"), None),
        P(("groups", "expert"), None),
        P(("groups", "expert"), None),
        P(None, "expert"),
        P(None, "expert"),
        P("expert", None),
        P(None, None, "expert"),
        P(None, None, "expert"),
    )
    out_specs = (
        P(("groups", "expert"), None),
        P(("groups", "expert"), None),
        P("groups", None, "expert"),
        P("groups", None, "expert"),
    )
    return jax.shard_map(body, mesh=mesh, in_specs=in_specs, out_specs=out_specs, check_vma=False)
```

```python
import functools
import math

import jax
import jax.numpy as jnp
from jax import lax
from jax.experimental import pallas as pl
from jax.experimental.pallas import tpu as pltpu
from jax.sharding import PartitionSpec as P

NN = (((1,), (0,)), ((), ()))
NT = (((1,), (1,)), ((), ()))
TN = (((0,), (0,)), ((), ()))
F32, B16 = jnp.float32, jnp.bfloat16


def send(value, mask):
    pairs = [(source, source ^ mask) for source in range(lax.axis_size("expert"))]
    return lax.ppermute(value, "expert", pairs)


def stages():
    found, bit, top = [], 1, lax.axis_size("expert").bit_length() - 1
    while bit < top:
        if bit + 1 < top:
            found.append((2**bit, 2 ** (bit + 1), 3 * 2**bit))
        else:
            found.append((2**bit,))
        bit += 2
    return found


def dot32(left, right, dims=NN):
    return lax.dot_general(left, right, dims, preferred_element_type=F32)


def in_vmem(kernel, outs, args, flops=0, outside=0, results=(), scratch=()):
    moved = sum(a.size * a.dtype.itemsize for a in args)
    spaces = [pltpu.HBM] * outside + [pltpu.VMEM] * (len(args) - outside)
    return pl.pallas_call(
        kernel,
        out_shape=[
            (jax.ShapeDtypeStruct if i in results else pltpu.VMEM)(shape, dtype)
            for i, (shape, dtype) in enumerate(outs)
        ],
        in_specs=[pl.BlockSpec(memory_space=space) for space in spaces],
        out_specs=[pl.BlockSpec(memory_space=pltpu.VMEM)] * len(outs),
        scratch_shapes=list(scratch),
        compiler_params=pltpu.CompilerParams(vmem_limit_bytes=20 * 2**20),
        cost_estimate=pl.CostEstimate(flops=flops, bytes_accessed=moved, transcendentals=0),
    )(*[pltpu.with_memory_space_constraint(a, space) for a, space in zip(args, spaces)])


def stacked(refs):
    return jnp.concatenate([ref[...].astype(F32) for ref in refs], axis=0)


def chunks_of(width, step=512):
    return [pl.ds(at, step) for at in range(0, width, step)]


def copied(sources, targets, sems):
    copies = [pltpu.make_async_copy(*pair, sems.at[i]) for i, pair in enumerate(zip(sources, targets))]
    for copy in copies:
        copy.start()
    return copies


def message_kernel(experts, width, *refs):
    sources, out_ref, probs_ref, ids_ref, sems = refs[:4], refs[4], refs[5], refs[6], refs[7]
    tail = out_ref.shape[1] - width
    targets = (out_ref.at[:, :width], out_ref.at[:, tail:], probs_ref, ids_ref)
    copies = copied(sources, targets, sems)
    for copy in copies[2:]:
        copy.wait()
    ids, probs = ids_ref[...], probs_ref[...]
    high = probs.astype(B16).astype(F32)
    low = probs - high
    lane = lax.broadcasted_iota(jnp.int32, (ids.shape[0], tail - width), 1)
    extra = jnp.zeros(lane.shape, F32)
    for k in range(ids.shape[1]):
        one = slice(k, k + 1)
        extra = jnp.where(lane == ids[:, one], high[:, one], extra)
        extra = jnp.where(lane == ids[:, one] + experts, low[:, one], extra)
    out_ref[:, width:tail] = extra.astype(B16)
    for copy in copies[:2]:
        copy.wait()


def weights_into(which, sources, raws, outs, narrow_ref, wide_ref, sems):
    pieces = sems.shape[0] // len(sources)
    parts = []
    for i, (source, raw) in enumerate(zip(sources, raws)):
        step = source.shape[0] // pieces
        for j in range(pieces):
            rows = pl.ds(j * step, step)
            sem = sems.at[i * pieces + j]
            parts.append((i, rows, pltpu.make_async_copy(source.at[rows, :], raw.at[rows, :], sem)))
    ahead = 5
    for _, _, copy in parts[:ahead]:
        copy.start()
    for at, (i, rows, copy) in enumerate(parts):
        copy.wait()
        if at + ahead < len(parts):
            parts[at + ahead][2].start()
        raw, out, kind = raws[i], outs[i], which + i
        if kind < 2:
            for line in range(rows.start, rows.start + rows.size, 128):
                lines = pl.ds(line, 128)
                factor = 1.0 + dot32(wide_ref[kind, :, lines], narrow_ref[kind], TN)
                out[lines, :] = (raw[lines, :].astype(F32) * factor).astype(B16)
        else:
            for lanes in chunks_of(raw.shape[1]):
                factor = 1.0 + dot32(narrow_ref[kind, :, rows], wide_ref[kind, :, lanes], TN)
                out[rows, lanes] = (raw[rows, lanes].astype(F32) * factor).astype(B16)


def weights_kernel(gate_ref, up_ref, down_ref, narrow_hbm, mine_hbm, other_ref, *refs):
    raws, outs, (narrow_out, wide_out, mine_ref, small_sems, sems) = refs[:3], refs[3:6], refs[6:]
    for copy in copied((narrow_hbm, mine_hbm), (narrow_out, mine_ref), small_sems):
        copy.wait()
    half = mine_ref.shape[2]
    is_lower = lax.axis_index("expert") % 2 == 0

    @pl.when(is_lower)
    def _():
        wide_out[:, :, :half] = mine_ref[...]
        wide_out[:, :, half:] = other_ref[...]

    @pl.when(jnp.logical_not(is_lower))
    def _():
        wide_out[:, :, :half] = other_ref[...]
        wide_out[:, :, half:] = mine_ref[...]

    weights_into(0, (gate_ref, up_ref, down_ref), raws, outs, narrow_out, wide_out, sems)


def picks_of(extra, wanted_experts, rows, capacity):
    count, lanes = extra.shape
    slots = count // rows * capacity
    named = (extra > 0.0).astype(B16)
    kinds = -(-len(wanted_experts) // 8) * 8
    lane = lax.broadcasted_iota(jnp.int32, (kinds, lanes), 1)
    line = lax.broadcasted_iota(jnp.int32, (kinds, lanes), 0)
    wanted = jnp.zeros((kinds, lanes), F32)
    for i, expert in enumerate(wanted_experts):
        wanted = jnp.where((line == i) & (lane == expert), 1.0, wanted)
    chosen = dot32(wanted.astype(B16), named, NT)
    earlier = lax.broadcasted_iota(jnp.int32, (count, count), 0)
    later = lax.broadcasted_iota(jnp.int32, (count, count), 1)
    before = (earlier // rows == later // rows) & (earlier < later)
    slot = dot32(chosen.astype(B16), before.astype(F32).astype(B16))
    to = lax.broadcasted_iota(jnp.int32, (slots, count), 0)
    of = lax.broadcasted_iota(jnp.int32, (slots, count), 1)
    in_block = to // capacity == of // rows
    place = (to % capacity).astype(F32)
    picks = []
    for i in range(len(wanted_experts)):
        pick = in_block & (place == slot[i : i + 1, :]) & (chosen[i : i + 1, :] > 0.5)
        picks.append(jnp.where(pick, 1.0, 0.0))
    return picks


def folds_of(rows, capacity, lanes):
    folds = rows // math.gcd(rows, capacity)
    return folds, -(-lanes // (128 * folds)) * 128


def write_rows(outs, rows):
    first = 0
    for out in outs:
        out[...] = rows[first : first + out.shape[0]].astype(B16)
        first += out.shape[0]


def pack_kernel(masks, offsets, rows, capacity, after_ref, *refs):
    del after_ref
    crossing = len(masks) > 2
    taken = len(refs) - 3 - len(masks[:2]) - crossing * len(offsets)
    blocks, refs = refs[:taken], refs[taken:]
    tokens_out, cot_out, pick_out, outs = *refs[:3], refs[3:]
    block = stacked(blocks[crossing:])
    held = block.astype(B16)
    full, width = tokens_out.shape[1], cot_out.shape[1]
    tokens_out[...] = held[:, :full]
    cot_out[...] = held[:, full:]
    me = lax.axis_index("expert")
    picks = picks_of(block[:, width:full], [(me ^ m) // 2 for m in masks], rows, capacity)
    pick_out[...] = jnp.concatenate(picks, axis=0)
    write_rows(outs[: len(picks[:2])], dot32(jnp.concatenate(picks[:2], axis=0).astype(B16), held))
    if crossing:
        block = blocks[0][...].astype(F32)
        lanes = block.shape[1]
        folds, step = folds_of(rows, capacity, lanes)
        extra = jnp.concatenate([block[:, width:full]] * folds, axis=0)
        if folds * step > lanes:
            block = jnp.concatenate([block, jnp.zeros((rows, folds * step - lanes), F32)], axis=1)
        pieces = [block[:, i * step : (i + 1) * step] for i in range(folds)]
        laid = jnp.concatenate(pieces, axis=0).astype(B16)
        picks = picks_of(extra, [(me ^ offset) // 2 for offset in offsets], rows, capacity)
        write_rows(outs[2:], dot32(jnp.concatenate(picks, axis=0).astype(B16), laid))


def unfolded(refs, folds):
    laid = stacked(refs).astype(B16)
    total, blocks = laid.shape[0], len(refs)
    capacity = total // (folds * blocks)
    to = lax.broadcasted_iota(jnp.int32, (total, total), 0)
    of = lax.broadcasted_iota(jnp.int32, (total, total), 1)
    same = to % capacity == of % capacity
    same &= to // (blocks * capacity) == of // capacity % folds
    same &= to // capacity % blocks == of // (folds * capacity)
    moved = dot32(jnp.where(same, 1.0, 0.0).astype(B16), laid)
    slots = blocks * capacity
    return jnp.concatenate([moved[i * slots : (i + 1) * slots] for i in range(folds)], axis=1)


def stack_kernel(folds, beside, order, tokens_ref, cot_ref, *refs):
    came, (tokens_out, cot_out) = refs[:-2], refs[-2:]
    came = [came[order.index(i)] for i in range(len(order))]
    near, folded = came[:beside], came[beside:]
    pieces = [ref[...].astype(F32) for ref in near]
    if folded:
        pieces.append(unfolded(folded, folds))
    full, both = tokens_out.shape[1], tokens_out.shape[1] + cot_out.shape[1]
    for out, lanes, own in (
        (tokens_out, slice(0, full), tokens_ref), (cot_out, slice(full, both), cot_ref)
    ):
        parts = [own[...].astype(F32)] + [piece[:, lanes] for piece in pieces]
        out[...] = jnp.concatenate(parts, axis=0).astype(B16)


def pre_kernel(experts, width, gate_ref, up_ref, *refs):
    pieces, (x_ref, prob_ref, pre_gate_ref, pre_up_ref) = refs[:-4], refs[-4:]
    for part in chunks_of(width):
        x_ref[:, part] = jnp.concatenate(
            [piece[:, part].astype(F32) for piece in pieces], axis=0
        ).astype(B16)
    extra = jnp.concatenate([piece[:, width:].astype(F32) for piece in pieces], axis=0)
    lane = lax.broadcasted_iota(jnp.int32, extra.shape, 1)
    own = (lane % experts == lax.axis_index("expert") // 2) & (lane < 2 * experts)
    probs = jnp.sum(jnp.where(own, extra, 0.0), axis=1, keepdims=True)
    prob_ref[...] = jnp.broadcast_to(probs, prob_ref.shape)
    pre_gate_ref[...] = dot32(x_ref[...], gate_ref[...])
    pre_up_ref[...] = dot32(x_ref[...], up_ref[...])


def mid_kernel(
    experts, width, gate_ref, up_ref, down_ref, prob_ref, pre_gate_ref, pre_up_ref, *refs
):
    pieces, outs = refs[:-6], refs[-6:]
    y_ref, hidden_ref, grad_gate_ref, grad_up_ref, mine_ref, give_ref = outs
    for part in chunks_of(width):
        y_ref[:, part] = jnp.concatenate(
            [piece[:, part].astype(F32) for piece in pieces], axis=0
        ).astype(B16)
    grad_full = dot32(y_ref[...], down_ref[...], NT)
    pre_gate, pre_up = pre_gate_ref[...], pre_up_ref[...]
    probs = prob_ref[:, :1]
    routed = probs > 0.0
    sigmoid_gate = jax.nn.sigmoid(pre_gate)
    activated = pre_gate * sigmoid_gate
    hidden = jnp.where(routed, activated * pre_up, 0.0)
    hidden_ref[...] = (hidden * probs).astype(B16)
    own_probs = jnp.sum(hidden * grad_full, axis=1, keepdims=True)
    grad_hidden = grad_full * probs
    grad_gate_ref[...] = jnp.where(
        routed, grad_hidden * pre_up * sigmoid_gate * (1.0 + pre_gate * (1.0 - sigmoid_gate)), 0.0
    ).astype(B16)
    grad_up_ref[...] = jnp.where(routed, grad_hidden * activated, 0.0).astype(B16)
    half = mine_ref.shape[0]
    for part in chunks_of(width):
        product = dot32(grad_gate_ref[...], gate_ref[part, :], NT)
        product = product + dot32(grad_up_ref[...], up_ref[part, :], NT)
        mine_ref[:, part] = product[:half].astype(B16)
        give_ref[:, part] = product[half:].astype(B16)
    lanes = mine_ref.shape[1] - width
    lane = lax.broadcasted_iota(jnp.int32, (2 * half, lanes), 1)
    expert = lax.axis_index("expert") // 2
    high = own_probs.astype(B16).astype(F32)
    extra = jnp.where(lane == expert, high, jnp.where(lane == expert + experts, own_probs - high, 0.0))
    mine_ref[:, width:] = extra[:half].astype(B16)
    give_ref[:, width:] = extra[half:].astype(B16)


def first_sum_kernel(experts, width, mine_ref, other_ref, after_ref, own_ref, *outs):
    del after_ref
    total = mine_ref[...].astype(F32) + other_ref[...].astype(F32)
    count = own_ref.shape[0]
    own_ref[...] = total[:count]
    extra = total[count:, width:]
    lane = lax.broadcasted_iota(jnp.int32, extra.shape, 1)
    lost = jnp.where(lane < experts, extra - extra.astype(B16).astype(F32), 0.0)
    extra = extra + pltpu.roll(lost, experts, 1) - lost
    slots = outs[0].shape[0]
    for i, out in enumerate(outs):
        part = slice(i * slots, (i + 1) * slots)
        out[:, :width] = total[count:, :width][part].astype(B16)
        out[:, width:] = extra[part].astype(B16)


def second_sum_kernel(ways, pick_ref, own_ref, *refs):
    came, own_out, outs = refs[: -2 - ways], refs[-1 - ways], refs[len(refs) - ways :]
    came = came[1:] + came[:1]
    total = own_ref[...] + dot32(pick_ref[...].astype(B16), stacked(came).astype(B16), TN)
    count = own_out.shape[0]
    own_out[...] = total[:count]
    for i, out in enumerate(outs):
        out[...] = total[(i + 1) * count : (i + 2) * count].astype(B16)


def down_grads_kernel(y_ref, hidden_ref, down_ref, narrow_ref, wide_ref, narrow_out, wide_out):
    width = y_ref.shape[1]
    narrow_out[...] = jnp.zeros_like(narrow_out)
    for part in chunks_of(width, width // 2):
        masked = dot32(hidden_ref[...], y_ref[:, part], TN) * down_ref[:, part].astype(F32)
        masked = masked.astype(B16)
        narrow_out[...] += dot32(wide_ref[2, :, part], masked, NT)
        wide_out[:, part] = dot32(narrow_ref[2], masked)


def feature_grads_kernel(
    x_ref, grad_gate_ref, grad_up_ref, gate_ref, up_ref, narrow_ref, wide_ref, after_ref,
    down_narrow_ref, down_wide_ref, narrow_out, keep_out, give_out, wide_all,
):
    del after_ref
    width, rank = x_ref.shape[1], narrow_ref.shape[1]
    lines = pl.ds(2 * rank, rank)
    narrow_out[lines, :] = down_narrow_ref[...]
    wide_all[lines, :] = down_wide_ref[...]
    for i, (grad, raw) in enumerate(((grad_gate_ref, gate_ref), (grad_up_ref, up_ref))):
        lines = pl.ds(i * rank, rank)
        narrow_out[lines, :] = jnp.zeros((rank, narrow_out.shape[1]), F32)
        for part in chunks_of(width, width // 2):
            masked = dot32(x_ref[:, part], grad[...], TN) * raw[part, :].astype(F32)
            masked = masked.astype(B16)
            narrow_out[lines, :] += dot32(wide_ref[i, :, part], masked)
            wide_all[lines, part] = dot32(narrow_ref[i], masked, NT)
    half = keep_out.shape[1]
    is_lower = lax.axis_index("expert") % 2 == 0

    @pl.when(is_lower)
    def _():
        keep_out[...] = wide_all[:, :half]
        give_out[...] = wide_all[:, half:].astype(B16)

    @pl.when(jnp.logical_not(is_lower))
    def _():
        keep_out[...] = wide_all[:, half:]
        give_out[...] = wide_all[:, :half].astype(B16)


def wide_kernel(keep_ref, given_ref, wide_out):
    wide_out[...] = keep_ref[...] + given_ref[...].astype(F32)


def last_kernel(experts, width, ids_ref, own_ref, *refs):
    came, (tokens_out, probs_out) = refs[:-2], refs[-2:]
    total = own_ref[...]
    for ref in came:
        total = total + ref[...].astype(F32)
    tokens_out[...] = total[:, :width].astype(B16)
    extra, ids = total[:, width:], ids_ref[...]
    lane = lax.broadcasted_iota(jnp.int32, extra.shape, 1)
    spot = lax.broadcasted_iota(jnp.int32, ids.shape, 1)
    probs = jnp.zeros(ids.shape, F32)
    for k in range(ids.shape[1]):
        wanted = ids[:, k : k + 1]
        found = jnp.where((lane == wanted) | (lane == wanted + experts), extra, 0.0)
        probs = jnp.where(spot == k, jnp.sum(found, axis=1, keepdims=True), probs)
    probs_out[...] = probs


def body(
    tokens,
    cotangent,
    route_probs,
    expert_ids,
    gate_weight,
    up_weight,
    down_weight,
    narrow,
    wide_factors,
):
    rows, width = tokens.shape
    hidden_units = gate_weight.shape[1]
    top_count = expert_ids.shape[1]
    rank = narrow.shape[1]
    devices = lax.axis_size("expert")
    experts = devices // 2
    capacity = min(rows, max(2, (3 * rows * top_count + 2 * experts - 1) // (2 * experts)))
    near, far = stages()[0], stages()[1:]
    count = rows * devices // 2 // (len(near) + 1)
    slots = count // rows * capacity
    half = count + len(near) * slots
    offsets = [0]
    for masks in far:
        offsets = [first ^ mask for first in offsets for mask in (0, *masks)]
    lanes = -(-2 * experts // 128) * 128
    full = width + lanes

    def pieces_of(block):
        for masks in reversed(far[1:]):
            block = jnp.concatenate([block] + [send(block, mask) for mask in masks], axis=0)
        if far:
            return [block] + [send(block, mask) for mask in far[0]]
        return [block]

    (message,) = in_vmem(
        functools.partial(message_kernel, experts, width),
        [((rows, full + width), B16)],
        (tokens, cotangent, route_probs, expert_ids),
        outside=4,
        scratch=[
            pltpu.VMEM(route_probs.shape, F32),
            pltpu.VMEM(expert_ids.shape, jnp.int32),
            pltpu.SemaphoreType.DMA((4,)),
        ],
    )
    pieces = pieces_of(message)
    crossed = [send(message, mask) for mask in near[2:]]
    matmul = 2 * 2 * half * width * hidden_units
    weights = (gate_weight, up_weight, down_weight)
    gate_raw, up_raw, down_raw, gate_eff, up_eff, down_eff, narrow, wide = in_vmem(
        weights_kernel,
        [(weight.shape, B16) for weight in weights] * 2
        + [(narrow.shape, B16), ((3, rank, width), B16)],
        (*weights, narrow, wide_factors, send(wide_factors, 1)),
        3 * matmul,
        outside=5,
        scratch=[
            pltpu.VMEM(wide_factors.shape, B16),
            pltpu.SemaphoreType.DMA((2,)),
            pltpu.SemaphoreType.DMA((12,)),
        ],
    )
    folds, step = folds_of(rows, capacity, full + width)
    crossing = len(offsets) if crossed else 0
    held, cot_held, pick, *packed = in_vmem(
        functools.partial(pack_kernel, near, offsets, rows, capacity),
        [((count, full), B16), ((count, width), B16), ((len(near) * slots, count), F32)]
        + [((slots, full + width), B16)] * len(near[:2])
        + [((folds * capacity, step), B16)] * crossing,
        [wide] + crossed + pieces,
    )
    came = [send(block, mask) for block, mask in zip(packed, near[:2])]
    folded = packed[2 : 2 + crossing]
    came += folded[:1] + [send(block, mask) for block, mask in zip(folded[1:], offsets[1:])]
    order = list(range(len(came)))
    if len(came) > 5:
        order = [0, 4, 1, 5, *order[6:], 3, 2]
    mine_rows, cot_mine = in_vmem(
        functools.partial(stack_kernel, folds, len(near[:2]), order),
        [((half, full), B16), ((half, width), B16)],
        [held, cot_held, *[came[i] for i in order]],
    )
    token_rows = [mine_rows, send(mine_rows, 1)]
    cot_rows = [cot_mine, send(cot_mine, 1)]
    packed_type = [((slots, full), B16)] * len(near)

    wide_type, unit_type = ((2 * half, width), B16), ((2 * half, hidden_units), B16)
    x, probs, pre_gate, pre_up = in_vmem(
        functools.partial(pre_kernel, experts, width),
        [wide_type, ((2 * half, 128), F32)] + [((2 * half, hidden_units), F32)] * 2,
        (gate_eff, up_eff, *token_rows),
        2 * matmul,
    )
    y, hidden, grad_gate, grad_up, mine, give = in_vmem(
        functools.partial(mid_kernel, experts, width),
        [wide_type] + [unit_type] * 3 + [((half, full), B16)] * 2,
        (gate_eff, up_eff, down_eff, probs, pre_gate, pre_up, *cot_rows),
        3 * matmul,
    )
    other = send(give, 1)
    down_narrow, down_wide = in_vmem(
        down_grads_kernel,
        [((rank, hidden_units), F32), ((rank, width), F32)],
        (y, hidden, down_raw, narrow, wide),
        2 * matmul,
    )
    own, *parts = in_vmem(
        functools.partial(first_sum_kernel, experts, width),
        [((count, full), F32)] + packed_type,
        (mine, other, down_narrow),
    )
    grad_narrow, keep, give = in_vmem(
        feature_grads_kernel,
        [((3 * rank, hidden_units), F32), ((3 * rank, width // 2), F32), ((3 * rank, width // 2), B16)],
        (x, grad_gate, grad_up, gate_raw, up_raw, narrow, wide, parts[-2], down_narrow, down_wide),
        4 * matmul,
        results=(0,),
        scratch=[pltpu.VMEM((3 * rank, width), F32)],
    )
    ways = len(far[0]) if far else 0
    own, *parts = in_vmem(
        functools.partial(second_sum_kernel, ways),
        [((count // (ways + 1), full), F32)] + [((count // (ways + 1), full), B16)] * ways,
        (pick, own, *[send(part, mask) for part, mask in zip(parts[-1:] + parts, near[-1:] + near[:-1])], keep),
    )
    came = [send(part, mask) for part, mask in zip(parts, far[0] if far else ())]
    for masks in far[1:]:
        total = own
        for part in came:
            total = total + part.astype(F32)
        own, *parts = jnp.split(total, len(masks) + 1, axis=0)
        came = [send(part.astype(B16), mask) for part, mask in zip(parts, masks)]
    (grad_wide,) = in_vmem(
        wide_kernel, [((3 * rank, width // 2), F32)], (keep, send(give, 1)), results=(0,)
    )
    grad_tokens, grad_probs = in_vmem(
        functools.partial(last_kernel, experts, width),
        [((rows, width), B16), (expert_ids.shape, F32)],
        (expert_ids, own, *came[1:], *came[:1]),
        results=(0, 1),
    )
    return (
        grad_tokens,
        grad_probs,
        grad_narrow.reshape(3, rank, hidden_units),
        grad_wide.reshape(3, rank, width // 2),
    )


def solution(mesh):
    in_specs = (
        P(("groups", "expert"), None),
        P(("groups", "expert"), None),
        P(("groups", "expert"), None),
        P(("groups", "expert"), None),
        P(None, "expert"),
        P(None, "expert"),
        P("expert", None),
        P(None, None, "expert"),
        P(None, None, "expert"),
    )
    out_specs = (
        P(("groups", "expert"), None),
        P(("groups", "expert"), None),
        P("groups", None, "expert"),
        P("groups", None, "expert"),
    )
    return jax.shard_map(body, mesh=mesh, in_specs=in_specs, out_specs=out_specs, check_vma=False)
```

```python
import functools
import math

import jax
import jax.numpy as jnp
from jax import lax
from jax.experimental import pallas as pl
from jax.experimental.pallas import tpu as pltpu
from jax.sharding import PartitionSpec as P

NN = (((1,), (0,)), ((), ()))
NT = (((1,), (1,)), ((), ()))
TN = (((0,), (0,)), ((), ()))
F32, B16 = jnp.float32, jnp.bfloat16


def send(value, mask):
    pairs = [(source, source ^ mask) for source in range(lax.axis_size("expert"))]
    return lax.ppermute(value, "expert", pairs)


def stages():
    found, bit, top = [], 1, lax.axis_size("expert").bit_length() - 1
    while bit < top:
        if bit + 1 < top:
            found.append((2**bit, 2 ** (bit + 1), 3 * 2**bit))
        else:
            found.append((2**bit,))
        bit += 2
    return found


def dot32(left, right, dims=NN):
    return lax.dot_general(left, right, dims, preferred_element_type=F32)


def in_vmem(kernel, outs, args, flops=0, outside=0, results=(), scratch=()):
    moved = sum(a.size * a.dtype.itemsize for a in args)
    spaces = [pltpu.HBM] * outside + [pltpu.VMEM] * (len(args) - outside)
    return pl.pallas_call(
        kernel,
        out_shape=[
            (jax.ShapeDtypeStruct if i in results else pltpu.VMEM)(shape, dtype)
            for i, (shape, dtype) in enumerate(outs)
        ],
        in_specs=[pl.BlockSpec(memory_space=space) for space in spaces],
        out_specs=[pl.BlockSpec(memory_space=pltpu.VMEM)] * len(outs),
        scratch_shapes=list(scratch),
        compiler_params=pltpu.CompilerParams(vmem_limit_bytes=20 * 2**20),
        cost_estimate=pl.CostEstimate(flops=flops, bytes_accessed=moved, transcendentals=0),
    )(*[pltpu.with_memory_space_constraint(a, space) for a, space in zip(args, spaces)])


def stacked(refs):
    return jnp.concatenate([ref[...].astype(F32) for ref in refs], axis=0)


def chunks_of(width, step=512):
    return [pl.ds(at, step) for at in range(0, width, step)]


def copied(sources, targets, sems):
    copies = [pltpu.make_async_copy(*pair, sems.at[i]) for i, pair in enumerate(zip(sources, targets))]
    for copy in copies:
        copy.start()
    return copies


def message_kernel(experts, width, *refs):
    sources, out_ref, probs_ref, ids_ref, sems = refs[:4], refs[4], refs[5], refs[6], refs[7]
    tail = out_ref.shape[1] - width
    targets = (out_ref.at[:, :width], out_ref.at[:, tail:], probs_ref, ids_ref)
    copies = copied(sources, targets, sems)
    for copy in copies[2:]:
        copy.wait()
    ids, probs = ids_ref[...], probs_ref[...]
    high = probs.astype(B16).astype(F32)
    low = probs - high
    lane = lax.broadcasted_iota(jnp.int32, (ids.shape[0], tail - width), 1)
    extra = jnp.zeros(lane.shape, F32)
    for k in range(ids.shape[1]):
        one = slice(k, k + 1)
        extra = jnp.where(lane == ids[:, one], high[:, one], extra)
        extra = jnp.where(lane == ids[:, one] + experts, low[:, one], extra)
    out_ref[:, width:tail] = extra.astype(B16)
    for copy in copies[:2]:
        copy.wait()


def weights_into(which, sources, raws, outs, narrow_ref, wide_ref, sems):
    pieces = sems.shape[0] // len(sources)
    parts = []
    for i, (source, raw) in enumerate(zip(sources, raws)):
        step = source.shape[0] // pieces
        for j in range(pieces):
            rows = pl.ds(j * step, step)
            sem = sems.at[i * pieces + j]
            parts.append((i, rows, pltpu.make_async_copy(source.at[rows, :], raw.at[rows, :], sem)))
    ahead = 5
    for _, _, copy in parts[:ahead]:
        copy.start()
    for at, (i, rows, copy) in enumerate(parts):
        copy.wait()
        if at + ahead < len(parts):
            parts[at + ahead][2].start()
        raw, out, kind = raws[i], outs[i], which + i
        if kind < 2:
            for line in range(rows.start, rows.start + rows.size, 128):
                lines = pl.ds(line, 128)
                factor = 1.0 + dot32(wide_ref[kind, :, lines], narrow_ref[kind], TN)
                out[lines, :] = (raw[lines, :].astype(F32) * factor).astype(B16)
        else:
            for lanes in chunks_of(raw.shape[1]):
                factor = 1.0 + dot32(narrow_ref[kind, :, rows], wide_ref[kind, :, lanes], TN)
                out[rows, lanes] = (raw[rows, lanes].astype(F32) * factor).astype(B16)


def up_side_kernel(gate_ref, up_ref, narrow_hbm, mine_hbm, other_ref, *refs):
    raws, outs, (narrow_out, wide_out, mine_ref, small_sems, sems) = refs[:2], refs[2:4], refs[4:]
    for copy in copied((narrow_hbm, mine_hbm), (narrow_out, mine_ref), small_sems):
        copy.wait()
    half = mine_ref.shape[2]
    is_lower = lax.axis_index("expert") % 2 == 0

    @pl.when(is_lower)
    def _():
        wide_out[:, :, :half] = mine_ref[...]
        wide_out[:, :, half:] = other_ref[...]

    @pl.when(jnp.logical_not(is_lower))
    def _():
        wide_out[:, :, :half] = other_ref[...]
        wide_out[:, :, half:] = mine_ref[...]

    weights_into(0, (gate_ref, up_ref), raws, outs, narrow_out, wide_out, sems)


def down_side_kernel(down_ref, narrow_ref, wide_ref, after_ref, raw, out, sems):
    del after_ref
    weights_into(2, (down_ref,), (raw,), (out,), narrow_ref, wide_ref, sems)


def picks_of(extra, wanted_experts, rows, capacity):
    count, lanes = extra.shape
    slots = count // rows * capacity
    named = (extra > 0.0).astype(B16)
    kinds = -(-len(wanted_experts) // 8) * 8
    lane = lax.broadcasted_iota(jnp.int32, (kinds, lanes), 1)
    line = lax.broadcasted_iota(jnp.int32, (kinds, lanes), 0)
    wanted = jnp.zeros((kinds, lanes), F32)
    for i, expert in enumerate(wanted_experts):
        wanted = jnp.where((line == i) & (lane == expert), 1.0, wanted)
    chosen = dot32(wanted.astype(B16), named, NT)
    earlier = lax.broadcasted_iota(jnp.int32, (count, count), 0)
    later = lax.broadcasted_iota(jnp.int32, (count, count), 1)
    before = (earlier // rows == later // rows) & (earlier < later)
    slot = dot32(chosen.astype(B16), before.astype(F32).astype(B16))
    to = lax.broadcasted_iota(jnp.int32, (slots, count), 0)
    of = lax.broadcasted_iota(jnp.int32, (slots, count), 1)
    in_block = to // capacity == of // rows
    place = (to % capacity).astype(F32)
    picks = []
    for i in range(len(wanted_experts)):
        pick = in_block & (place == slot[i : i + 1, :]) & (chosen[i : i + 1, :] > 0.5)
        picks.append(jnp.where(pick, 1.0, 0.0))
    return picks


def folds_of(rows, capacity, lanes):
    folds = rows // math.gcd(rows, capacity)
    return folds, -(-lanes // (128 * folds)) * 128


def write_rows(outs, rows):
    first = 0
    for out in outs:
        out[...] = rows[first : first + out.shape[0]].astype(B16)
        first += out.shape[0]


def pack_kernel(masks, rows, capacity, lanes, waits, *refs):
    refs = refs[waits:]
    sent = len(masks[:3])
    blocks, pick_out, outs = refs[: -1 - sent], refs[-1 - sent], refs[-sent:]
    block = stacked(blocks)
    me = lax.axis_index("expert")
    picks = picks_of(block[:, lanes], [(me ^ mask) // 2 for mask in masks], rows, capacity)
    pick_out[...] = jnp.concatenate(picks, axis=0)
    picks = jnp.concatenate(picks[:sent], axis=0).astype(B16)
    write_rows(outs, dot32(picks, block.astype(B16)))


def cross_kernel(offsets, rows, capacity, lanes, after_ref, block_ref, *outs):
    del after_ref
    block = block_ref[...].astype(F32)
    width = block.shape[1]
    folds, step = folds_of(rows, capacity, width)
    extra = jnp.concatenate([block[:, lanes]] * folds, axis=0)
    if folds * step > width:
        block = jnp.concatenate([block, jnp.zeros((rows, folds * step - width), F32)], axis=1)
    pieces = [block[:, i * step : (i + 1) * step] for i in range(folds)]
    laid = jnp.concatenate(pieces, axis=0).astype(B16)
    me = lax.axis_index("expert")
    picks = picks_of(extra, [(me ^ offset) // 2 for offset in offsets], rows, capacity)
    write_rows(outs, dot32(jnp.concatenate(picks, axis=0).astype(B16), laid))


def unfolded(refs, folds):
    laid = stacked(refs).astype(B16)
    total, blocks = laid.shape[0], len(refs)
    capacity = total // (folds * blocks)
    to = lax.broadcasted_iota(jnp.int32, (total, total), 0)
    of = lax.broadcasted_iota(jnp.int32, (total, total), 1)
    same = to % capacity == of % capacity
    same &= to // (blocks * capacity) == of // capacity % folds
    same &= to // capacity % blocks == of // (folds * capacity)
    moved = dot32(jnp.where(same, 1.0, 0.0).astype(B16), laid)
    slots = blocks * capacity
    return jnp.concatenate([moved[i * slots : (i + 1) * slots] for i in range(folds)], axis=1)


def stack_kernel(folds, beside, order, after_ref, *refs):
    del after_ref
    came, (tokens_out, cot_out) = refs[:-2], refs[-2:]
    came = [came[order.index(i)] for i in range(len(order))]
    near, folded = came[:beside], came[beside:]
    pieces = [ref[...].astype(F32) for ref in near]
    if folded:
        pieces.append(unfolded(folded, folds))
    full, both = tokens_out.shape[1], tokens_out.shape[1] + cot_out.shape[1]
    for out, lanes in ((tokens_out, slice(0, full)), (cot_out, slice(full, both))):
        out[...] = jnp.concatenate([piece[:, lanes] for piece in pieces], axis=0).astype(B16)


def pre_kernel(experts, width, gate_ref, up_ref, *refs):
    pieces, (x_ref, prob_ref, pre_gate_ref, pre_up_ref) = refs[:-4], refs[-4:]
    for part in chunks_of(width):
        x_ref[:, part] = jnp.concatenate(
            [piece[:, part].astype(F32) for piece in pieces], axis=0
        ).astype(B16)
    extra = jnp.concatenate([piece[:, width:].astype(F32) for piece in pieces], axis=0)
    lane = lax.broadcasted_iota(jnp.int32, extra.shape, 1)
    own = (lane % experts == lax.axis_index("expert") // 2) & (lane < 2 * experts)
    probs = jnp.sum(jnp.where(own, extra, 0.0), axis=1, keepdims=True)
    prob_ref[...] = jnp.broadcast_to(probs, prob_ref.shape)
    pre_gate_ref[...] = dot32(x_ref[...], gate_ref[...])
    pre_up_ref[...] = dot32(x_ref[...], up_ref[...])


def mid_kernel(
    experts, width, gate_ref, up_ref, down_ref, prob_ref, pre_gate_ref, pre_up_ref, *refs
):
    pieces, outs = refs[:-6], refs[-6:]
    y_ref, hidden_ref, grad_gate_ref, grad_up_ref, mine_ref, give_ref = outs
    for part in chunks_of(width):
        y_ref[:, part] = jnp.concatenate(
            [piece[:, part].astype(F32) for piece in pieces], axis=0
        ).astype(B16)
    grad_full = dot32(y_ref[...], down_ref[...], NT)
    pre_gate, pre_up = pre_gate_ref[...], pre_up_ref[...]
    probs = prob_ref[:, :1]
    routed = probs > 0.0
    sigmoid_gate = jax.nn.sigmoid(pre_gate)
    activated = pre_gate * sigmoid_gate
    hidden = jnp.where(routed, activated * pre_up, 0.0)
    hidden_ref[...] = (hidden * probs).astype(B16)
    own_probs = jnp.sum(hidden * grad_full, axis=1, keepdims=True)
    grad_hidden = grad_full * probs
    grad_gate_ref[...] = jnp.where(
        routed, grad_hidden * pre_up * sigmoid_gate * (1.0 + pre_gate * (1.0 - sigmoid_gate)), 0.0
    ).astype(B16)
    grad_up_ref[...] = jnp.where(routed, grad_hidden * activated, 0.0).astype(B16)
    half = mine_ref.shape[0]
    for part in chunks_of(width):
        product = dot32(grad_gate_ref[...], gate_ref[part, :], NT)
        product = product + dot32(grad_up_ref[...], up_ref[part, :], NT)
        mine_ref[:, part] = product[:half].astype(B16)
        give_ref[:, part] = product[half:].astype(B16)
    lanes = mine_ref.shape[1] - width
    lane = lax.broadcasted_iota(jnp.int32, (2 * half, lanes), 1)
    expert = lax.axis_index("expert") // 2
    high = own_probs.astype(B16).astype(F32)
    extra = jnp.where(lane == expert, high, jnp.where(lane == expert + experts, own_probs - high, 0.0))
    mine_ref[:, width:] = extra[:half].astype(B16)
    give_ref[:, width:] = extra[half:].astype(B16)


def first_sum_kernel(experts, width, mine_ref, other_ref, after_ref, *outs):
    del after_ref
    total = mine_ref[...].astype(F32) + other_ref[...].astype(F32)
    rows, extra = total[:, :width], total[:, width:]
    lane = lax.broadcasted_iota(jnp.int32, extra.shape, 1)
    lost = jnp.where(lane < experts, extra - extra.astype(B16).astype(F32), 0.0)
    extra = extra + pltpu.roll(lost, experts, 1) - lost
    slots = outs[0].shape[0]
    for i, out in enumerate(outs):
        part = slice(i * slots, (i + 1) * slots)
        out[:, :width] = rows[part].astype(B16)
        out[:, width:] = extra[part].astype(B16)


def second_sum_kernel(ways, pick_ref, own_ref, *refs):
    came, own_out, outs = refs[: -2 - ways], refs[-1 - ways], refs[len(refs) - ways :]
    came = (own_ref,) + came[1:] + came[:1]
    total = dot32(pick_ref[...].astype(B16), stacked(came).astype(B16), TN)
    count = own_out.shape[0]
    own_out[...] = total[:count]
    for i, out in enumerate(outs):
        out[...] = total[(i + 1) * count : (i + 2) * count].astype(B16)


def down_grads_kernel(y_ref, hidden_ref, down_ref, narrow_ref, wide_ref, narrow_out, wide_out):
    width = y_ref.shape[1]
    narrow_out[...] = jnp.zeros_like(narrow_out)
    for part in chunks_of(width, width // 2):
        masked = dot32(hidden_ref[...], y_ref[:, part], TN) * down_ref[:, part].astype(F32)
        masked = masked.astype(B16)
        narrow_out[...] += dot32(wide_ref[2, :, part], masked, NT)
        wide_out[:, part] = dot32(narrow_ref[2], masked)


def feature_grads_kernel(
    x_ref, grad_gate_ref, grad_up_ref, gate_ref, up_ref, narrow_ref, wide_ref, after_ref,
    down_narrow_ref, down_wide_ref, narrow_out, keep_out, give_out, wide_all,
):
    del after_ref
    width, rank = x_ref.shape[1], narrow_ref.shape[1]
    lines = pl.ds(2 * rank, rank)
    narrow_out[lines, :] = down_narrow_ref[...]
    wide_all[lines, :] = down_wide_ref[...]
    for i, (grad, raw) in enumerate(((grad_gate_ref, gate_ref), (grad_up_ref, up_ref))):
        lines = pl.ds(i * rank, rank)
        narrow_out[lines, :] = jnp.zeros((rank, narrow_out.shape[1]), F32)
        for part in chunks_of(width, width // 2):
            masked = dot32(x_ref[:, part], grad[...], TN) * raw[part, :].astype(F32)
            masked = masked.astype(B16)
            narrow_out[lines, :] += dot32(wide_ref[i, :, part], masked)
            wide_all[lines, part] = dot32(narrow_ref[i], masked, NT)
    half = keep_out.shape[1]
    is_lower = lax.axis_index("expert") % 2 == 0

    @pl.when(is_lower)
    def _():
        keep_out[...] = wide_all[:, :half]
        give_out[...] = wide_all[:, half:].astype(B16)

    @pl.when(jnp.logical_not(is_lower))
    def _():
        keep_out[...] = wide_all[:, half:]
        give_out[...] = wide_all[:, :half].astype(B16)


def wide_kernel(keep_ref, given_ref, wide_out):
    wide_out[...] = keep_ref[...] + given_ref[...].astype(F32)


def last_kernel(experts, width, ids_ref, own_ref, *refs):
    came, (tokens_out, probs_out) = refs[:-2], refs[-2:]
    total = own_ref[...]
    for ref in came:
        total = total + ref[...].astype(F32)
    tokens_out[...] = total[:, :width].astype(B16)
    extra, ids = total[:, width:], ids_ref[...]
    lane = lax.broadcasted_iota(jnp.int32, extra.shape, 1)
    spot = lax.broadcasted_iota(jnp.int32, ids.shape, 1)
    probs = jnp.zeros(ids.shape, F32)
    for k in range(ids.shape[1]):
        wanted = ids[:, k : k + 1]
        found = jnp.where((lane == wanted) | (lane == wanted + experts), extra, 0.0)
        probs = jnp.where(spot == k, jnp.sum(found, axis=1, keepdims=True), probs)
    probs_out[...] = probs


def body(
    tokens,
    cotangent,
    route_probs,
    expert_ids,
    gate_weight,
    up_weight,
    down_weight,
    narrow,
    wide_factors,
):
    rows, width = tokens.shape
    hidden_units = gate_weight.shape[1]
    top_count = expert_ids.shape[1]
    rank = narrow.shape[1]
    devices = lax.axis_size("expert")
    experts = devices // 2
    capacity = min(rows, max(2, (3 * rows * top_count + 2 * experts - 1) // (2 * experts)))
    near, far = stages()[0], stages()[1:]
    count = rows * devices // 2 // (len(near) + 1)
    slots = count // rows * capacity
    half = (1 + len(near)) * slots
    offsets = [0]
    for masks in far:
        offsets = [first ^ mask for first in offsets for mask in (0, *masks)]
    lanes = -(-2 * experts // 128) * 128
    full = width + lanes

    def pieces_of(block):
        for masks in reversed(far[1:]):
            block = jnp.concatenate([block] + [send(block, mask) for mask in masks], axis=0)
        if far:
            return [block] + [send(block, mask) for mask in far[0]]
        return [block]

    (message,) = in_vmem(
        functools.partial(message_kernel, experts, width),
        [((rows, full + width), B16)],
        (tokens, cotangent, route_probs, expert_ids),
        outside=4,
        scratch=[
            pltpu.VMEM(route_probs.shape, F32),
            pltpu.VMEM(expert_ids.shape, jnp.int32),
            pltpu.SemaphoreType.DMA((4,)),
        ],
    )
    pieces = pieces_of(message)
    crossed = [send(message, mask) for mask in near[2:]]
    matmul = 2 * 2 * half * width * hidden_units
    gate_raw, up_raw, gate_eff, up_eff, narrow, wide = in_vmem(
        up_side_kernel,
        [(gate_weight.shape, B16)] * 4 + [(narrow.shape, B16), ((3, rank, width), B16)],
        (gate_weight, up_weight, narrow, wide_factors, send(wide_factors, 1)),
        2 * matmul,
        outside=4,
        scratch=[
            pltpu.VMEM(wide_factors.shape, B16),
            pltpu.SemaphoreType.DMA((2,)),
            pltpu.SemaphoreType.DMA((8,)),
        ],
    )
    folds, step = folds_of(rows, capacity, full + width)
    probs_at = slice(width, full)
    folded = []
    for block in crossed:
        folded += in_vmem(
            functools.partial(cross_kernel, offsets, rows, capacity, probs_at),
            [((folds * capacity, step), B16)] * len(offsets),
            [wide, block],
        )
    beside = near[:2]
    pick, *packed = in_vmem(
        functools.partial(
            pack_kernel, (0, *near), rows, capacity, probs_at, 1 + len(folded[:1])
        ),
        [(((1 + len(near)) * slots, count), F32)]
        + [((slots, full + width), B16)] * (1 + len(beside)),
        [wide] + folded[:1] + pieces,
    )
    came = packed[:1] + [send(block, mask) for block, mask in zip(packed[1:], beside)]
    came += folded[:1] + [send(block, mask) for block, mask in zip(folded[1:], offsets[1:])]
    order = list(range(len(came)))
    if len(came) > 6:
        order = [0, 1, 5, 2, 6, *order[7:], 4, 3]
    down_raw, down_eff = in_vmem(
        down_side_kernel,
        [(down_weight.shape, B16)] * 2,
        (down_weight, narrow, wide, pick),
        matmul,
        outside=1,
        scratch=[pltpu.SemaphoreType.DMA((4,))],
    )
    mine_rows, cot_mine = in_vmem(
        functools.partial(stack_kernel, folds, 1 + len(beside), order),
        [((half, full), B16), ((half, width), B16)],
        [down_eff] + [came[i] for i in order],
    )
    token_rows = [mine_rows, send(mine_rows, 1)]
    cot_rows = [cot_mine, send(cot_mine, 1)]
    packed_type = [((slots, full), B16)] * (1 + len(near))

    wide_type, unit_type = ((2 * half, width), B16), ((2 * half, hidden_units), B16)
    x, probs, pre_gate, pre_up = in_vmem(
        functools.partial(pre_kernel, experts, width),
        [wide_type, ((2 * half, 128), F32)] + [((2 * half, hidden_units), F32)] * 2,
        (gate_eff, up_eff, *token_rows),
        2 * matmul,
    )
    y, hidden, grad_gate, grad_up, mine, give = in_vmem(
        functools.partial(mid_kernel, experts, width),
        [wide_type] + [unit_type] * 3 + [((half, full), B16)] * 2,
        (gate_eff, up_eff, down_eff, probs, pre_gate, pre_up, *cot_rows),
        3 * matmul,
    )
    other = send(give, 1)
    down_narrow, down_wide = in_vmem(
        down_grads_kernel,
        [((rank, hidden_units), F32), ((rank, width), F32)],
        (y, hidden, down_raw, narrow, wide),
        2 * matmul,
    )
    own, *parts = in_vmem(
        functools.partial(first_sum_kernel, experts, width),
        packed_type,
        (mine, other, down_narrow),
    )
    grad_narrow, keep, give = in_vmem(
        feature_grads_kernel,
        [((3 * rank, hidden_units), F32), ((3 * rank, width // 2), F32), ((3 * rank, width // 2), B16)],
        (x, grad_gate, grad_up, gate_raw, up_raw, narrow, wide, parts[-2], down_narrow, down_wide),
        4 * matmul,
        results=(0,),
        scratch=[pltpu.VMEM((3 * rank, width), F32)],
    )
    ways = len(far[0]) if far else 0
    own, *parts = in_vmem(
        functools.partial(second_sum_kernel, ways),
        [((count // (ways + 1), full), F32)] + [((count // (ways + 1), full), B16)] * ways,
        (pick, own, *[send(part, mask) for part, mask in zip(parts[-1:] + parts, near[-1:] + near[:-1])], keep),
    )
    came = [send(part, mask) for part, mask in zip(parts, far[0] if far else ())]
    for masks in far[1:]:
        total = own
        for part in came:
            total = total + part.astype(F32)
        own, *parts = jnp.split(total, len(masks) + 1, axis=0)
        came = [send(part.astype(B16), mask) for part, mask in zip(parts, masks)]
    (grad_wide,) = in_vmem(
        wide_kernel, [((3 * rank, width // 2), F32)], (keep, send(give, 1)), results=(0,)
    )
    grad_tokens, grad_probs = in_vmem(
        functools.partial(last_kernel, experts, width),
        [((rows, width), B16), (expert_ids.shape, F32)],
        (expert_ids, own, *came[1:], *came[:1]),
        results=(0, 1),
    )
    return (
        grad_tokens,
        grad_probs,
        grad_narrow.reshape(3, rank, hidden_units),
        grad_wide.reshape(3, rank, width // 2),
    )


def solution(mesh):
    in_specs = (
        P(("groups", "expert"), None),
        P(("groups", "expert"), None),
        P(("groups", "expert"), None),
        P(("groups", "expert"), None),
        P(None, "expert"),
        P(None, "expert"),
        P("expert", None),
        P(None, None, "expert"),
        P(None, None, "expert"),
    )
    out_specs = (
        P(("groups", "expert"), None),
        P(("groups", "expert"), None),
        P("groups", None, "expert"),
        P("groups", None, "expert"),
    )
    return jax.shard_map(body, mesh=mesh, in_specs=in_specs, out_specs=out_specs, check_vma=False)
```

```python
import functools
import math

import jax
import jax.numpy as jnp
from jax import lax
from jax.experimental import pallas as pl
from jax.experimental.pallas import tpu as pltpu
from jax.sharding import PartitionSpec as P

NN = (((1,), (0,)), ((), ()))
NT = (((1,), (1,)), ((), ()))
TN = (((0,), (0,)), ((), ()))
F32, B16 = jnp.float32, jnp.bfloat16


def send(value, mask):
    pairs = [(source, source ^ mask) for source in range(lax.axis_size("expert"))]
    return lax.ppermute(value, "expert", pairs)


def stages():
    found, bit, top = [], 1, lax.axis_size("expert").bit_length() - 1
    while bit < top:
        if bit + 1 < top:
            found.append((2**bit, 2 ** (bit + 1), 3 * 2**bit))
        else:
            found.append((2**bit,))
        bit += 2
    return found


def dot32(left, right, dims=NN):
    return lax.dot_general(left, right, dims, preferred_element_type=F32)


def in_vmem(kernel, outs, args, flops=0, outside=0, results=(), scratch=()):
    moved = sum(a.size * a.dtype.itemsize for a in args)
    spaces = [pltpu.HBM] * outside + [pltpu.VMEM] * (len(args) - outside)
    return pl.pallas_call(
        kernel,
        out_shape=[
            (jax.ShapeDtypeStruct if i in results else pltpu.VMEM)(shape, dtype)
            for i, (shape, dtype) in enumerate(outs)
        ],
        in_specs=[pl.BlockSpec(memory_space=space) for space in spaces],
        out_specs=[pl.BlockSpec(memory_space=pltpu.VMEM)] * len(outs),
        scratch_shapes=list(scratch),
        compiler_params=pltpu.CompilerParams(vmem_limit_bytes=20 * 2**20),
        cost_estimate=pl.CostEstimate(flops=flops, bytes_accessed=moved, transcendentals=0),
    )(*[pltpu.with_memory_space_constraint(a, space) for a, space in zip(args, spaces)])


def stacked(refs):
    return jnp.concatenate([ref[...].astype(F32) for ref in refs], axis=0)


def chunks_of(width, step=512):
    return [pl.ds(at, step) for at in range(0, width, step)]


def copied(sources, targets, sems):
    copies = [pltpu.make_async_copy(*pair, sems.at[i]) for i, pair in enumerate(zip(sources, targets))]
    for copy in copies:
        copy.start()
    return copies


def message_kernel(experts, width, *refs):
    sources, out_ref, probs_ref, ids_ref, sems = refs[:4], refs[4], refs[5], refs[6], refs[7]
    tail = out_ref.shape[1] - width
    targets = (out_ref.at[:, :width], out_ref.at[:, tail:], probs_ref, ids_ref)
    copies = copied(sources, targets, sems)
    for copy in copies[2:]:
        copy.wait()
    ids, probs = ids_ref[...], probs_ref[...]
    high = probs.astype(B16).astype(F32)
    low = probs - high
    lane = lax.broadcasted_iota(jnp.int32, (ids.shape[0], tail - width), 1)
    extra = jnp.zeros(lane.shape, F32)
    for k in range(ids.shape[1]):
        one = slice(k, k + 1)
        extra = jnp.where(lane == ids[:, one], high[:, one], extra)
        extra = jnp.where(lane == ids[:, one] + experts, low[:, one], extra)
    out_ref[:, width:tail] = extra.astype(B16)
    for copy in copies[:2]:
        copy.wait()


def weights_into(which, sources, raws, outs, narrow_ref, wide_ref, sems):
    pieces = sems.shape[0] // len(sources)
    parts = []
    for i, (source, raw) in enumerate(zip(sources, raws)):
        step = source.shape[0] // pieces
        for j in range(pieces):
            rows = pl.ds(j * step, step)
            sem = sems.at[i * pieces + j]
            parts.append((i, rows, pltpu.make_async_copy(source.at[rows, :], raw.at[rows, :], sem)))
    ahead = 5
    for _, _, copy in parts[:ahead]:
        copy.start()
    for at, (i, rows, copy) in enumerate(parts):
        copy.wait()
        if at + ahead < len(parts):
            parts[at + ahead][2].start()
        raw, out, kind = raws[i], outs[i], which + i
        if kind < 2:
            for line in range(rows.start, rows.start + rows.size, 128):
                lines = pl.ds(line, 128)
                factor = 1.0 + dot32(wide_ref[kind, :, lines], narrow_ref[kind], TN)
                out[lines, :] = (raw[lines, :].astype(F32) * factor).astype(B16)
        else:
            for lanes in chunks_of(raw.shape[1]):
                factor = 1.0 + dot32(narrow_ref[kind, :, rows], wide_ref[kind, :, lanes], TN)
                out[rows, lanes] = (raw[rows, lanes].astype(F32) * factor).astype(B16)


def up_side_kernel(gate_ref, up_ref, narrow_hbm, mine_hbm, other_ref, *refs):
    raws, outs, (narrow_out, wide_out, mine_ref, small_sems, sems) = refs[:2], refs[2:4], refs[4:]
    for copy in copied((narrow_hbm, mine_hbm), (narrow_out, mine_ref), small_sems):
        copy.wait()
    half = mine_ref.shape[2]
    is_lower = lax.axis_index("expert") % 2 == 0

    @pl.when(is_lower)
    def _():
        wide_out[:, :, :half] = mine_ref[...]
        wide_out[:, :, half:] = other_ref[...]

    @pl.when(jnp.logical_not(is_lower))
    def _():
        wide_out[:, :, :half] = other_ref[...]
        wide_out[:, :, half:] = mine_ref[...]

    weights_into(0, (gate_ref, up_ref), raws, outs, narrow_out, wide_out, sems)


def down_side_kernel(down_ref, narrow_ref, wide_ref, after_ref, raw, out, sems):
    del after_ref
    weights_into(2, (down_ref,), (raw,), (out,), narrow_ref, wide_ref, sems)


def picks_of(extra, wanted_experts, rows, capacity):
    count, lanes = extra.shape
    slots = count // rows * capacity
    named = (extra > 0.0).astype(B16)
    kinds = -(-len(wanted_experts) // 8) * 8
    lane = lax.broadcasted_iota(jnp.int32, (kinds, lanes), 1)
    line = lax.broadcasted_iota(jnp.int32, (kinds, lanes), 0)
    wanted = jnp.zeros((kinds, lanes), F32)
    for i, expert in enumerate(wanted_experts):
        wanted = jnp.where((line == i) & (lane == expert), 1.0, wanted)
    chosen = dot32(wanted.astype(B16), named, NT)
    earlier = lax.broadcasted_iota(jnp.int32, (count, count), 0)
    later = lax.broadcasted_iota(jnp.int32, (count, count), 1)
    before = (earlier // rows == later // rows) & (earlier < later)
    slot = dot32(chosen.astype(B16), before.astype(F32).astype(B16))
    to = lax.broadcasted_iota(jnp.int32, (slots, count), 0)
    of = lax.broadcasted_iota(jnp.int32, (slots, count), 1)
    in_block = to // capacity == of // rows
    place = (to % capacity).astype(F32)
    picks = []
    for i in range(len(wanted_experts)):
        pick = in_block & (place == slot[i : i + 1, :]) & (chosen[i : i + 1, :] > 0.5)
        picks.append(jnp.where(pick, 1.0, 0.0))
    return picks


def folds_of(rows, capacity, lanes):
    folds = rows // math.gcd(rows, capacity)
    return folds, -(-lanes // (128 * folds)) * 128


def write_rows(outs, rows):
    first = 0
    for out in outs:
        out[...] = rows[first : first + out.shape[0]].astype(B16)
        first += out.shape[0]


def pack_kernel(masks, rows, capacity, lanes, waits, *refs):
    refs = refs[waits:]
    sent = len(masks[:3])
    blocks, pick_out, outs = refs[: -1 - sent], refs[-1 - sent], refs[-sent:]
    block = stacked(blocks)
    me = lax.axis_index("expert")
    picks = picks_of(block[:, lanes], [(me ^ mask) // 2 for mask in masks], rows, capacity)
    pick_out[...] = jnp.concatenate(picks, axis=0)
    picks = jnp.concatenate(picks[:sent], axis=0).astype(B16)
    write_rows(outs, dot32(picks, block.astype(B16)))


def cross_kernel(offsets, rows, capacity, lanes, after_ref, block_ref, *outs):
    del after_ref
    block = block_ref[...].astype(F32)
    width = block.shape[1]
    folds, step = folds_of(rows, capacity, width)
    extra = jnp.concatenate([block[:, lanes]] * folds, axis=0)
    laid = lane_pieces(block, folds, step).astype(B16)
    me = lax.axis_index("expert")
    picks = picks_of(extra, [(me ^ offset) // 2 for offset in offsets], rows, capacity)
    picks = jnp.concatenate(picks, axis=0)
    outs[0][...] = picks
    write_rows(outs[1:], dot32(picks.astype(B16), laid))


def lane_pieces(block, folds, step):
    rows, width = block.shape
    if folds * step > width:
        block = jnp.concatenate([block, jnp.zeros((rows, folds * step - width), F32)], axis=1)
    return jnp.concatenate([block[:, i * step : (i + 1) * step] for i in range(folds)], axis=0)


def piece_order(total, folds, blocks, back):
    capacity = total // (folds * blocks)
    to = lax.broadcasted_iota(jnp.int32, (total, total), 1 if back else 0)
    of = lax.broadcasted_iota(jnp.int32, (total, total), 0 if back else 1)
    same = to % capacity == of % capacity
    same &= to // (blocks * capacity) == of // capacity % folds
    same &= to // capacity % blocks == of // (folds * capacity)
    return jnp.where(same, 1.0, 0.0).astype(B16)


def beside_lanes(laid, folds):
    rows = laid.shape[0] // folds
    return jnp.concatenate([laid[i * rows : (i + 1) * rows] for i in range(folds)], axis=1)


def unfolded(refs, folds):
    laid = stacked(refs).astype(B16)
    return beside_lanes(dot32(piece_order(laid.shape[0], folds, len(refs), False), laid), folds)


def stack_kernel(folds, beside, order, after_ref, *refs):
    del after_ref
    came, (tokens_out, cot_out) = refs[:-2], refs[-2:]
    came = [came[order.index(i)] for i in range(len(order))]
    near, folded = came[:beside], came[beside:]
    pieces = [ref[...].astype(F32) for ref in near]
    if folded:
        pieces.append(unfolded(folded, folds))
    full, both = tokens_out.shape[1], tokens_out.shape[1] + cot_out.shape[1]
    for out, lanes in ((tokens_out, slice(0, full)), (cot_out, slice(full, both))):
        out[...] = jnp.concatenate([piece[:, lanes] for piece in pieces], axis=0).astype(B16)


def pre_kernel(experts, width, gate_ref, up_ref, *refs):
    pieces, (x_ref, prob_ref, pre_gate_ref, pre_up_ref) = refs[:-4], refs[-4:]
    for part in chunks_of(width):
        x_ref[:, part] = jnp.concatenate(
            [piece[:, part].astype(F32) for piece in pieces], axis=0
        ).astype(B16)
    extra = jnp.concatenate([piece[:, width:].astype(F32) for piece in pieces], axis=0)
    lane = lax.broadcasted_iota(jnp.int32, extra.shape, 1)
    own = (lane % experts == lax.axis_index("expert") // 2) & (lane < 2 * experts)
    probs = jnp.sum(jnp.where(own, extra, 0.0), axis=1, keepdims=True)
    prob_ref[...] = jnp.broadcast_to(probs, prob_ref.shape)
    pre_gate_ref[...] = dot32(x_ref[...], gate_ref[...])
    pre_up_ref[...] = dot32(x_ref[...], up_ref[...])


def mid_kernel(
    experts, width, gate_ref, up_ref, down_ref, prob_ref, pre_gate_ref, pre_up_ref, *refs
):
    pieces, outs = refs[:-6], refs[-6:]
    y_ref, hidden_ref, grad_gate_ref, grad_up_ref, mine_ref, give_ref = outs
    for part in chunks_of(width):
        y_ref[:, part] = jnp.concatenate(
            [piece[:, part].astype(F32) for piece in pieces], axis=0
        ).astype(B16)
    grad_full = dot32(y_ref[...], down_ref[...], NT)
    pre_gate, pre_up = pre_gate_ref[...], pre_up_ref[...]
    probs = prob_ref[:, :1]
    routed = probs > 0.0
    sigmoid_gate = jax.nn.sigmoid(pre_gate)
    activated = pre_gate * sigmoid_gate
    hidden = jnp.where(routed, activated * pre_up, 0.0)
    hidden_ref[...] = (hidden * probs).astype(B16)
    own_probs = jnp.sum(hidden * grad_full, axis=1, keepdims=True)
    grad_hidden = grad_full * probs
    grad_gate_ref[...] = jnp.where(
        routed, grad_hidden * pre_up * sigmoid_gate * (1.0 + pre_gate * (1.0 - sigmoid_gate)), 0.0
    ).astype(B16)
    grad_up_ref[...] = jnp.where(routed, grad_hidden * activated, 0.0).astype(B16)
    half = mine_ref.shape[0]
    for part in chunks_of(width):
        product = dot32(grad_gate_ref[...], gate_ref[part, :], NT)
        product = product + dot32(grad_up_ref[...], up_ref[part, :], NT)
        mine_ref[:, part] = product[:half].astype(B16)
        give_ref[:, part] = product[half:].astype(B16)
    lanes = mine_ref.shape[1] - width
    lane = lax.broadcasted_iota(jnp.int32, (2 * half, lanes), 1)
    expert = lax.axis_index("expert") // 2
    high = own_probs.astype(B16).astype(F32)
    extra = jnp.where(lane == expert, high, jnp.where(lane == expert + experts, own_probs - high, 0.0))
    mine_ref[:, width:] = extra[:half].astype(B16)
    give_ref[:, width:] = extra[half:].astype(B16)


def first_sum_kernel(experts, width, near, folds, mine_ref, other_ref, after_ref, *outs):
    del after_ref
    total = mine_ref[...].astype(F32) + other_ref[...].astype(F32)
    extra = total[:, width:]
    lane = lax.broadcasted_iota(jnp.int32, extra.shape, 1)
    lost = jnp.where(lane < experts, extra - extra.astype(B16).astype(F32), 0.0)
    extra = extra + pltpu.roll(lost, experts, 1) - lost
    slots = outs[0].shape[0]
    for i, out in enumerate(outs[:near]):
        part = slice(i * slots, (i + 1) * slots)
        out[:, :width] = total[part, :width].astype(B16)
        out[:, width:] = extra[part].astype(B16)
    if outs[near:]:
        rest = jnp.concatenate([total[near * slots :, :width], extra[near * slots :]], axis=1)
        laid = lane_pieces(rest, folds, outs[near].shape[1]).astype(B16)
        write_rows(outs[near:], dot32(piece_order(laid.shape[0], folds, len(outs[near:]), True), laid))


def second_sum_kernel(near, folds, crossing, ways, give_ref, pick_ref, *refs):
    refs[-1][...] = give_ref[...]
    refs = refs[:-1]
    came, refs = refs[:near], refs[near:]
    total = dot32(pick_ref[...].astype(B16), stacked(came).astype(B16), TN)
    if crossing:
        cross_pick, came, refs = refs[0], refs[1 : 1 + crossing], refs[1 + crossing :]
        block = dot32(cross_pick[...].astype(B16), stacked(came).astype(B16), TN)
        refs[-1][...] = beside_lanes(block, folds)[:, : total.shape[1]].astype(B16)
    own_out, outs = refs[0], refs[1 : 1 + ways]
    count = own_out.shape[0]
    own_out[...] = total[:count]
    for i, out in enumerate(outs):
        out[...] = total[(i + 1) * count : (i + 2) * count].astype(B16)


def down_grads_kernel(y_ref, hidden_ref, down_ref, narrow_ref, masked_out, wide_out):
    width = y_ref.shape[1]
    for part in chunks_of(width, width // 2):
        masked = dot32(hidden_ref[...], y_ref[:, part], TN) * down_ref[:, part].astype(F32)
        masked = masked.astype(B16)
        masked_out[:, part] = masked
        wide_out[:, part] = dot32(narrow_ref[2], masked)


def feature_grads_kernel(
    x_ref, grad_gate_ref, grad_up_ref, gate_ref, up_ref, narrow_ref, after_ref, down_wide_ref,
    masked_gate, masked_up, keep_out, give_out, wide_all,
):
    del after_ref
    width, rank = x_ref.shape[1], narrow_ref.shape[1]
    wide_all[pl.ds(2 * rank, rank), :] = down_wide_ref[...]
    sides = ((grad_gate_ref, gate_ref, masked_gate), (grad_up_ref, up_ref, masked_up))
    for i, (grad, raw, out) in enumerate(sides):
        for part in chunks_of(width, width // 2):
            masked = dot32(x_ref[:, part], grad[...], TN) * raw[part, :].astype(F32)
            masked = masked.astype(B16)
            out[part, :] = masked
            wide_all[pl.ds(i * rank, rank), part] = dot32(narrow_ref[i], masked, NT)
    half = keep_out.shape[1]
    is_lower = lax.axis_index("expert") % 2 == 0

    @pl.when(is_lower)
    def _():
        keep_out[...] = wide_all[:, :half]
        give_out[...] = wide_all[:, half:].astype(B16)

    @pl.when(jnp.logical_not(is_lower))
    def _():
        keep_out[...] = wide_all[:, half:]
        give_out[...] = wide_all[:, :half].astype(B16)


def narrow_kernel(masked_gate, masked_up, masked_down, wide_ref, after_ref, narrow_out):
    del after_ref
    rank = wide_ref.shape[1]
    for i, (masked, dims) in enumerate(((masked_gate, NN), (masked_up, NN), (masked_down, NT))):
        narrow_out[pl.ds(i * rank, rank), :] = dot32(wide_ref[i], masked[...], dims)


def last_kernel(experts, width, ids_ref, keep_ref, own_ref, *refs):
    came, given_ref, (tokens_out, probs_out, wide_out) = refs[:-4], refs[-4], refs[-3:]
    wide_out[...] = keep_ref[...] + given_ref[...].astype(F32)
    total = own_ref[...]
    for ref in came:
        total = total + ref[...].astype(F32)
    tokens_out[...] = total[:, :width].astype(B16)
    extra, ids = total[:, width:], ids_ref[...]
    lane = lax.broadcasted_iota(jnp.int32, extra.shape, 1)
    spot = lax.broadcasted_iota(jnp.int32, ids.shape, 1)
    probs = jnp.zeros(ids.shape, F32)
    for k in range(ids.shape[1]):
        wanted = ids[:, k : k + 1]
        found = jnp.where((lane == wanted) | (lane == wanted + experts), extra, 0.0)
        probs = jnp.where(spot == k, jnp.sum(found, axis=1, keepdims=True), probs)
    probs_out[...] = probs


def body(
    tokens,
    cotangent,
    route_probs,
    expert_ids,
    gate_weight,
    up_weight,
    down_weight,
    narrow,
    wide_factors,
):
    rows, width = tokens.shape
    hidden_units = gate_weight.shape[1]
    top_count = expert_ids.shape[1]
    rank = narrow.shape[1]
    devices = lax.axis_size("expert")
    experts = devices // 2
    capacity = min(rows, max(2, (3 * rows * top_count + 2 * experts - 1) // (2 * experts)))
    near, far = stages()[0], stages()[1:]
    count = rows * devices // 2 // (len(near) + 1)
    slots = count // rows * capacity
    half = (1 + len(near)) * slots
    offsets = [0]
    for masks in far:
        offsets = [first ^ mask for first in offsets for mask in (0, *masks)]
    lanes = -(-2 * experts // 128) * 128
    full = width + lanes

    def pieces_of(block):
        for masks in reversed(far[1:]):
            block = jnp.concatenate([block] + [send(block, mask) for mask in masks], axis=0)
        if far:
            return [block] + [send(block, mask) for mask in far[0]]
        return [block]

    (message,) = in_vmem(
        functools.partial(message_kernel, experts, width),
        [((rows, full + width), B16)],
        (tokens, cotangent, route_probs, expert_ids),
        outside=4,
        scratch=[
            pltpu.VMEM(route_probs.shape, F32),
            pltpu.VMEM(expert_ids.shape, jnp.int32),
            pltpu.SemaphoreType.DMA((4,)),
        ],
    )
    pieces = pieces_of(message)
    crossed = [send(message, mask) for mask in near[2:]]
    matmul = 2 * 2 * half * width * hidden_units
    gate_raw, up_raw, gate_eff, up_eff, narrow, wide = in_vmem(
        up_side_kernel,
        [(gate_weight.shape, B16)] * 4 + [(narrow.shape, B16), ((3, rank, width), B16)],
        (gate_weight, up_weight, narrow, wide_factors, send(wide_factors, 1)),
        2 * matmul,
        outside=4,
        scratch=[
            pltpu.VMEM(wide_factors.shape, B16),
            pltpu.SemaphoreType.DMA((2,)),
            pltpu.SemaphoreType.DMA((8,)),
        ],
    )
    folds, step = folds_of(rows, capacity, full + width)
    probs_at = slice(width, full)
    cross_pick, folded = [], []
    for block in crossed:
        picked, *folded = in_vmem(
            functools.partial(cross_kernel, offsets, rows, capacity, probs_at),
            [((len(offsets) * folds * capacity, folds * rows), F32)]
            + [((folds * capacity, step), B16)] * len(offsets),
            [wide, block],
        )
        cross_pick = [picked]
    beside = near[:2]
    pick, *packed = in_vmem(
        functools.partial(
            pack_kernel, (0, *beside), rows, capacity, probs_at, 1 + len(folded[:1])
        ),
        [(((1 + len(beside)) * slots, count), F32)]
        + [((slots, full + width), B16)] * (1 + len(beside)),
        [wide] + folded[:1] + pieces,
    )
    came = packed[:1] + [send(block, mask) for block, mask in zip(packed[1:], beside)]
    came += folded[:1] + [send(block, mask) for block, mask in zip(folded[1:], offsets[1:])]
    order = list(range(len(came)))
    if len(came) > 6:
        order = [0, 1, 5, 2, 6, *order[7:], 4, 3]
    down_raw, down_eff = in_vmem(
        down_side_kernel,
        [(down_weight.shape, B16)] * 2,
        (down_weight, narrow, wide, pick),
        matmul,
        outside=1,
        scratch=[pltpu.SemaphoreType.DMA((4,))],
    )
    mine_rows, cot_mine = in_vmem(
        functools.partial(stack_kernel, folds, 1 + len(beside), order),
        [((half, full), B16), ((half, width), B16)],
        [down_eff] + [came[i] for i in order],
    )
    token_rows = [mine_rows, send(mine_rows, 1)]
    cot_rows = [cot_mine, send(cot_mine, 1)]

    wide_type, unit_type = ((2 * half, width), B16), ((2 * half, hidden_units), B16)
    x, probs, pre_gate, pre_up = in_vmem(
        functools.partial(pre_kernel, experts, width),
        [wide_type, ((2 * half, 128), F32)] + [((2 * half, hidden_units), F32)] * 2,
        (gate_eff, up_eff, *token_rows),
        2 * matmul,
    )
    y, hidden, grad_gate, grad_up, mine, give = in_vmem(
        functools.partial(mid_kernel, experts, width),
        [wide_type] + [unit_type] * 3 + [((half, full), B16)] * 2,
        (gate_eff, up_eff, down_eff, probs, pre_gate, pre_up, *cot_rows),
        3 * matmul,
    )
    other = send(give, 1)
    masked_down, down_wide = in_vmem(
        down_grads_kernel,
        [(down_weight.shape, B16), ((rank, width), F32)],
        (y, hidden, down_raw, narrow),
        2 * matmul,
    )
    near_count, cross_count = 1 + len(beside), len(folded)
    fold_step = folds_of(rows, capacity, full)[1]
    sums = in_vmem(
        functools.partial(first_sum_kernel, experts, width, near_count, folds),
        [((slots, full), B16)] * near_count
        + [((folds * capacity, fold_step), B16)] * cross_count,
        (mine, other, down_wide),
    )
    masked_gate, masked_up, keep, give = in_vmem(
        feature_grads_kernel,
        [(gate_weight.shape, B16)] * 2
        + [((3 * rank, width // 2), F32), ((3 * rank, width // 2), B16)],
        (x, grad_gate, grad_up, gate_raw, up_raw, narrow, sums[0], down_wide),
        4 * matmul,
        scratch=[pltpu.VMEM((3 * rank, width), F32)],
    )
    came = [sums[0]] + [send(part, mask) for part, mask in zip(sums[1:near_count], beside)]
    crossing = sums[near_count:]
    came += [*cross_pick, *crossing[:1]]
    came += [send(part, mask) for part, mask in zip(crossing[1:], offsets[1:])]
    ways = len(far[0]) if far else 0
    own, *parts = in_vmem(
        functools.partial(second_sum_kernel, near_count, folds, cross_count, ways),
        [((count // (ways + 1), full), F32)]
        + [((count // (ways + 1), full), B16)] * ways
        + [((rows, full), B16)] * len(crossed)
        + [(give.shape, B16)],
        (give, pick, *came),
    )
    *parts, give = parts
    (grad_narrow,) = in_vmem(
        narrow_kernel,
        [((3 * rank, hidden_units), F32)],
        (masked_gate, masked_up, masked_down, wide, parts[-1]),
        2 * matmul,
        results=(0,),
    )
    from_cross = [send(part, mask) for part, mask in zip(parts[ways:], near[2:])]
    came = [send(part, mask) for part, mask in zip(parts[:ways], far[0] if far else ())]
    for masks in far[1:]:
        total = own
        for part in came:
            total = total + part.astype(F32)
        own, *parts = jnp.split(total, len(masks) + 1, axis=0)
        came = [send(part.astype(B16), mask) for part, mask in zip(parts, masks)]
    came = came[1:] + from_cross + came[:1]
    grad_tokens, grad_probs, grad_wide = in_vmem(
        functools.partial(last_kernel, experts, width),
        [((rows, width), B16), (expert_ids.shape, F32), ((3 * rank, width // 2), F32)],
        (expert_ids, keep, own, *came, send(give, 1)),
        results=(0, 1, 2),
    )
    return (
        grad_tokens,
        grad_probs,
        grad_narrow.reshape(3, rank, hidden_units),
        grad_wide.reshape(3, rank, width // 2),
    )


def solution(mesh):
    in_specs = (
        P(("groups", "expert"), None),
        P(("groups", "expert"), None),
        P(("groups", "expert"), None),
        P(("groups", "expert"), None),
        P(None, "expert"),
        P(None, "expert"),
        P("expert", None),
        P(None, None, "expert"),
        P(None, None, "expert"),
    )
    out_specs = (
        P(("groups", "expert"), None),
        P(("groups", "expert"), None),
        P("groups", None, "expert"),
        P("groups", None, "expert"),
    )
    return jax.shard_map(body, mesh=mesh, in_specs=in_specs, out_specs=out_specs, check_vma=False)
```

```python
import functools
import math

import jax
import jax.numpy as jnp
from jax import lax
from jax.experimental import pallas as pl
from jax.experimental.pallas import tpu as pltpu
from jax.sharding import PartitionSpec as P

NN = (((1,), (0,)), ((), ()))
NT = (((1,), (1,)), ((), ()))
TN = (((0,), (0,)), ((), ()))
F32, B16 = jnp.float32, jnp.bfloat16


def send(value, mask):
    pairs = [(source, source ^ mask) for source in range(lax.axis_size("expert"))]
    return lax.ppermute(value, "expert", pairs)


def stages():
    found, bit, top = [], 1, lax.axis_size("expert").bit_length() - 1
    while bit < top:
        if bit + 1 < top:
            found.append((2**bit, 2 ** (bit + 1), 3 * 2**bit))
        else:
            found.append((2**bit,))
        bit += 2
    return found


def dot32(left, right, dims=NN):
    return lax.dot_general(left, right, dims, preferred_element_type=F32)


def in_vmem(kernel, outs, args, flops=0, outside=0, results=(), scratch=()):
    moved = sum(a.size * a.dtype.itemsize for a in args)
    spaces = [pltpu.HBM] * outside + [pltpu.VMEM] * (len(args) - outside)
    return pl.pallas_call(
        kernel,
        out_shape=[
            (jax.ShapeDtypeStruct if i in results else pltpu.VMEM)(shape, dtype)
            for i, (shape, dtype) in enumerate(outs)
        ],
        in_specs=[pl.BlockSpec(memory_space=space) for space in spaces],
        out_specs=[pl.BlockSpec(memory_space=pltpu.VMEM)] * len(outs),
        scratch_shapes=list(scratch),
        compiler_params=pltpu.CompilerParams(vmem_limit_bytes=8 * 2**20),
        cost_estimate=pl.CostEstimate(flops=flops, bytes_accessed=moved, transcendentals=0),
    )(*[pltpu.with_memory_space_constraint(a, space) for a, space in zip(args, spaces)])


def stacked(refs):
    return jnp.concatenate([ref[...].astype(F32) for ref in refs], axis=0)


def chunks_of(width, step=512):
    return [pl.ds(at, step) for at in range(0, width, step)]


def copied(sources, targets, sems):
    copies = [pltpu.make_async_copy(*pair, sems.at[i]) for i, pair in enumerate(zip(sources, targets))]
    for copy in copies:
        copy.start()
    return copies


def message_kernel(experts, width, *refs):
    sources, out_ref, probs_ref, ids_ref, sems = refs[:4], refs[4], refs[5], refs[6], refs[7]
    tail = out_ref.shape[1] - width
    targets = (out_ref.at[:, :width], out_ref.at[:, tail:], probs_ref, ids_ref)
    copies = copied(sources, targets, sems)
    for copy in copies[2:]:
        copy.wait()
    ids, probs = ids_ref[...], probs_ref[...]
    high = probs.astype(B16).astype(F32)
    low = probs - high
    lane = lax.broadcasted_iota(jnp.int32, (ids.shape[0], tail - width), 1)
    extra = jnp.zeros(lane.shape, F32)
    for k in range(ids.shape[1]):
        one = slice(k, k + 1)
        extra = jnp.where(lane == ids[:, one], high[:, one], extra)
        extra = jnp.where(lane == ids[:, one] + experts, low[:, one], extra)
    out_ref[:, width:tail] = extra.astype(B16)
    for copy in copies[:2]:
        copy.wait()


def started(sources, raws, sems, ahead):
    pieces, parts = sems.shape[0] // len(sources), []
    for i, (source, raw) in enumerate(zip(sources, raws)):
        step = source.shape[0] // pieces
        for j in range(pieces):
            rows = pl.ds(j * step, step)
            sem = sems.at[i * pieces + j]
            parts.append((i, rows, pltpu.make_async_copy(source.at[rows, :], raw.at[rows, :], sem)))
    for _, _, copy in parts[:ahead]:
        copy.start()
    return parts


def up_side_kernel(gate_ref, up_ref, narrow_hbm, mine_hbm, other_ref, *refs):
    raws, outs, (narrow_out, wide_out, mine_ref, small_sems, sems) = refs[:2], refs[2:4], refs[4:]
    for copy in copied((narrow_hbm, mine_hbm), (narrow_out, mine_ref), small_sems):
        copy.wait()
    half = mine_ref.shape[2]
    is_lower = lax.axis_index("expert") % 2 == 0

    @pl.when(is_lower)
    def _():
        wide_out[:, :, :half] = mine_ref[...]
        wide_out[:, :, half:] = other_ref[...]

    @pl.when(jnp.logical_not(is_lower))
    def _():
        wide_out[:, :, :half] = other_ref[...]
        wide_out[:, :, half:] = mine_ref[...]

    ahead = 5
    parts = started((gate_ref, up_ref), raws, sems, ahead)
    for at, (i, rows, copy) in enumerate(parts):
        copy.wait()
        if at + ahead < len(parts):
            parts[at + ahead][2].start()
        for line in range(rows.start, rows.start + rows.size, 128):
            lines = pl.ds(line, 128)
            factor = 1.0 + dot32(wide_out[i, :, lines], narrow_out[i], TN)
            outs[i][lines, :] = (raws[i][lines, :].astype(F32) * factor).astype(B16)


def down_side_kernel(
    down_ref, narrow_ref, wide_ref, gate_ref, up_ref, after_ref, raw, down_out, gate_out, up_out, sems
):
    del after_ref
    parts = started((down_ref,), (raw,), sems, sems.shape[0])
    for source, out in ((gate_ref, gate_out), (up_ref, up_out)):
        for lines in chunks_of(source.shape[0]):
            out[:, lines] = source[lines, :].T
    for _, rows, copy in parts:
        copy.wait()
        for lanes in chunks_of(raw.shape[1]):
            factor = 1.0 + dot32(narrow_ref[2, :, rows], wide_ref[2, :, lanes], TN)
            down_out[lanes, rows] = (raw[rows, lanes].astype(F32) * factor).astype(B16).T


def picks_of(extra, wanted_experts, rows, capacity):
    count, lanes = extra.shape
    slots = count // rows * capacity
    named = (extra > 0.0).astype(B16)
    kinds = -(-len(wanted_experts) // 8) * 8
    lane = lax.broadcasted_iota(jnp.int32, (kinds, lanes), 1)
    line = lax.broadcasted_iota(jnp.int32, (kinds, lanes), 0)
    wanted = jnp.zeros((kinds, lanes), F32)
    for i, expert in enumerate(wanted_experts):
        wanted = jnp.where((line == i) & (lane == expert), 1.0, wanted)
    chosen = dot32(wanted.astype(B16), named, NT)
    earlier = lax.broadcasted_iota(jnp.int32, (count, count), 0)
    later = lax.broadcasted_iota(jnp.int32, (count, count), 1)
    before = (earlier // rows == later // rows) & (earlier < later)
    slot = dot32(chosen.astype(B16), before.astype(F32).astype(B16))
    to = lax.broadcasted_iota(jnp.int32, (slots, count), 0)
    of = lax.broadcasted_iota(jnp.int32, (slots, count), 1)
    in_block = to // capacity == of // rows
    place = (to % capacity).astype(F32)
    picks = []
    for i in range(len(wanted_experts)):
        pick = in_block & (place == slot[i : i + 1, :]) & (chosen[i : i + 1, :] > 0.5)
        picks.append(jnp.where(pick, 1.0, 0.0))
    return picks


def folds_of(rows, capacity, lanes):
    folds = rows // math.gcd(rows, capacity)
    return folds, -(-lanes // (128 * folds)) * 128


def write_rows(outs, rows):
    first = 0
    for out in outs:
        out[...] = rows[first : first + out.shape[0]].astype(B16)
        first += out.shape[0]


def pack_kernel(masks, offsets, rows, capacity, lanes, blocks, after_ref, *refs):
    del after_ref
    came, refs = refs[:blocks], refs[blocks:]
    crossing = refs[0].shape[0] == rows and len(refs) > 1 + len(masks)
    crossed, (pick_out, *outs) = (refs[:1], refs[1:]) if crossing else ((), refs)
    block = stacked(came[::-1])
    me = lax.axis_index("expert")
    picks = picks_of(block[:, lanes], [(me ^ mask) // 2 for mask in masks], rows, capacity)
    picks = jnp.concatenate(picks, axis=0)
    pick_out[...] = picks
    write_rows(outs[: len(masks)], dot32(picks.astype(B16), block.astype(B16)))
    for ref in crossed:
        block = ref[...].astype(F32)
        folds, step = folds_of(rows, capacity, block.shape[1])
        extra = jnp.concatenate([block[:, lanes]] * folds, axis=0)
        picks = picks_of(extra, [(me ^ offset) // 2 for offset in offsets], rows, capacity)
        picks = jnp.concatenate(picks, axis=0)
        outs[len(masks)][...] = picks
        laid = lane_pieces(block, folds, step).astype(B16)
        write_rows(outs[len(masks) + 1 :], dot32(picks.astype(B16), laid))


def lane_pieces(block, folds, step):
    rows, width = block.shape
    if folds * step > width:
        block = jnp.concatenate([block, jnp.zeros((rows, folds * step - width), F32)], axis=1)
    return jnp.concatenate([block[:, i * step : (i + 1) * step] for i in range(folds)], axis=0)


def piece_order(total, folds, blocks, back):
    capacity = total // (folds * blocks)
    to = lax.broadcasted_iota(jnp.int32, (total, total), 1 if back else 0)
    of = lax.broadcasted_iota(jnp.int32, (total, total), 0 if back else 1)
    same = to % capacity == of % capacity
    same &= to // (blocks * capacity) == of // capacity % folds
    same &= to // capacity % blocks == of // (folds * capacity)
    return jnp.where(same, 1.0, 0.0).astype(B16)


def beside_lanes(laid, folds):
    rows = laid.shape[0] // folds
    return jnp.concatenate([laid[i * rows : (i + 1) * rows] for i in range(folds)], axis=1)


def unfolded(refs, folds):
    laid = stacked(refs).astype(B16)
    return beside_lanes(dot32(piece_order(laid.shape[0], folds, len(refs), False), laid), folds)


def stack_kernel(folds, beside, order, after_ref, *refs):
    del after_ref
    came, (tokens_out, cot_out) = refs[:-2], refs[-2:]
    came = [came[order.index(i)] for i in range(len(order))]
    near, folded = came[:beside], came[beside:]
    pieces = [ref[...].astype(F32) for ref in near]
    if folded:
        pieces.append(unfolded(folded, folds))
    full, both = tokens_out.shape[1], tokens_out.shape[1] + cot_out.shape[1]
    for out, lanes in ((tokens_out, slice(0, full)), (cot_out, slice(full, both))):
        out[...] = jnp.concatenate([piece[:, lanes] for piece in pieces], axis=0).astype(B16)


def pre_kernel(experts, width, gate_ref, up_ref, *refs):
    pieces, (x_ref, prob_ref, pre_gate_ref, pre_up_ref) = refs[:-4], refs[-4:]
    for part in chunks_of(width):
        x_ref[:, part] = jnp.concatenate(
            [piece[:, part].astype(F32) for piece in pieces], axis=0
        ).astype(B16)
    extra = jnp.concatenate([piece[:, width:].astype(F32) for piece in pieces], axis=0)
    lane = lax.broadcasted_iota(jnp.int32, extra.shape, 1)
    own = (lane % experts == lax.axis_index("expert") // 2) & (lane < 2 * experts)
    probs = jnp.sum(jnp.where(own, extra, 0.0), axis=1, keepdims=True)
    prob_ref[...] = jnp.broadcast_to(probs, prob_ref.shape)
    pre_gate_ref[...] = dot32(x_ref[...], gate_ref[...])
    pre_up_ref[...] = dot32(x_ref[...], up_ref[...])


def mid_kernel(
    experts, width, gate_ref, up_ref, down_ref, prob_ref, pre_gate_ref, pre_up_ref, *refs
):
    pieces, outs = refs[:-6], refs[-6:]
    y_ref, hidden_ref, grad_gate_ref, grad_up_ref, mine_ref, give_ref = outs
    for part in chunks_of(width):
        y_ref[:, part] = jnp.concatenate(
            [piece[:, part].astype(F32) for piece in pieces], axis=0
        ).astype(B16)
    grad_full = dot32(y_ref[...], down_ref[...])
    pre_gate, pre_up = pre_gate_ref[...], pre_up_ref[...]
    probs = prob_ref[:, :1]
    routed = probs > 0.0
    sigmoid_gate = jax.nn.sigmoid(pre_gate)
    activated = pre_gate * sigmoid_gate
    hidden = jnp.where(routed, activated * pre_up, 0.0)
    hidden_ref[...] = (hidden * probs).astype(B16)
    own_probs = jnp.sum(hidden * grad_full, axis=1, keepdims=True)
    grad_hidden = grad_full * probs
    grad_gate_ref[...] = jnp.where(
        routed, grad_hidden * pre_up * sigmoid_gate * (1.0 + pre_gate * (1.0 - sigmoid_gate)), 0.0
    ).astype(B16)
    grad_up_ref[...] = jnp.where(routed, grad_hidden * activated, 0.0).astype(B16)
    half = mine_ref.shape[0]
    for part in chunks_of(width):
        product = dot32(grad_gate_ref[...], gate_ref[:, part])
        product = product + dot32(grad_up_ref[...], up_ref[:, part])
        mine_ref[:, part] = product[:half].astype(B16)
        give_ref[:, part] = product[half:].astype(B16)
    lanes = mine_ref.shape[1] - width
    lane = lax.broadcasted_iota(jnp.int32, (2 * half, lanes), 1)
    expert = lax.axis_index("expert") // 2
    high = own_probs.astype(B16).astype(F32)
    extra = jnp.where(lane == expert, high, jnp.where(lane == expert + experts, own_probs - high, 0.0))
    mine_ref[:, width:] = extra[:half].astype(B16)
    give_ref[:, width:] = extra[half:].astype(B16)


def first_sum_kernel(experts, width, near, folds, mine_ref, other_ref, after_ref, *outs):
    del after_ref
    total = mine_ref[...].astype(F32) + other_ref[...].astype(F32)
    extra = total[:, width:]
    lane = lax.broadcasted_iota(jnp.int32, extra.shape, 1)
    lost = jnp.where(lane < experts, extra - extra.astype(B16).astype(F32), 0.0)
    extra = extra + pltpu.roll(lost, experts, 1) - lost
    slots = outs[0].shape[0]
    for i, out in enumerate(outs[:near]):
        part = slice(i * slots, (i + 1) * slots)
        out[:, :width] = total[part, :width].astype(B16)
        out[:, width:] = extra[part].astype(B16)
    if outs[near:]:
        rest = jnp.concatenate([total[near * slots :, :width], extra[near * slots :]], axis=1)
        laid = lane_pieces(rest, folds, outs[near].shape[1]).astype(B16)
        write_rows(outs[near:], dot32(piece_order(laid.shape[0], folds, len(outs[near:]), True), laid))


def second_sum_kernel(near, folds, crossing, ways, order, give_ref, pick_ref, *refs):
    refs[-1][...] = give_ref[...]
    refs = refs[:-1]
    came = [refs[order.index(i)] for i in range(len(order))]
    came, refs = came[:near], (*came[near:], *refs[len(order) :])
    total = dot32(pick_ref[...].astype(B16), stacked(came).astype(B16), TN)
    if crossing:
        cross_pick, came, refs = refs[0], refs[1 : 1 + crossing], refs[1 + crossing :]
        block = dot32(cross_pick[...].astype(B16), stacked(came).astype(B16), TN)
        refs[-1][...] = beside_lanes(block, folds)[:, : total.shape[1]].astype(B16)
    own_out, outs = refs[0], refs[1 : 1 + ways]
    count = own_out.shape[0]
    own_out[...] = total[:count]
    for i, out in enumerate(outs):
        out[...] = total[(i + 1) * count : (i + 2) * count].astype(B16)


def up_grads_kernel(x_ref, grad_ref, raw_ref, narrow_ref, masked_out, wide_out):
    width = x_ref.shape[1]
    for part in chunks_of(width, width // 2):
        masked = dot32(x_ref[:, part], grad_ref[...], TN) * raw_ref[part, :].astype(F32)
        masked = masked.astype(B16)
        masked_out[part, :] = masked
        wide_out[:, part] = dot32(narrow_ref[1], masked, NT)


def other_grads_kernel(
    x_ref, grad_ref, gate_ref, y_ref, hidden_ref, down_ref, narrow_ref, after_ref, up_wide_ref,
    masked_gate, masked_down, keep_out, give_out, wide_all,
):
    del after_ref
    width, rank = x_ref.shape[1], narrow_ref.shape[1]
    wide_all[pl.ds(rank, rank), :] = up_wide_ref[...]
    for part in chunks_of(width, width // 2):
        masked = dot32(x_ref[:, part], grad_ref[...], TN) * gate_ref[part, :].astype(F32)
        masked = masked.astype(B16)
        masked_gate[part, :] = masked
        wide_all[pl.ds(0, rank), part] = dot32(narrow_ref[0], masked, NT)
        masked = dot32(hidden_ref[...], y_ref[:, part], TN) * down_ref[:, part].astype(F32)
        masked = masked.astype(B16)
        masked_down[:, part] = masked
        wide_all[pl.ds(2 * rank, rank), part] = dot32(narrow_ref[2], masked)
    half = keep_out.shape[1]
    is_lower = lax.axis_index("expert") % 2 == 0

    @pl.when(is_lower)
    def _():
        keep_out[...] = wide_all[:, :half]
        give_out[...] = wide_all[:, half:].astype(B16)

    @pl.when(jnp.logical_not(is_lower))
    def _():
        keep_out[...] = wide_all[:, half:]
        give_out[...] = wide_all[:, :half].astype(B16)


def narrow_kernel(masked_gate, masked_up, masked_down, wide_ref, after_ref, narrow_out):
    del after_ref
    rank = wide_ref.shape[1]
    for i, (masked, dims) in enumerate(((masked_gate, NN), (masked_up, NN), (masked_down, NT))):
        narrow_out[pl.ds(i * rank, rank), :] = dot32(wide_ref[i], masked[...], dims)


def last_kernel(experts, width, ids_ref, keep_ref, own_ref, *refs):
    came, given_ref, (tokens_out, probs_out, wide_out) = refs[:-4], refs[-4], refs[-3:]
    wide_out[...] = keep_ref[...] + given_ref[...].astype(F32)
    total = own_ref[...]
    for ref in came:
        total = total + ref[...].astype(F32)
    tokens_out[...] = total[:, :width].astype(B16)
    extra, ids = total[:, width:], ids_ref[...]
    lane = lax.broadcasted_iota(jnp.int32, extra.shape, 1)
    spot = lax.broadcasted_iota(jnp.int32, ids.shape, 1)
    probs = jnp.zeros(ids.shape, F32)
    for k in range(ids.shape[1]):
        wanted = ids[:, k : k + 1]
        found = jnp.where((lane == wanted) | (lane == wanted + experts), extra, 0.0)
        probs = jnp.where(spot == k, jnp.sum(found, axis=1, keepdims=True), probs)
    probs_out[...] = probs


def body(
    tokens,
    cotangent,
    route_probs,
    expert_ids,
    gate_weight,
    up_weight,
    down_weight,
    narrow,
    wide_factors,
):
    rows, width = tokens.shape
    hidden_units = gate_weight.shape[1]
    top_count = expert_ids.shape[1]
    rank = narrow.shape[1]
    devices = lax.axis_size("expert")
    experts = devices // 2
    capacity = min(rows, max(2, (3 * rows * top_count + 2 * experts - 1) // (2 * experts)))
    near, far = stages()[0], stages()[1:]
    count = rows * devices // 2 // (len(near) + 1)
    slots = count // rows * capacity
    half = (1 + len(near)) * slots
    offsets = [0]
    for masks in far:
        offsets = [first ^ mask for first in offsets for mask in (0, *masks)]
    lanes = -(-2 * experts // 128) * 128
    full = width + lanes

    def pieces_of(block):
        for masks in reversed(far[1:]):
            block = jnp.concatenate([block] + [send(block, mask) for mask in masks], axis=0)
        if far:
            return [block] + [send(block, mask) for mask in far[0]]
        return [block]

    (message,) = in_vmem(
        functools.partial(message_kernel, experts, width),
        [((rows, full + width), B16)],
        (tokens, cotangent, route_probs, expert_ids),
        outside=4,
        scratch=[
            pltpu.VMEM(route_probs.shape, F32),
            pltpu.VMEM(expert_ids.shape, jnp.int32),
            pltpu.SemaphoreType.DMA((4,)),
        ],
    )
    pieces = pieces_of(message)
    crossed = [send(message, mask) for mask in near[2:]]
    matmul = 2 * 2 * half * width * hidden_units
    gate_raw, up_raw, gate_eff, up_eff, narrow, wide = in_vmem(
        up_side_kernel,
        [(gate_weight.shape, B16)] * 4 + [(narrow.shape, B16), ((3, rank, width), B16)],
        (gate_weight, up_weight, narrow, wide_factors, send(wide_factors, 1)),
        2 * matmul,
        outside=4,
        scratch=[
            pltpu.VMEM(wide_factors.shape, B16),
            pltpu.SemaphoreType.DMA((2,)),
            pltpu.SemaphoreType.DMA((8,)),
        ],
    )
    folds, step = folds_of(rows, capacity, full + width)
    probs_at = slice(width, full)
    beside = near[:2]
    pick, *packed = in_vmem(
        functools.partial(
            pack_kernel, (0, *beside), offsets, rows, capacity, probs_at, len(pieces)
        ),
        [(((1 + len(beside)) * slots, count), F32)]
        + [((slots, full + width), B16)] * (1 + len(beside))
        + [((len(offsets) * folds * capacity, folds * rows), F32)] * len(crossed)
        + [((folds * capacity, step), B16)] * (len(offsets) * len(crossed)),
        [wide] + pieces[::-1] + crossed,
    )
    packed, cross_pick, folded = packed[: 1 + len(beside)], packed[1 + len(beside) :], []
    cross_pick, folded = cross_pick[:1], cross_pick[1:]
    came = packed[:1] + [send(block, mask) for block, mask in zip(packed[1:], beside)]
    came += folded[:1] + [send(block, mask) for block, mask in zip(folded[1:], offsets[1:])]
    order = list(range(len(came)))
    if len(came) > 6:
        order = [0, 1, 5, 2, 6, *order[7:], 4, 3]
    down_raw, down_turned, gate_turned, up_turned = in_vmem(
        down_side_kernel,
        [(down_weight.shape, B16), (gate_weight.shape, B16)] + [(down_weight.shape, B16)] * 2,
        (down_weight, narrow, wide, gate_eff, up_eff, pick),
        matmul,
        outside=1,
        scratch=[pltpu.SemaphoreType.DMA((4,))],
    )
    mine_rows, cot_mine = in_vmem(
        functools.partial(stack_kernel, folds, 1 + len(beside), order),
        [((half, full), B16), ((half, width), B16)],
        [down_turned] + [came[i] for i in order],
    )
    token_rows = [mine_rows, send(mine_rows, 1)]
    cot_rows = [cot_mine, send(cot_mine, 1)]

    wide_type, unit_type = ((2 * half, width), B16), ((2 * half, hidden_units), B16)
    x, probs, pre_gate, pre_up = in_vmem(
        functools.partial(pre_kernel, experts, width),
        [wide_type, ((2 * half, 128), F32)] + [((2 * half, hidden_units), F32)] * 2,
        (gate_eff, up_eff, *token_rows),
        2 * matmul,
    )
    y, hidden, grad_gate, grad_up, mine, give = in_vmem(
        functools.partial(mid_kernel, experts, width),
        [wide_type] + [unit_type] * 3 + [((half, full), B16)] * 2,
        (gate_turned, up_turned, down_turned, probs, pre_gate, pre_up, *cot_rows),
        3 * matmul,
    )
    other = send(give, 1)
    masked_up, up_wide = in_vmem(
        up_grads_kernel,
        [(up_weight.shape, B16), ((rank, width), F32)],
        (x, grad_up, up_raw, narrow),
        2 * matmul,
    )
    near_count, cross_count = 1 + len(beside), len(folded)
    fold_step = folds_of(rows, capacity, full)[1]
    sums = in_vmem(
        functools.partial(first_sum_kernel, experts, width, near_count, folds),
        [((slots, full), B16)] * near_count
        + [((folds * capacity, fold_step), B16)] * cross_count,
        (mine, other, up_wide),
    )
    masked_gate, masked_down, keep, give = in_vmem(
        other_grads_kernel,
        [(gate_weight.shape, B16), (down_weight.shape, B16)]
        + [((3 * rank, width // 2), F32), ((3 * rank, width // 2), B16)],
        (x, grad_gate, gate_raw, y, hidden, down_raw, narrow, sums[0], up_wide),
        4 * matmul,
        scratch=[pltpu.VMEM((3 * rank, width), F32)],
    )
    came = [sums[0]] + [send(part, mask) for part, mask in zip(sums[1:near_count], beside)]
    crossing = sums[near_count:]
    came += [*cross_pick, *crossing[:1]]
    came += [send(part, mask) for part, mask in zip(crossing[1:], offsets[1:])]
    order = list(range(len(came)))
    if len(came) > 7:
        order = [0, 3, 4, 1, 6, 2, 7, *order[8:], 5]
    ways = len(far[0]) if far else 0
    own, *parts = in_vmem(
        functools.partial(second_sum_kernel, near_count, folds, cross_count, ways, order),
        [((count // (ways + 1), full), F32)]
        + [((count // (ways + 1), full), B16)] * ways
        + [((rows, full), B16)] * len(crossed)
        + [(give.shape, B16)],
        (give, pick, *[came[i] for i in order]),
    )
    *parts, give = parts
    (grad_narrow,) = in_vmem(
        narrow_kernel,
        [((3 * rank, hidden_units), F32)],
        (masked_gate, masked_up, masked_down, wide, parts[-1]),
        2 * matmul,
        results=(0,),
    )
    from_cross = [send(part, mask) for part, mask in zip(parts[ways:], near[2:])]
    came = [send(part, mask) for part, mask in zip(parts[:ways], far[0] if far else ())]
    for masks in far[1:]:
        total = own
        for part in came:
            total = total + part.astype(F32)
        own, *parts = jnp.split(total, len(masks) + 1, axis=0)
        came = [send(part.astype(B16), mask) for part, mask in zip(parts, masks)]
    came = came[1:] + from_cross + came[:1]
    grad_tokens, grad_probs, grad_wide = in_vmem(
        functools.partial(last_kernel, experts, width),
        [((rows, width), B16), (expert_ids.shape, F32), ((3 * rank, width // 2), F32)],
        (expert_ids, keep, own, *came, send(give, 1)),
        results=(0, 1, 2),
    )
    return (
        grad_tokens,
        grad_probs,
        grad_narrow.reshape(3, rank, hidden_units),
        grad_wide.reshape(3, rank, width // 2),
    )


def solution(mesh):
    in_specs = (
        P(("groups", "expert"), None),
        P(("groups", "expert"), None),
        P(("groups", "expert"), None),
        P(("groups", "expert"), None),
        P(None, "expert"),
        P(None, "expert"),
        P("expert", None),
        P(None, None, "expert"),
        P(None, None, "expert"),
    )
    out_specs = (
        P(("groups", "expert"), None),
        P(("groups", "expert"), None),
        P("groups", None, "expert"),
        P("groups", None, "expert"),
    )
    return jax.shard_map(body, mesh=mesh, in_specs=in_specs, out_specs=out_specs, check_vma=False)
```

```python
import functools
import math

import jax
import jax.numpy as jnp
from jax import lax
from jax.experimental import pallas as pl
from jax.experimental.pallas import tpu as pltpu
from jax.sharding import PartitionSpec as P

NN = (((1,), (0,)), ((), ()))
NT = (((1,), (1,)), ((), ()))
TN = (((0,), (0,)), ((), ()))
F32, B16 = jnp.float32, jnp.bfloat16


def send(value, mask):
    pairs = [(source, source ^ mask) for source in range(lax.axis_size("expert"))]
    return lax.ppermute(value, "expert", pairs)


def stages():
    found, bit, top = [], 1, lax.axis_size("expert").bit_length() - 1
    while bit < top:
        if bit + 1 < top:
            found.append((2**bit, 2 ** (bit + 1), 3 * 2**bit))
        else:
            found.append((2**bit,))
        bit += 2
    return found


def dot32(left, right, dims=NN):
    return lax.dot_general(left, right, dims, preferred_element_type=F32)


def in_vmem(kernel, outs, args, flops=0, outside=0, results=(), scratch=()):
    moved = sum(a.size * a.dtype.itemsize for a in args)
    spaces = [pltpu.HBM] * outside + [pltpu.VMEM] * (len(args) - outside)
    return pl.pallas_call(
        kernel,
        out_shape=[
            (jax.ShapeDtypeStruct if i in results else pltpu.VMEM)(shape, dtype)
            for i, (shape, dtype) in enumerate(outs)
        ],
        in_specs=[pl.BlockSpec(memory_space=space) for space in spaces],
        out_specs=[pl.BlockSpec(memory_space=pltpu.VMEM)] * len(outs),
        scratch_shapes=list(scratch),
        compiler_params=pltpu.CompilerParams(vmem_limit_bytes=8 * 2**20),
        cost_estimate=pl.CostEstimate(flops=flops, bytes_accessed=moved, transcendentals=0),
    )(*[pltpu.with_memory_space_constraint(a, space) for a, space in zip(args, spaces)])


def stacked(refs):
    return jnp.concatenate([ref[...].astype(F32) for ref in refs], axis=0)


def chunks_of(width, step=512):
    return [pl.ds(at, step) for at in range(0, width, step)]


def copied(sources, targets, sems):
    copies = [pltpu.make_async_copy(*pair, sems.at[i]) for i, pair in enumerate(zip(sources, targets))]
    for copy in copies:
        copy.start()
    return copies


def message_kernel(experts, tokens_ref, cot_ref, probs_ref, ids_ref, out_ref):
    width = tokens_ref.shape[1]
    tail = out_ref.shape[1] - width
    ids, probs = ids_ref[...], probs_ref[...]
    high = probs.astype(B16).astype(F32)
    low = probs - high
    lane = lax.broadcasted_iota(jnp.int32, (ids.shape[0], tail - width), 1)
    extra = jnp.zeros(lane.shape, F32)
    for k in range(ids.shape[1]):
        one = slice(k, k + 1)
        extra = jnp.where(lane == ids[:, one], high[:, one], extra)
        extra = jnp.where(lane == ids[:, one] + experts, low[:, one], extra)
    out_ref[:, :width] = tokens_ref[...]
    out_ref[:, width:tail] = extra.astype(B16)
    out_ref[:, tail:] = cot_ref[...]


def started(sources, raws, sems, ahead):
    pieces, parts = sems.shape[0] // len(sources), []
    for i, (source, raw) in enumerate(zip(sources, raws)):
        step = source.shape[0] // pieces
        for j in range(pieces):
            rows = pl.ds(j * step, step)
            sem = sems.at[i * pieces + j]
            parts.append((i, rows, pltpu.make_async_copy(source.at[rows, :], raw.at[rows, :], sem)))
    for _, _, copy in parts[:ahead]:
        copy.start()
    return parts


def up_side_kernel(gate_ref, up_ref, narrow_hbm, mine_hbm, other_ref, *refs):
    raws, outs, (narrow_out, wide_out, mine_ref, small_sems, sems) = refs[:2], refs[2:4], refs[4:]
    for copy in copied((narrow_hbm, mine_hbm), (narrow_out, mine_ref), small_sems):
        copy.wait()
    half = mine_ref.shape[2]
    is_lower = lax.axis_index("expert") % 2 == 0

    @pl.when(is_lower)
    def _():
        wide_out[:, :, :half] = mine_ref[...]
        wide_out[:, :, half:] = other_ref[...]

    @pl.when(jnp.logical_not(is_lower))
    def _():
        wide_out[:, :, :half] = other_ref[...]
        wide_out[:, :, half:] = mine_ref[...]

    ahead = 5
    parts = started((gate_ref, up_ref), raws, sems, ahead)
    for at, (i, rows, copy) in enumerate(parts):
        copy.wait()
        if at + ahead < len(parts):
            parts[at + ahead][2].start()
        for line in range(rows.start, rows.start + rows.size, 128):
            lines = pl.ds(line, 128)
            factor = 1.0 + dot32(wide_out[i, :, lines], narrow_out[i], TN)
            outs[i][lines, :] = (raws[i][lines, :].astype(F32) * factor).astype(B16)


def down_side_kernel(
    down_ref, narrow_ref, wide_ref, gate_ref, up_ref, after_ref, raw, down_out, gate_out, up_out, sems
):
    del after_ref
    parts = started((down_ref,), (raw,), sems, sems.shape[0])
    for source, out in ((gate_ref, gate_out), (up_ref, up_out)):
        for lines in chunks_of(source.shape[0]):
            out[:, lines] = source[lines, :].T
    for _, rows, copy in parts:
        copy.wait()
        for lanes in chunks_of(raw.shape[1]):
            factor = 1.0 + dot32(narrow_ref[2, :, rows], wide_ref[2, :, lanes], TN)
            down_out[lanes, rows] = (raw[rows, lanes].astype(F32) * factor).astype(B16).T


def picks_of(extra, wanted_experts, rows, capacity):
    count, lanes = extra.shape
    slots = count // rows * capacity
    named = (extra > 0.0).astype(B16)
    kinds = -(-len(wanted_experts) // 8) * 8
    lane = lax.broadcasted_iota(jnp.int32, (kinds, lanes), 1)
    line = lax.broadcasted_iota(jnp.int32, (kinds, lanes), 0)
    wanted = jnp.zeros((kinds, lanes), F32)
    for i, expert in enumerate(wanted_experts):
        wanted = jnp.where((line == i) & (lane == expert), 1.0, wanted)
    chosen = dot32(wanted.astype(B16), named, NT)
    earlier = lax.broadcasted_iota(jnp.int32, (count, count), 0)
    later = lax.broadcasted_iota(jnp.int32, (count, count), 1)
    before = (earlier // rows == later // rows) & (earlier < later)
    slot = dot32(chosen.astype(B16), before.astype(F32).astype(B16))
    to = lax.broadcasted_iota(jnp.int32, (slots, count), 0)
    of = lax.broadcasted_iota(jnp.int32, (slots, count), 1)
    in_block = to // capacity == of // rows
    place = (to % capacity).astype(F32)
    picks = []
    for i in range(len(wanted_experts)):
        pick = in_block & (place == slot[i : i + 1, :]) & (chosen[i : i + 1, :] > 0.5)
        picks.append(jnp.where(pick, 1.0, 0.0))
    return picks


def folds_of(rows, capacity, lanes):
    folds = rows // math.gcd(rows, capacity)
    return folds, -(-lanes // (128 * folds)) * 128


def write_rows(outs, rows):
    first = 0
    for out in outs:
        out[...] = rows[first : first + out.shape[0]].astype(B16)
        first += out.shape[0]


def pack_kernel(masks, offsets, rows, capacity, lanes, blocks, after_ref, *refs):
    del after_ref
    came, refs = refs[:blocks], refs[blocks:]
    crossing = refs[0].shape[0] == rows and len(refs) > 1 + len(masks)
    crossed, (pick_out, *outs) = (refs[:1], refs[1:]) if crossing else ((), refs)
    block = stacked(came[::-1])
    me = lax.axis_index("expert")
    picks = picks_of(block[:, lanes], [(me ^ mask) // 2 for mask in masks], rows, capacity)
    picks = jnp.concatenate(picks, axis=0)
    pick_out[...] = picks
    write_rows(outs[: len(masks)], dot32(picks.astype(B16), block.astype(B16)))
    for ref in crossed:
        block = ref[...].astype(F32)
        folds, step = folds_of(rows, capacity, block.shape[1])
        extra = jnp.concatenate([block[:, lanes]] * folds, axis=0)
        picks = picks_of(extra, [(me ^ offset) // 2 for offset in offsets], rows, capacity)
        picks = jnp.concatenate(picks, axis=0)
        outs[len(masks)][...] = picks
        laid = lane_pieces(block, folds, step).astype(B16)
        write_rows(outs[len(masks) + 1 :], dot32(picks.astype(B16), laid))


def lane_pieces(block, folds, step):
    rows, width = block.shape
    if folds * step > width:
        block = jnp.concatenate([block, jnp.zeros((rows, folds * step - width), F32)], axis=1)
    return jnp.concatenate([block[:, i * step : (i + 1) * step] for i in range(folds)], axis=0)


def piece_order(total, folds, blocks, back):
    capacity = total // (folds * blocks)
    to = lax.broadcasted_iota(jnp.int32, (total, total), 1 if back else 0)
    of = lax.broadcasted_iota(jnp.int32, (total, total), 0 if back else 1)
    same = to % capacity == of % capacity
    same &= to // (blocks * capacity) == of // capacity % folds
    same &= to // capacity % blocks == of // (folds * capacity)
    return jnp.where(same, 1.0, 0.0).astype(B16)


def beside_lanes(laid, folds):
    rows = laid.shape[0] // folds
    return jnp.concatenate([laid[i * rows : (i + 1) * rows] for i in range(folds)], axis=1)


def unfolded(refs, folds):
    laid = stacked(refs).astype(B16)
    return beside_lanes(dot32(piece_order(laid.shape[0], folds, len(refs), False), laid), folds)


def stack_kernel(folds, beside, order, after_ref, *refs):
    del after_ref
    came, (tokens_out, cot_out) = refs[:-2], refs[-2:]
    came = [came[order.index(i)] for i in range(len(order))]
    near, folded = came[:beside], came[beside:]
    pieces = [ref[...].astype(F32) for ref in near]
    if folded:
        pieces.append(unfolded(folded, folds))
    full, both = tokens_out.shape[1], tokens_out.shape[1] + cot_out.shape[1]
    for out, lanes in ((tokens_out, slice(0, full)), (cot_out, slice(full, both))):
        out[...] = jnp.concatenate([piece[:, lanes] for piece in pieces], axis=0).astype(B16)


def pre_kernel(experts, width, gate_ref, up_ref, *refs):
    pieces, (x_ref, prob_ref, pre_gate_ref, pre_up_ref) = refs[:-4], refs[-4:]
    for part in chunks_of(width):
        x_ref[:, part] = jnp.concatenate(
            [piece[:, part].astype(F32) for piece in pieces], axis=0
        ).astype(B16)
    extra = jnp.concatenate([piece[:, width:].astype(F32) for piece in pieces], axis=0)
    lane = lax.broadcasted_iota(jnp.int32, extra.shape, 1)
    own = (lane % experts == lax.axis_index("expert") // 2) & (lane < 2 * experts)
    probs = jnp.sum(jnp.where(own, extra, 0.0), axis=1, keepdims=True)
    prob_ref[...] = jnp.broadcast_to(probs, prob_ref.shape)
    pre_gate_ref[...] = dot32(x_ref[...], gate_ref[...])
    pre_up_ref[...] = dot32(x_ref[...], up_ref[...])


def mid_kernel(
    experts, width, gate_ref, up_ref, down_ref, prob_ref, pre_gate_ref, pre_up_ref, *refs
):
    pieces, outs = refs[:-6], refs[-6:]
    y_ref, hidden_ref, grad_gate_ref, grad_up_ref, mine_ref, give_ref = outs
    for part in chunks_of(width):
        y_ref[:, part] = jnp.concatenate(
            [piece[:, part].astype(F32) for piece in pieces], axis=0
        ).astype(B16)
    grad_full = dot32(y_ref[...], down_ref[...])
    pre_gate, pre_up = pre_gate_ref[...], pre_up_ref[...]
    probs = prob_ref[:, :1]
    routed = probs > 0.0
    sigmoid_gate = jax.nn.sigmoid(pre_gate)
    activated = pre_gate * sigmoid_gate
    hidden = jnp.where(routed, activated * pre_up, 0.0)
    hidden_ref[...] = (hidden * probs).astype(B16)
    own_probs = jnp.sum(hidden * grad_full, axis=1, keepdims=True)
    grad_hidden = grad_full * probs
    grad_gate_ref[...] = jnp.where(
        routed, grad_hidden * pre_up * sigmoid_gate * (1.0 + pre_gate * (1.0 - sigmoid_gate)), 0.0
    ).astype(B16)
    grad_up_ref[...] = jnp.where(routed, grad_hidden * activated, 0.0).astype(B16)
    half = mine_ref.shape[0]
    for part in chunks_of(width):
        product = dot32(grad_gate_ref[...], gate_ref[:, part])
        product = product + dot32(grad_up_ref[...], up_ref[:, part])
        mine_ref[:, part] = product[:half].astype(B16)
        give_ref[:, part] = product[half:].astype(B16)
    lanes = mine_ref.shape[1] - width
    lane = lax.broadcasted_iota(jnp.int32, (2 * half, lanes), 1)
    expert = lax.axis_index("expert") // 2
    high = own_probs.astype(B16).astype(F32)
    extra = jnp.where(lane == expert, high, jnp.where(lane == expert + experts, own_probs - high, 0.0))
    mine_ref[:, width:] = extra[:half].astype(B16)
    give_ref[:, width:] = extra[half:].astype(B16)


def first_sum_kernel(experts, width, near, folds, mine_ref, other_ref, after_ref, *outs):
    del after_ref
    total = mine_ref[...].astype(F32) + other_ref[...].astype(F32)
    extra = total[:, width:]
    lane = lax.broadcasted_iota(jnp.int32, extra.shape, 1)
    lost = jnp.where(lane < experts, extra - extra.astype(B16).astype(F32), 0.0)
    extra = extra + pltpu.roll(lost, experts, 1) - lost
    slots = outs[0].shape[0]
    for i, out in enumerate(outs[:near]):
        part = slice(i * slots, (i + 1) * slots)
        out[:, :width] = total[part, :width].astype(B16)
        out[:, width:] = extra[part].astype(B16)
    if outs[near:]:
        rest = jnp.concatenate([total[near * slots :, :width], extra[near * slots :]], axis=1)
        laid = lane_pieces(rest, folds, outs[near].shape[1]).astype(B16)
        write_rows(outs[near:], dot32(piece_order(laid.shape[0], folds, len(outs[near:]), True), laid))


def second_sum_kernel(near, folds, crossing, ways, order, give_ref, pick_ref, *refs):
    refs[-1][...] = give_ref[...]
    refs = refs[:-1]
    came = [refs[order.index(i)] for i in range(len(order))]
    came, refs = came[:near], (*came[near:], *refs[len(order) :])
    total = dot32(pick_ref[...].astype(B16), stacked(came).astype(B16), TN)
    if crossing:
        cross_pick, came, refs = refs[0], refs[1 : 1 + crossing], refs[1 + crossing :]
        block = dot32(cross_pick[...].astype(B16), stacked(came).astype(B16), TN)
        refs[-1][...] = beside_lanes(block, folds)[:, : total.shape[1]].astype(B16)
    own_out, outs = refs[0], refs[1 : 1 + ways]
    count = own_out.shape[0]
    own_out[...] = total[:count]
    for i, out in enumerate(outs):
        out[...] = total[(i + 1) * count : (i + 2) * count].astype(B16)


def up_grads_kernel(x_ref, grad_ref, raw_ref, narrow_ref, masked_out, wide_out):
    width = x_ref.shape[1]
    for part in chunks_of(width, width // 2):
        masked = dot32(x_ref[:, part], grad_ref[...], TN) * raw_ref[part, :].astype(F32)
        masked = masked.astype(B16)
        masked_out[part, :] = masked
        wide_out[:, part] = dot32(narrow_ref[1], masked, NT)


def other_grads_kernel(
    x_ref, grad_ref, gate_ref, y_ref, hidden_ref, down_ref, narrow_ref, after_ref, up_wide_ref,
    masked_gate, masked_down, keep_out, give_out, wide_all,
):
    del after_ref
    width, rank = x_ref.shape[1], narrow_ref.shape[1]
    wide_all[pl.ds(rank, rank), :] = up_wide_ref[...]
    for part in chunks_of(width, width // 2):
        masked = dot32(x_ref[:, part], grad_ref[...], TN) * gate_ref[part, :].astype(F32)
        masked = masked.astype(B16)
        masked_gate[part, :] = masked
        wide_all[pl.ds(0, rank), part] = dot32(narrow_ref[0], masked, NT)
        masked = dot32(hidden_ref[...], y_ref[:, part], TN) * down_ref[:, part].astype(F32)
        masked = masked.astype(B16)
        masked_down[:, part] = masked
        wide_all[pl.ds(2 * rank, rank), part] = dot32(narrow_ref[2], masked)
    half = keep_out.shape[1]
    is_lower = lax.axis_index("expert") % 2 == 0

    @pl.when(is_lower)
    def _():
        keep_out[...] = wide_all[:, :half]
        give_out[...] = wide_all[:, half:].astype(B16)

    @pl.when(jnp.logical_not(is_lower))
    def _():
        keep_out[...] = wide_all[:, half:]
        give_out[...] = wide_all[:, :half].astype(B16)


def narrow_kernel(masked_gate, masked_up, masked_down, wide_ref, after_ref, narrow_out):
    del after_ref
    rank = wide_ref.shape[1]
    for i, (masked, dims) in enumerate(((masked_gate, NN), (masked_up, NN), (masked_down, NT))):
        narrow_out[pl.ds(i * rank, rank), :] = dot32(wide_ref[i], masked[...], dims)


def last_kernel(experts, width, ids_ref, keep_ref, own_ref, *refs):
    came, given_ref, (tokens_out, probs_out, wide_out) = refs[:-4], refs[-4], refs[-3:]
    wide_out[...] = keep_ref[...] + given_ref[...].astype(F32)
    total = own_ref[...]
    for ref in came:
        total = total + ref[...].astype(F32)
    tokens_out[...] = total[:, :width].astype(B16)
    extra, ids = total[:, width:], ids_ref[...]
    lane = lax.broadcasted_iota(jnp.int32, extra.shape, 1)
    spot = lax.broadcasted_iota(jnp.int32, ids.shape, 1)
    probs = jnp.zeros(ids.shape, F32)
    for k in range(ids.shape[1]):
        wanted = ids[:, k : k + 1]
        found = jnp.where((lane == wanted) | (lane == wanted + experts), extra, 0.0)
        probs = jnp.where(spot == k, jnp.sum(found, axis=1, keepdims=True), probs)
    probs_out[...] = probs


def body(
    tokens,
    cotangent,
    route_probs,
    expert_ids,
    gate_weight,
    up_weight,
    down_weight,
    narrow,
    wide_factors,
):
    rows, width = tokens.shape
    hidden_units = gate_weight.shape[1]
    top_count = expert_ids.shape[1]
    rank = narrow.shape[1]
    devices = lax.axis_size("expert")
    experts = devices // 2
    capacity = min(rows, max(2, (3 * rows * top_count + 2 * experts - 1) // (2 * experts)))
    near, far = stages()[0], stages()[1:]
    count = rows * devices // 2 // (len(near) + 1)
    slots = count // rows * capacity
    half = (1 + len(near)) * slots
    offsets = [0]
    for masks in far:
        offsets = [first ^ mask for first in offsets for mask in (0, *masks)]
    lanes = -(-2 * experts // 128) * 128
    full = width + lanes

    def pieces_of(block):
        for masks in reversed(far[1:]):
            block = jnp.concatenate([block] + [send(block, mask) for mask in masks], axis=0)
        if far:
            return [block] + [send(block, mask) for mask in far[0]]
        return [block]

    sources = (tokens, cotangent, route_probs, expert_ids)
    message = pl.pallas_call(
        functools.partial(message_kernel, experts),
        grid=(1,),
        out_shape=pltpu.VMEM((rows, full + width), B16),
        in_specs=[pl.BlockSpec(source.shape, lambda step: (0, 0)) for source in sources],
        out_specs=pl.BlockSpec(memory_space=pltpu.VMEM),
        compiler_params=pltpu.CompilerParams(vmem_limit_bytes=8 * 2**20),
        cost_estimate=pl.CostEstimate(flops=0, bytes_accessed=4 * rows * (full + width), transcendentals=0),
    )(*[pltpu.with_memory_space_constraint(source, pltpu.HBM) for source in sources])
    pieces = pieces_of(message)
    crossed = [send(message, mask) for mask in near[2:]]
    matmul = 2 * 2 * half * width * hidden_units
    gate_raw, up_raw, gate_eff, up_eff, narrow, wide = in_vmem(
        up_side_kernel,
        [(gate_weight.shape, B16)] * 4 + [(narrow.shape, B16), ((3, rank, width), B16)],
        (gate_weight, up_weight, narrow, wide_factors, send(wide_factors, 1)),
        2 * matmul,
        outside=4,
        scratch=[
            pltpu.VMEM(wide_factors.shape, B16),
            pltpu.SemaphoreType.DMA((2,)),
            pltpu.SemaphoreType.DMA((8,)),
        ],
    )
    folds, step = folds_of(rows, capacity, full + width)
    probs_at = slice(width, full)
    beside = near[:2]
    pick, *packed = in_vmem(
        functools.partial(
            pack_kernel, (0, *beside), offsets, rows, capacity, probs_at, len(pieces)
        ),
        [(((1 + len(beside)) * slots, count), F32)]
        + [((slots, full + width), B16)] * (1 + len(beside))
        + [((len(offsets) * folds * capacity, folds * rows), F32)] * len(crossed)
        + [((folds * capacity, step), B16)] * (len(offsets) * len(crossed)),
        [wide] + pieces[::-1] + crossed,
    )
    packed, cross_pick, folded = packed[: 1 + len(beside)], packed[1 + len(beside) :], []
    cross_pick, folded = cross_pick[:1], cross_pick[1:]
    came = packed[:1] + [send(block, mask) for block, mask in zip(packed[1:], beside)]
    came += folded[:1] + [send(block, mask) for block, mask in zip(folded[1:], offsets[1:])]
    order = list(range(len(came)))
    if len(came) > 6:
        order = [0, 1, 5, 2, 6, *order[7:], 4, 3]
    down_raw, down_turned, gate_turned, up_turned = in_vmem(
        down_side_kernel,
        [(down_weight.shape, B16), (gate_weight.shape, B16)] + [(down_weight.shape, B16)] * 2,
        (down_weight, narrow, wide, gate_eff, up_eff, pick),
        matmul,
        outside=1,
        scratch=[pltpu.SemaphoreType.DMA((4,))],
    )
    mine_rows, cot_mine = in_vmem(
        functools.partial(stack_kernel, folds, 1 + len(beside), order),
        [((half, full), B16), ((half, width), B16)],
        [down_turned] + [came[i] for i in order],
    )
    token_rows = [mine_rows, send(mine_rows, 1)]
    cot_rows = [cot_mine, send(cot_mine, 1)]

    wide_type, unit_type = ((2 * half, width), B16), ((2 * half, hidden_units), B16)
    x, probs, pre_gate, pre_up = in_vmem(
        functools.partial(pre_kernel, experts, width),
        [wide_type, ((2 * half, 128), F32)] + [((2 * half, hidden_units), F32)] * 2,
        (gate_eff, up_eff, *token_rows),
        2 * matmul,
    )
    y, hidden, grad_gate, grad_up, mine, give = in_vmem(
        functools.partial(mid_kernel, experts, width),
        [wide_type] + [unit_type] * 3 + [((half, full), B16)] * 2,
        (gate_turned, up_turned, down_turned, probs, pre_gate, pre_up, *cot_rows),
        3 * matmul,
    )
    other = send(give, 1)
    masked_up, up_wide = in_vmem(
        up_grads_kernel,
        [(up_weight.shape, B16), ((rank, width), F32)],
        (x, grad_up, up_raw, narrow),
        2 * matmul,
    )
    near_count, cross_count = 1 + len(beside), len(folded)
    fold_step = folds_of(rows, capacity, full)[1]
    sums = in_vmem(
        functools.partial(first_sum_kernel, experts, width, near_count, folds),
        [((slots, full), B16)] * near_count
        + [((folds * capacity, fold_step), B16)] * cross_count,
        (mine, other, up_wide),
    )
    masked_gate, masked_down, keep, give = in_vmem(
        other_grads_kernel,
        [(gate_weight.shape, B16), (down_weight.shape, B16)]
        + [((3 * rank, width // 2), F32), ((3 * rank, width // 2), B16)],
        (x, grad_gate, gate_raw, y, hidden, down_raw, narrow, sums[0], up_wide),
        4 * matmul,
        scratch=[pltpu.VMEM((3 * rank, width), F32)],
    )
    came = [sums[0]] + [send(part, mask) for part, mask in zip(sums[1:near_count], beside)]
    crossing = sums[near_count:]
    came += [*cross_pick, *crossing[:1]]
    came += [send(part, mask) for part, mask in zip(crossing[1:], offsets[1:])]
    order = list(range(len(came)))
    if len(came) > 7:
        order = [0, 3, 4, 1, 6, 2, 7, *order[8:], 5]
    ways = len(far[0]) if far else 0
    own, *parts = in_vmem(
        functools.partial(second_sum_kernel, near_count, folds, cross_count, ways, order),
        [((count // (ways + 1), full), F32)]
        + [((count // (ways + 1), full), B16)] * ways
        + [((rows, full), B16)] * len(crossed)
        + [(give.shape, B16)],
        (give, pick, *[came[i] for i in order]),
    )
    *parts, give = parts
    (grad_narrow,) = in_vmem(
        narrow_kernel,
        [((3 * rank, hidden_units), F32)],
        (masked_gate, masked_up, masked_down, wide, parts[-1]),
        2 * matmul,
        results=(0,),
    )
    from_cross = [send(part, mask) for part, mask in zip(parts[ways:], near[2:])]
    came = [send(part, mask) for part, mask in zip(parts[:ways], far[0] if far else ())]
    for masks in far[1:]:
        total = own
        for part in came:
            total = total + part.astype(F32)
        own, *parts = jnp.split(total, len(masks) + 1, axis=0)
        came = [send(part.astype(B16), mask) for part, mask in zip(parts, masks)]
    came = came[1:] + from_cross + came[:1]
    grad_tokens, grad_probs, grad_wide = in_vmem(
        functools.partial(last_kernel, experts, width),
        [((rows, width), B16), (expert_ids.shape, F32), ((3 * rank, width // 2), F32)],
        (expert_ids, keep, own, *came, send(give, 1)),
        results=(0, 1, 2),
    )
    return (
        grad_tokens,
        grad_probs,
        grad_narrow.reshape(3, rank, hidden_units),
        grad_wide.reshape(3, rank, width // 2),
    )


def solution(mesh):
    in_specs = (
        P(("groups", "expert"), None),
        P(("groups", "expert"), None),
        P(("groups", "expert"), None),
        P(("groups", "expert"), None),
        P(None, "expert"),
        P(None, "expert"),
        P("expert", None),
        P(None, None, "expert"),
        P(None, None, "expert"),
    )
    out_specs = (
        P(("groups", "expert"), None),
        P(("groups", "expert"), None),
        P("groups", None, "expert"),
        P("groups", None, "expert"),
    )
    return jax.shard_map(body, mesh=mesh, in_specs=in_specs, out_specs=out_specs, check_vma=False)
```

```python
import functools
import math

import jax
import jax.numpy as jnp
from jax import lax
from jax.experimental import pallas as pl
from jax.experimental.pallas import tpu as pltpu
from jax.sharding import PartitionSpec as P

NN = (((1,), (0,)), ((), ()))
NT = (((1,), (1,)), ((), ()))
TN = (((0,), (0,)), ((), ()))
F32, B16 = jnp.float32, jnp.bfloat16


def send(value, mask):
    pairs = [(source, source ^ mask) for source in range(lax.axis_size("expert"))]
    return lax.ppermute(value, "expert", pairs)


def stages():
    found, bit, top = [], 1, lax.axis_size("expert").bit_length() - 1
    while bit < top:
        if bit + 1 < top:
            found.append((2**bit, 2 ** (bit + 1), 3 * 2**bit))
        else:
            found.append((2**bit,))
        bit += 2
    return found


def dot32(left, right, dims=NN):
    return lax.dot_general(left, right, dims, preferred_element_type=F32)


def in_vmem(kernel, outs, args, flops=0, outside=0, results=(), scratch=()):
    moved = sum(a.size * a.dtype.itemsize for a in args)
    spaces = [pltpu.HBM] * outside + [pltpu.VMEM] * (len(args) - outside)
    return pl.pallas_call(
        kernel,
        out_shape=[
            (jax.ShapeDtypeStruct if i in results else pltpu.VMEM)(shape, dtype)
            for i, (shape, dtype) in enumerate(outs)
        ],
        in_specs=[pl.BlockSpec(memory_space=space) for space in spaces],
        out_specs=[pl.BlockSpec(memory_space=pltpu.VMEM)] * len(outs),
        scratch_shapes=list(scratch),
        compiler_params=pltpu.CompilerParams(vmem_limit_bytes=8 * 2**20),
        cost_estimate=pl.CostEstimate(flops=flops, bytes_accessed=moved, transcendentals=0),
    )(*[pltpu.with_memory_space_constraint(a, space) for a, space in zip(args, spaces)])


def stacked(refs):
    return jnp.concatenate([ref[...].astype(F32) for ref in refs], axis=0)


def chunks_of(width, step=512):
    return [pl.ds(at, step) for at in range(0, width, step)]


def copied(sources, targets, sems):
    copies = [pltpu.make_async_copy(*pair, sems.at[i]) for i, pair in enumerate(zip(sources, targets))]
    for copy in copies:
        copy.start()
    return copies


def message_kernel(experts, tokens_ref, cot_ref, probs_ref, ids_ref, out_ref):
    width = tokens_ref.shape[1]
    tail = out_ref.shape[1] - width
    ids, probs = ids_ref[...], probs_ref[...]
    high = probs.astype(B16).astype(F32)
    low = probs - high
    lane = lax.broadcasted_iota(jnp.int32, (ids.shape[0], tail - width), 1)
    extra = jnp.zeros(lane.shape, F32)
    for k in range(ids.shape[1]):
        one = slice(k, k + 1)
        extra = jnp.where(lane == ids[:, one], high[:, one], extra)
        extra = jnp.where(lane == ids[:, one] + experts, low[:, one], extra)
    out_ref[:, :width] = tokens_ref[...]
    out_ref[:, width:tail] = extra.astype(B16)
    out_ref[:, tail:] = cot_ref[...]


def started(sources, raws, sems, ahead):
    pieces, parts = sems.shape[0] // len(sources), []
    for i, (source, raw) in enumerate(zip(sources, raws)):
        step = source.shape[0] // pieces
        for j in range(pieces):
            rows = pl.ds(j * step, step)
            sem = sems.at[i * pieces + j]
            parts.append((i, rows, pltpu.make_async_copy(source.at[rows, :], raw.at[rows, :], sem)))
    for _, _, copy in parts[:ahead]:
        copy.start()
    return parts


def up_side_kernel(gate_ref, up_ref, narrow_hbm, mine_hbm, other_ref, *refs):
    raws, outs, (narrow_out, wide_out, mine_ref, small_sems, sems) = refs[:2], refs[2:4], refs[4:]
    for copy in copied((narrow_hbm, mine_hbm), (narrow_out, mine_ref), small_sems):
        copy.wait()
    half = mine_ref.shape[2]
    is_lower = lax.axis_index("expert") % 2 == 0

    @pl.when(is_lower)
    def _():
        wide_out[:, :, :half] = mine_ref[...]
        wide_out[:, :, half:] = other_ref[...]

    @pl.when(jnp.logical_not(is_lower))
    def _():
        wide_out[:, :, :half] = other_ref[...]
        wide_out[:, :, half:] = mine_ref[...]

    ahead = 5
    parts = started((gate_ref, up_ref), raws, sems, ahead)
    for at, (i, rows, copy) in enumerate(parts):
        copy.wait()
        if at + ahead < len(parts):
            parts[at + ahead][2].start()
        for line in range(rows.start, rows.start + rows.size, 128):
            lines = pl.ds(line, 128)
            factor = 1.0 + dot32(wide_out[i, :, lines], narrow_out[i], TN)
            outs[i][lines, :] = (raws[i][lines, :].astype(F32) * factor).astype(B16)


def down_side_kernel(
    down_ref, narrow_ref, wide_ref, gate_ref, up_ref, after_ref, raw, down_out, gate_out, up_out, sems
):
    del after_ref
    parts = started((down_ref,), (raw,), sems, sems.shape[0])
    for source, out in ((gate_ref, gate_out), (up_ref, up_out)):
        for lines in chunks_of(source.shape[0]):
            out[:, lines] = source[lines, :].T
    for _, rows, copy in parts:
        copy.wait()
        for lanes in chunks_of(raw.shape[1]):
            factor = 1.0 + dot32(narrow_ref[2, :, rows], wide_ref[2, :, lanes], TN)
            down_out[lanes, rows] = (raw[rows, lanes].astype(F32) * factor).astype(B16).T


def picks_of(extra, wanted_experts, rows, capacity):
    count, lanes = extra.shape
    slots = count // rows * capacity
    named = (extra > 0.0).astype(B16)
    kinds = -(-len(wanted_experts) // 8) * 8
    lane = lax.broadcasted_iota(jnp.int32, (kinds, lanes), 1)
    line = lax.broadcasted_iota(jnp.int32, (kinds, lanes), 0)
    wanted = jnp.zeros((kinds, lanes), F32)
    for i, expert in enumerate(wanted_experts):
        wanted = jnp.where((line == i) & (lane == expert), 1.0, wanted)
    chosen = dot32(wanted.astype(B16), named, NT)
    earlier = lax.broadcasted_iota(jnp.int32, (count, count), 0)
    later = lax.broadcasted_iota(jnp.int32, (count, count), 1)
    before = (earlier // rows == later // rows) & (earlier < later)
    slot = dot32(chosen.astype(B16), before.astype(F32).astype(B16))
    to = lax.broadcasted_iota(jnp.int32, (slots, count), 0)
    of = lax.broadcasted_iota(jnp.int32, (slots, count), 1)
    in_block = to // capacity == of // rows
    place = (to % capacity).astype(F32)
    picks = []
    for i in range(len(wanted_experts)):
        pick = in_block & (place == slot[i : i + 1, :]) & (chosen[i : i + 1, :] > 0.5)
        picks.append(jnp.where(pick, 1.0, 0.0))
    return picks


def folds_of(rows, capacity, lanes):
    folds = rows // math.gcd(rows, capacity)
    return folds, -(-lanes // (128 * folds)) * 128


def write_rows(outs, rows):
    first = 0
    for out in outs:
        out[...] = rows[first : first + out.shape[0]].astype(B16)
        first += out.shape[0]


def pack_kernel(masks, offsets, rows, capacity, lanes, blocks, after_ref, *refs):
    del after_ref
    came, refs = refs[:blocks], refs[blocks:]
    crossing = refs[0].shape[0] == rows and len(refs) > 1 + len(masks)
    crossed, (pick_out, *outs) = (refs[:1], refs[1:]) if crossing else ((), refs)
    block = stacked(came[::-1])
    me = lax.axis_index("expert")
    picks = picks_of(block[:, lanes], [(me ^ mask) // 2 for mask in masks], rows, capacity)
    picks = jnp.concatenate(picks, axis=0)
    pick_out[...] = picks
    write_rows(outs[: len(masks)], dot32(picks.astype(B16), block.astype(B16)))
    for ref in crossed:
        block = ref[...].astype(F32)
        folds, step = folds_of(rows, capacity, block.shape[1])
        extra = jnp.concatenate([block[:, lanes]] * folds, axis=0)
        picks = picks_of(extra, [(me ^ offset) // 2 for offset in offsets], rows, capacity)
        picks = jnp.concatenate(picks, axis=0)
        outs[len(masks)][...] = picks
        laid = lane_pieces(block, folds, step).astype(B16)
        write_rows(outs[len(masks) + 1 :], dot32(picks.astype(B16), laid))


def lane_pieces(block, folds, step):
    rows, width = block.shape
    if folds * step > width:
        block = jnp.concatenate([block, jnp.zeros((rows, folds * step - width), F32)], axis=1)
    return jnp.concatenate([block[:, i * step : (i + 1) * step] for i in range(folds)], axis=0)


def piece_order(total, folds, blocks, back):
    capacity = total // (folds * blocks)
    to = lax.broadcasted_iota(jnp.int32, (total, total), 1 if back else 0)
    of = lax.broadcasted_iota(jnp.int32, (total, total), 0 if back else 1)
    same = to % capacity == of % capacity
    same &= to // (blocks * capacity) == of // capacity % folds
    same &= to // capacity % blocks == of // (folds * capacity)
    return jnp.where(same, 1.0, 0.0).astype(B16)


def beside_lanes(laid, folds):
    rows = laid.shape[0] // folds
    return jnp.concatenate([laid[i * rows : (i + 1) * rows] for i in range(folds)], axis=1)


def unfolded(refs, folds):
    laid = stacked(refs).astype(B16)
    return beside_lanes(dot32(piece_order(laid.shape[0], folds, len(refs), False), laid), folds)


def stack_kernel(folds, beside, order, after_ref, *refs):
    del after_ref
    came, (tokens_out, cot_out) = refs[:-2], refs[-2:]
    came = [came[order.index(i)] for i in range(len(order))]
    near, folded = came[:beside], came[beside:]
    pieces = [ref[...].astype(F32) for ref in near]
    if folded:
        pieces.append(unfolded(folded, folds))
    full, both = tokens_out.shape[1], tokens_out.shape[1] + cot_out.shape[1]
    for out, lanes in ((tokens_out, slice(0, full)), (cot_out, slice(full, both))):
        out[...] = jnp.concatenate([piece[:, lanes] for piece in pieces], axis=0).astype(B16)


def pre_kernel(experts, width, gate_ref, up_ref, *refs):
    pieces, (x_ref, prob_ref, pre_gate_ref, pre_up_ref) = refs[:-4], refs[-4:]
    for part in chunks_of(width):
        x_ref[:, part] = jnp.concatenate(
            [piece[:, part].astype(F32) for piece in pieces], axis=0
        ).astype(B16)
    extra = jnp.concatenate([piece[:, width:].astype(F32) for piece in pieces], axis=0)
    lane = lax.broadcasted_iota(jnp.int32, extra.shape, 1)
    own = (lane % experts == lax.axis_index("expert") // 2) & (lane < 2 * experts)
    probs = jnp.sum(jnp.where(own, extra, 0.0), axis=1, keepdims=True)
    prob_ref[...] = jnp.broadcast_to(probs, prob_ref.shape)
    pre_gate_ref[...] = dot32(x_ref[...], gate_ref[...])
    pre_up_ref[...] = dot32(x_ref[...], up_ref[...])


def mid_kernel(
    experts, width, gate_ref, up_ref, down_ref, prob_ref, pre_gate_ref, pre_up_ref, *refs
):
    pieces, outs = refs[:-6], refs[-6:]
    y_ref, hidden_ref, grad_gate_ref, grad_up_ref, mine_ref, give_ref = outs
    for part in chunks_of(width):
        y_ref[:, part] = jnp.concatenate(
            [piece[:, part].astype(F32) for piece in pieces], axis=0
        ).astype(B16)
    grad_full = dot32(y_ref[...], down_ref[...])
    pre_gate, pre_up = pre_gate_ref[...], pre_up_ref[...]
    probs = prob_ref[:, :1]
    routed = probs > 0.0
    sigmoid_gate = jax.nn.sigmoid(pre_gate)
    activated = pre_gate * sigmoid_gate
    hidden = jnp.where(routed, activated * pre_up, 0.0)
    hidden_ref[...] = (hidden * probs).astype(B16)
    own_probs = jnp.sum(hidden * grad_full, axis=1, keepdims=True)
    grad_hidden = grad_full * probs
    grad_gate_ref[...] = jnp.where(
        routed, grad_hidden * pre_up * sigmoid_gate * (1.0 + pre_gate * (1.0 - sigmoid_gate)), 0.0
    ).astype(B16)
    grad_up_ref[...] = jnp.where(routed, grad_hidden * activated, 0.0).astype(B16)
    half = mine_ref.shape[0]
    for part in chunks_of(width):
        product = dot32(grad_gate_ref[...], gate_ref[:, part])
        product = product + dot32(grad_up_ref[...], up_ref[:, part])
        mine_ref[:, part] = product[:half].astype(B16)
        give_ref[:, part] = product[half:].astype(B16)
    lanes = mine_ref.shape[1] - width
    lane = lax.broadcasted_iota(jnp.int32, (2 * half, lanes), 1)
    expert = lax.axis_index("expert") // 2
    high = own_probs.astype(B16).astype(F32)
    extra = jnp.where(lane == expert, high, jnp.where(lane == expert + experts, own_probs - high, 0.0))
    mine_ref[:, width:] = extra[:half].astype(B16)
    give_ref[:, width:] = extra[half:].astype(B16)


def first_sum_kernel(experts, width, near, folds, mine_ref, other_ref, after_ref, *outs):
    del after_ref
    total = mine_ref[...].astype(F32) + other_ref[...].astype(F32)
    extra = total[:, width:]
    lane = lax.broadcasted_iota(jnp.int32, extra.shape, 1)
    lost = jnp.where(lane < experts, extra - extra.astype(B16).astype(F32), 0.0)
    extra = extra + pltpu.roll(lost, experts, 1) - lost
    slots = outs[0].shape[0]
    for i, out in enumerate(outs[:near]):
        part = slice(i * slots, (i + 1) * slots)
        out[:, :width] = total[part, :width].astype(B16)
        out[:, width:] = extra[part].astype(B16)
    if outs[near:]:
        rest = jnp.concatenate([total[near * slots :, :width], extra[near * slots :]], axis=1)
        laid = lane_pieces(rest, folds, outs[near].shape[1]).astype(B16)
        write_rows(outs[near:], dot32(piece_order(laid.shape[0], folds, len(outs[near:]), True), laid))


def second_sum_kernel(near, folds, crossing, ways, order, give_ref, pick_ref, *refs):
    refs[-1][...] = give_ref[...]
    refs = refs[:-1]
    came = [refs[order.index(i)] for i in range(len(order))]
    came, refs = came[:near], (*came[near:], *refs[len(order) :])
    total = dot32(pick_ref[...].astype(B16), stacked(came).astype(B16), TN)
    if crossing:
        cross_pick, came, refs = refs[0], refs[1 : 1 + crossing], refs[1 + crossing :]
        block = dot32(cross_pick[...].astype(B16), stacked(came).astype(B16), TN)
        refs[-1][...] = beside_lanes(block, folds)[:, : total.shape[1]].astype(B16)
    own_out, outs = refs[0], refs[1 : 1 + ways]
    count = own_out.shape[0]
    own_out[...] = total[:count]
    for i, out in enumerate(outs):
        out[...] = total[(i + 1) * count : (i + 2) * count].astype(B16)


def up_grads_kernel(x_ref, grad_ref, raw_ref, narrow_ref, masked_out, wide_out, turned_out):
    width = x_ref.shape[1]
    for part in chunks_of(width, width // 2):
        turned = x_ref[:, part].T
        turned_out[part, :] = turned
        masked = dot32(turned, grad_ref[...]) * raw_ref[part, :].astype(F32)
        masked = masked.astype(B16)
        masked_out[part, :] = masked
        wide_out[:, part] = dot32(narrow_ref[1], masked, NT)


def other_grads_kernel(
    x_ref, grad_ref, gate_ref, y_ref, hidden_ref, down_ref, narrow_ref, after_ref, up_wide_ref,
    masked_gate, masked_down, keep_out, give_out, wide_all,
):
    del after_ref
    width, rank = x_ref.shape[0], narrow_ref.shape[1]
    wide_all[pl.ds(rank, rank), :] = up_wide_ref[...]
    for part in chunks_of(width, width // 2):
        masked = dot32(x_ref[part, :], grad_ref[...]) * gate_ref[part, :].astype(F32)
        masked = masked.astype(B16)
        masked_gate[part, :] = masked
        wide_all[pl.ds(0, rank), part] = dot32(narrow_ref[0], masked, NT)
        masked = dot32(hidden_ref[...], y_ref[:, part], TN) * down_ref[:, part].astype(F32)
        masked = masked.astype(B16)
        masked_down[:, part] = masked
        wide_all[pl.ds(2 * rank, rank), part] = dot32(narrow_ref[2], masked)
    half = keep_out.shape[1]
    is_lower = lax.axis_index("expert") % 2 == 0

    @pl.when(is_lower)
    def _():
        keep_out[...] = wide_all[:, :half]
        give_out[...] = wide_all[:, half:].astype(B16)

    @pl.when(jnp.logical_not(is_lower))
    def _():
        keep_out[...] = wide_all[:, half:]
        give_out[...] = wide_all[:, :half].astype(B16)


def narrow_kernel(masked_gate, masked_up, masked_down, wide_ref, after_ref, narrow_out):
    del after_ref
    rank = wide_ref.shape[1]
    for i, (masked, dims) in enumerate(((masked_gate, NN), (masked_up, NN), (masked_down, NT))):
        narrow_out[pl.ds(i * rank, rank), :] = dot32(wide_ref[i], masked[...], dims)


def last_kernel(experts, width, ids_ref, keep_ref, own_ref, *refs):
    came, given_ref, (tokens_out, probs_out, wide_out) = refs[:-4], refs[-4], refs[-3:]
    wide_out[...] = keep_ref[...] + given_ref[...].astype(F32)
    total = own_ref[...]
    for ref in came:
        total = total + ref[...].astype(F32)
    tokens_out[...] = total[:, :width].astype(B16)
    extra, ids = total[:, width:], ids_ref[...]
    lane = lax.broadcasted_iota(jnp.int32, extra.shape, 1)
    spot = lax.broadcasted_iota(jnp.int32, ids.shape, 1)
    probs = jnp.zeros(ids.shape, F32)
    for k in range(ids.shape[1]):
        wanted = ids[:, k : k + 1]
        found = jnp.where((lane == wanted) | (lane == wanted + experts), extra, 0.0)
        probs = jnp.where(spot == k, jnp.sum(found, axis=1, keepdims=True), probs)
    probs_out[...] = probs


def body(
    tokens,
    cotangent,
    route_probs,
    expert_ids,
    gate_weight,
    up_weight,
    down_weight,
    narrow,
    wide_factors,
):
    rows, width = tokens.shape
    hidden_units = gate_weight.shape[1]
    top_count = expert_ids.shape[1]
    rank = narrow.shape[1]
    devices = lax.axis_size("expert")
    experts = devices // 2
    capacity = min(rows, max(2, (3 * rows * top_count + 2 * experts - 1) // (2 * experts)))
    near, far = stages()[0], stages()[1:]
    count = rows * devices // 2 // (len(near) + 1)
    slots = count // rows * capacity
    half = (1 + len(near)) * slots
    offsets = [0]
    for masks in far:
        offsets = [first ^ mask for first in offsets for mask in (0, *masks)]
    lanes = -(-2 * experts // 128) * 128
    full = width + lanes

    def pieces_of(block):
        for masks in reversed(far[1:]):
            block = jnp.concatenate([block] + [send(block, mask) for mask in masks], axis=0)
        if far:
            return [block] + [send(block, mask) for mask in far[0]]
        return [block]

    sources = (tokens, cotangent, route_probs, expert_ids)
    message = pl.pallas_call(
        functools.partial(message_kernel, experts),
        grid=(1,),
        out_shape=pltpu.VMEM((rows, full + width), B16),
        in_specs=[pl.BlockSpec(source.shape, lambda step: (0, 0)) for source in sources],
        out_specs=pl.BlockSpec(memory_space=pltpu.VMEM),
        compiler_params=pltpu.CompilerParams(vmem_limit_bytes=8 * 2**20),
        cost_estimate=pl.CostEstimate(flops=0, bytes_accessed=4 * rows * (full + width), transcendentals=0),
    )(*[pltpu.with_memory_space_constraint(source, pltpu.HBM) for source in sources])
    pieces = pieces_of(message)
    crossed = [send(message, mask) for mask in near[2:]]
    matmul = 2 * 2 * half * width * hidden_units
    gate_raw, up_raw, gate_eff, up_eff, narrow, wide = in_vmem(
        up_side_kernel,
        [(gate_weight.shape, B16)] * 4 + [(narrow.shape, B16), ((3, rank, width), B16)],
        (gate_weight, up_weight, narrow, wide_factors, send(wide_factors, 1)),
        2 * matmul,
        outside=4,
        scratch=[
            pltpu.VMEM(wide_factors.shape, B16),
            pltpu.SemaphoreType.DMA((2,)),
            pltpu.SemaphoreType.DMA((8,)),
        ],
    )
    folds, step = folds_of(rows, capacity, full + width)
    probs_at = slice(width, full)
    beside = near[:2]
    pick, *packed = in_vmem(
        functools.partial(
            pack_kernel, (0, *beside), offsets, rows, capacity, probs_at, len(pieces)
        ),
        [(((1 + len(beside)) * slots, count), F32)]
        + [((slots, full + width), B16)] * (1 + len(beside))
        + [((len(offsets) * folds * capacity, folds * rows), F32)] * len(crossed)
        + [((folds * capacity, step), B16)] * (len(offsets) * len(crossed)),
        [wide] + pieces[::-1] + crossed,
    )
    packed, cross_pick, folded = packed[: 1 + len(beside)], packed[1 + len(beside) :], []
    cross_pick, folded = cross_pick[:1], cross_pick[1:]
    came = packed[:1] + [send(block, mask) for block, mask in zip(packed[1:], beside)]
    came += folded[:1] + [send(block, mask) for block, mask in zip(folded[1:], offsets[1:])]
    order = list(range(len(came)))
    if len(came) > 6:
        order = [0, 1, 5, 2, 6, *order[7:], 4, 3]
    down_raw, down_turned, gate_turned, up_turned = in_vmem(
        down_side_kernel,
        [(down_weight.shape, B16), (gate_weight.shape, B16)] + [(down_weight.shape, B16)] * 2,
        (down_weight, narrow, wide, gate_eff, up_eff, pick),
        matmul,
        outside=1,
        scratch=[pltpu.SemaphoreType.DMA((4,))],
    )
    mine_rows, cot_mine = in_vmem(
        functools.partial(stack_kernel, folds, 1 + len(beside), order),
        [((half, full), B16), ((half, width), B16)],
        [down_turned] + [came[i] for i in order],
    )
    token_rows = [mine_rows, send(mine_rows, 1)]
    cot_rows = [cot_mine, send(cot_mine, 1)]

    wide_type, unit_type = ((2 * half, width), B16), ((2 * half, hidden_units), B16)
    x, probs, pre_gate, pre_up = in_vmem(
        functools.partial(pre_kernel, experts, width),
        [wide_type, ((2 * half, 128), F32)] + [((2 * half, hidden_units), F32)] * 2,
        (gate_eff, up_eff, *token_rows),
        2 * matmul,
    )
    y, hidden, grad_gate, grad_up, mine, give = in_vmem(
        functools.partial(mid_kernel, experts, width),
        [wide_type] + [unit_type] * 3 + [((half, full), B16)] * 2,
        (gate_turned, up_turned, down_turned, probs, pre_gate, pre_up, *cot_rows),
        3 * matmul,
    )
    other = send(give, 1)
    masked_up, up_wide, turned = in_vmem(
        up_grads_kernel,
        [(up_weight.shape, B16), ((rank, width), F32), ((width, 2 * half), B16)],
        (x, grad_up, up_raw, narrow),
        2 * matmul,
    )
    near_count, cross_count = 1 + len(beside), len(folded)
    fold_step = folds_of(rows, capacity, full)[1]
    sums = in_vmem(
        functools.partial(first_sum_kernel, experts, width, near_count, folds),
        [((slots, full), B16)] * near_count
        + [((folds * capacity, fold_step), B16)] * cross_count,
        (mine, other, up_wide),
    )
    masked_gate, masked_down, keep, give = in_vmem(
        other_grads_kernel,
        [(gate_weight.shape, B16), (down_weight.shape, B16)]
        + [((3 * rank, width // 2), F32), ((3 * rank, width // 2), B16)],
        (turned, grad_gate, gate_raw, y, hidden, down_raw, narrow, sums[0], up_wide),
        4 * matmul,
        scratch=[pltpu.VMEM((3 * rank, width), F32)],
    )
    came = [sums[0]] + [send(part, mask) for part, mask in zip(sums[1:near_count], beside)]
    crossing = sums[near_count:]
    came += [*cross_pick, *crossing[:1]]
    came += [send(part, mask) for part, mask in zip(crossing[1:], offsets[1:])]
    order = list(range(len(came)))
    if len(came) > 7:
        order = [0, 3, 4, 1, 6, 2, 7, *order[8:], 5]
    ways = len(far[0]) if far else 0
    own, *parts = in_vmem(
        functools.partial(second_sum_kernel, near_count, folds, cross_count, ways, order),
        [((count // (ways + 1), full), F32)]
        + [((count // (ways + 1), full), B16)] * ways
        + [((rows, full), B16)] * len(crossed)
        + [(give.shape, B16)],
        (give, pick, *[came[i] for i in order]),
    )
    *parts, give = parts
    (grad_narrow,) = in_vmem(
        narrow_kernel,
        [((3 * rank, hidden_units), F32)],
        (masked_gate, masked_up, masked_down, wide, parts[-1]),
        2 * matmul,
        results=(0,),
    )
    from_cross = [send(part, mask) for part, mask in zip(parts[ways:], near[2:])]
    came = [send(part, mask) for part, mask in zip(parts[:ways], far[0] if far else ())]
    for masks in far[1:]:
        total = own
        for part in came:
            total = total + part.astype(F32)
        own, *parts = jnp.split(total, len(masks) + 1, axis=0)
        came = [send(part.astype(B16), mask) for part, mask in zip(parts, masks)]
    came = came[1:] + from_cross + came[:1]
    grad_tokens, grad_probs, grad_wide = in_vmem(
        functools.partial(last_kernel, experts, width),
        [((rows, width), B16), (expert_ids.shape, F32), ((3 * rank, width // 2), F32)],
        (expert_ids, keep, own, *came, send(give, 1)),
        results=(0, 1, 2),
    )
    return (
        grad_tokens,
        grad_probs,
        grad_narrow.reshape(3, rank, hidden_units),
        grad_wide.reshape(3, rank, width // 2),
    )


def solution(mesh):
    in_specs = (
        P(("groups", "expert"), None),
        P(("groups", "expert"), None),
        P(("groups", "expert"), None),
        P(("groups", "expert"), None),
        P(None, "expert"),
        P(None, "expert"),
        P("expert", None),
        P(None, None, "expert"),
        P(None, None, "expert"),
    )
    out_specs = (
        P(("groups", "expert"), None),
        P(("groups", "expert"), None),
        P("groups", None, "expert"),
        P("groups", None, "expert"),
    )
    return jax.shard_map(body, mesh=mesh, in_specs=in_specs, out_specs=out_specs, check_vma=False)
```
